32 devices in a mesh: dp: 4 (over y, core), seq: 8 (over z, x).
Axes of the slice: x: 2, y: 2, z: 4, core: 2. Of those that a mesh axis runs over, the one named last changes fastest.
Arguments:
- video_in: bfloat16 [4, 16, 32, 64, 128], P('dp', 'seq'), may hold values from -110 to 180
- w_spatial: bfloat16 [3, 3, 128, 128], replicated, may hold values from -0.1875 to 0.1875
- w_temporal: bfloat16 [3, 128, 128], replicated, may hold values from -0.3125 to 0.3125
- norm_gain: float32 [128], replicated, may hold values from 0.5 to 1.5
- norm_shift: float32 [128], replicated, may hold values from -3 to 3
- cotangent: bfloat16 [4, 16, 16, 32, 128], P('dp', 'seq'), may hold values from -6 to 6
Outputs:
- encoded: bfloat16 [4, 16, 16, 32, 128], P('dp', 'seq')
- grad_spatial: float32 [3, 3, 128, 128], replicated
- grad_temporal: float32 [3, 128, 128], replicated
- grad_gain: float32 [128], replicated
- grad_shift: float32 [128], replicated
The draws below stay inside these ranges and needn't reach their ends.
All inputs are finite; a program needn't handle non-finite values.
Results may differ from the reference program's by a relative error of at most 0.0056.
Values may be sent and summed in bfloat16 or wider, within the bound.
No kernel may reach another device: no remote copies, remote signals or barrier semaphores. Data moves between devices by JAX's collectives and lax.ppermute only.
A program may use at most 128 MiB of HBM per device.

```python
import math
import jax
import jax.numpy as jnp
from jax import lax

C = 128
GROUPS = 32
FRAMES = 8
OW = 32
CLIP_BATCHES = 4
BATCH_FRAMES = 16
CLIPS = 8
OH = 16
H = 32
W = 64


def draw_video_in(key, part):
    key = jax.random.fold_in(key, 11)
    key_noise = jax.random.fold_in(key, 1)
    key_frame_list = jax.random.fold_in(key, 2)
    full_shape = (CLIP_BATCHES, BATCH_FRAMES, H, W, C)
    frame_position = jnp.arange(BATCH_FRAMES, dtype=jnp.float32) / float(BATCH_FRAMES - 1)
    row_pos = jnp.arange(H, dtype=jnp.float32) / float(H - 1)
    frame_group_size = jnp.exp(jax.random.uniform(key_frame_list, (CLIP_BATCHES, BATCH_FRAMES), jnp.float32, 0.0, math.log(3.0)))
    jitter = jnp.clip(jax.random.normal(key_noise, full_shape, jnp.float32), -4.0, 4.0)
    growth_factor = 3.0
    frame_scaling = jnp.power(growth_factor, frame_position)[None, :] * frame_group_size
    row_scale = jnp.power(3.0, row_pos)
    return (jitter * frame_scaling[:, :, None, None, None] * row_scale[None, None, :, None, None]).astype(jnp.bfloat16)


def shard_levels(key, shape, split, least, top_value):
    def one(dim, blocks):
        steps = jax.random.uniform(jax.random.fold_in(jax.random.fold_in(key, 6), dim), (blocks,), jnp.float32, least / len(split), top_value / len(split))
        return jnp.repeat(jnp.exp(steps), shape[dim] // blocks).reshape((-1,) + (1,) * (len(shape) - dim - 1))

    gain = one(*split[0])
    for cut in split[1:]:
        gain = gain * one(*cut)
    return gain


def normal_values(own_key, extent, spread, limit, cuts=(), kind=jnp.bfloat16):
    array = spread * jax.random.normal(own_key, extent, jnp.float32)
    if cuts:
        array = array * shard_levels(own_key, extent, cuts, -0.22, 0.18)
    return jnp.clip(array, -limit, limit).astype(kind)


def setup_inputs(seed: int = 0) -> dict:
    seeds = jax.random.split(jax.random.key(seed), 7)
    return {
        "video_in": draw_video_in(jax.random.fold_in(seeds[6], 71), 0),
        "w_spatial": normal_values(seeds[1], (3, 3, C, C), (9 * C) ** -0.5, 0.1875),
        "w_temporal": normal_values(seeds[2], (3, C, C), (3 * C) ** -0.5, 0.3125),
        "norm_gain": jnp.clip(1.0 + 0.1 * jax.random.normal(seeds[3], (C,), jnp.float32), 0.5, 1.5),
        "norm_shift": normal_values(seeds[4], (C,), 0.5, 3.0, (), jnp.float32),
        "cotangent": normal_values(seeds[5], (CLIP_BATCHES, BATCH_FRAMES, OH, OW, C), 1.0, 6.0, ((0, 4), (1, 8))),
    }


HIGHEST = lax.Precision.HIGHEST

def patch_rows(frames):
    height = frames.shape[1]
    width = frames.shape[2]
    channels = frames.shape[3]
    padded = jnp.pad(frames, ((0, 0), (1, 1), (1, 1), (0, 0)))
    tap_list = [padded[:, tap_row:tap_row + height:2, tap_col:tap_col + width:2, :] for tap_row in range(3) for tap_col in range(3)]
    return jnp.concatenate(tap_list, axis=-1).reshape(-1, 9 * channels)

def group_total(values):
    return values.reshape(GROUPS, -1).sum(axis=1)

def widen_groups(values):
    return jnp.repeat(values, C // GROUPS)

def delayed(values, steps):
    return jnp.concatenate([jnp.zeros((steps,) + values.shape[1:], values.dtype), values[:-steps]], axis=0)

def advanced(values, steps):
    return jnp.concatenate([values[steps:], jnp.zeros((steps,) + values.shape[1:], values.dtype)], axis=0)

def reference(video_in, w_spatial, w_temporal, norm_gain, norm_shift, cotangent):
    loss_scale = float(CLIP_BATCHES * BATCH_FRAMES * OH * OW) ** (-0.5)
    members = FRAMES * OH * OW * (C // GROUPS)
    spatial_flat = w_spatial.astype(jnp.float32).reshape(9 * C, C)
    forward_kernel = w_temporal.astype(jnp.float32).reshape(3 * C, C)
    backward_kernel = jnp.transpose(w_temporal, (0, 2, 1)).astype(jnp.float32).reshape(3 * C, C)
    contract_rows = (((0,), (0,)), ((), ()))
    clips_in = video_in.reshape(CLIPS, FRAMES, H, W, C)
    clips_cot = cotangent.reshape(CLIPS, FRAMES, OH, OW, C)

    def one_clip(clip_pair):
        frames, cot_clip = clip_pair
        patches = patch_rows(frames.astype(jnp.float32))
        spatial = jnp.dot(patches, spatial_flat, precision=HIGHEST).reshape(FRAMES, OH, OW, C)
        group_mean = group_total(spatial.sum(axis=(0, 1, 2))) / members
        centered = spatial - widen_groups(group_mean)
        group_var = group_total((centered * centered).sum(axis=(0, 1, 2))) / members
        inv_std = widen_groups(lax.rsqrt(group_var + 1e-05))
        normed = centered * inv_std
        before_act = normed * norm_gain + norm_shift
        activation = lax.optimization_barrier(jax.nn.silu(before_act).astype(jnp.bfloat16))
        act_wide = activation.astype(jnp.float32)
        forward_in = jnp.concatenate([act_wide, delayed(act_wide, 1), delayed(act_wide, 2)], axis=-1).reshape(-1, 3 * C)
        encoded = jnp.dot(forward_in, forward_kernel, precision=HIGHEST).astype(jnp.bfloat16).reshape(FRAMES, OH, OW, C)
        cot_wide = cot_clip.astype(jnp.float32)
        grad_temporal = lax.dot_general(forward_in, cot_wide.reshape(-1, C), contract_rows, precision=HIGHEST) * loss_scale
        backward_in = jnp.concatenate([cot_wide, advanced(cot_wide, 1), advanced(cot_wide, 2)], axis=-1).reshape(-1, 3 * C)
        back_act = lax.optimization_barrier(jnp.dot(backward_in, backward_kernel, precision=HIGHEST).astype(jnp.bfloat16))
        back_act = back_act.astype(jnp.float32).reshape(FRAMES, OH, OW, C)
        gate_sig = jax.nn.sigmoid(before_act)
        back_pre = back_act * loss_scale * gate_sig * (1.0 + before_act * (1.0 - gate_sig))
        clip_shift = back_pre.sum(axis=(0, 1, 2))
        clip_gain = (back_pre * normed).sum(axis=(0, 1, 2))
        group_shift = group_total(norm_gain * clip_shift) / members
        group_gain = group_total(norm_gain * clip_gain) / members
        back_spatial = (norm_gain * back_pre - widen_groups(group_shift) - normed * widen_groups(group_gain)) * inv_std
        back_spatial = lax.optimization_barrier(back_spatial.astype(jnp.bfloat16)).astype(jnp.float32)
        grad_spatial = lax.dot_general(patches, back_spatial.reshape(-1, C), contract_rows, precision=HIGHEST)
        return (encoded, grad_spatial, grad_temporal, clip_gain, clip_shift)
    encoded, grad_spatial, grad_temporal, grad_gain, grad_shift = lax.map(one_clip, (clips_in, clips_cot))
    encoded = encoded.reshape(CLIP_BATCHES, BATCH_FRAMES, OH, OW, C)
    return (encoded, grad_spatial.sum(axis=0).reshape(3, 3, C, C), grad_temporal.sum(axis=0).reshape(3, C, C), grad_gain.sum(axis=0), grad_shift.sum(axis=0))
```

```python
import functools

import jax
import jax.numpy as jnp
from jax import lax
from jax.experimental import pallas as pl
from jax.experimental.pallas import tpu as pltpu
from jax.sharding import PartitionSpec as P

GROUPS = 32
FRAMES = 8
STEP_ROWS = 8
VMEM_BYTES = 48 * 1024 * 1024

WHOLE = pl.BlockSpec(memory_space=pltpu.VMEM)
SCALAR = pl.BlockSpec(memory_space=pltpu.SMEM)


def dot(left, right):
    return jnp.dot(left, right, preferred_element_type=jnp.float32)


def dot_transposed(left, right):
    return lax.dot_general(
        left, right, (((1,), (1,)), ((), ())), preferred_element_type=jnp.float32
    )


def each(count, body):
    if count <= 8:
        for step in range(count):
            body(step)
    else:
        lax.fori_loop(0, count, lambda step, carry: (body(step), carry)[1], 0)


def call(kernel, out_shape, in_specs, scratch=(), flops=0, moved=0):
    return pl.pallas_call(
        kernel,
        out_shape=out_shape,
        in_specs=in_specs,
        out_specs=jax.tree.map(lambda _: WHOLE, out_shape),
        scratch_shapes=list(scratch),
        compiler_params=pltpu.CompilerParams(vmem_limit_bytes=VMEM_BYTES),
        cost_estimate=pl.CostEstimate(flops=flops, bytes_accessed=moved, transcendentals=0),
    )


def group_spread(values, lanes):
    channels = values.shape[-1]
    shift = 1
    while shift < lanes:
        values = values + pltpu.roll(values, channels - shift, 1)
        shift *= 2
    lane = lax.broadcasted_iota(jnp.int32, values.shape, 1)
    values = jnp.where(lax.rem(lane, lanes) == 0, values, 0.0)
    shift = 1
    while shift < lanes:
        values = values + pltpu.roll(values, shift, 1)
        shift *= 2
    return values


def conv_kernel(video, weights, spatial, stats, odd, even, wide):
    frames, height, width, channels = video.shape
    out_rows, out_cols = height // 2, width // 2
    positions = frames * out_rows * out_cols
    for slot in range(2 * STEP_ROWS):
        wide[slot, 0:8] = jnp.zeros((8, channels), jnp.float32)

    for frame in range(frames):
        odd[frame, 0] = jnp.zeros((out_cols, 3 * channels), jnp.bfloat16)

        def separate(step, frame=frame):
            for row in range(STEP_ROWS):
                for parity in range(2):
                    slot = 2 * row + parity
                    wide[slot, 8 : 8 + width] = video[
                        frame, 2 * (step * STEP_ROWS + row) + parity
                    ].astype(jnp.float32)
            for row in range(STEP_ROWS):
                for parity in range(2):
                    slot = 2 * row + parity
                    for tap in range(3):
                        value = wide[slot, pl.ds(7 + tap, out_cols, stride=2), :].astype(
                            jnp.bfloat16
                        )
                        lanes = slice(tap * channels, (tap + 1) * channels)
                        if parity:
                            odd[frame, step * STEP_ROWS + row + 1, :, lanes] = value
                        else:
                            even[frame, step * STEP_ROWS + row, :, lanes] = value

        each(out_rows // STEP_ROWS, separate)

        def multiply(step, frame=frame):
            flat = (STEP_ROWS * out_cols, 3 * channels)
            first = step * STEP_ROWS
            total = dot(odd[frame, pl.ds(first, STEP_ROWS)].reshape(flat), weights[0])
            total += dot(even[frame, pl.ds(first, STEP_ROWS)].reshape(flat), weights[1])
            total += dot(odd[frame, pl.ds(first + 1, STEP_ROWS)].reshape(flat), weights[2])
            spatial[frame, pl.ds(first, STEP_ROWS)] = total.reshape(STEP_ROWS, out_cols, channels)

        each(out_rows // STEP_ROWS, multiply)

    steps = positions // (STEP_ROWS * out_cols)
    per_frame = out_rows // STEP_ROWS

    def block(step):
        return spatial[step // per_frame, pl.ds((step % per_frame) * STEP_ROWS, STEP_ROWS)]

    def fold(values):
        return values.reshape(-1, 8, channels).sum(axis=0)

    def fold_all(term):
        if steps <= 8:
            total = term(0)
            for step in range(1, steps):
                total += term(step)
            return total
        return lax.fori_loop(
            0, steps, lambda step, total: total + term(step), jnp.zeros((8, channels), jnp.float32)
        )

    mean = fold_all(lambda step: fold(block(step))).sum(axis=0, keepdims=True) / positions
    square = fold_all(lambda step: fold((block(step) - mean) ** 2)).sum(axis=0, keepdims=True)
    row = lax.broadcasted_iota(jnp.int32, (8, channels), 0)
    packed = jnp.where(row == 0, mean, jnp.where(row == 1, square, 0.0))
    for slot in range(stats.shape[0]):
        stats[slot] = packed


def clip_norm(stats, positions, lanes):
    cells = stats.shape[0] * lanes
    means = [stats[member, 0:1] for member in range(stats.shape[0])]
    squares = [stats[member, 1:2] for member in range(stats.shape[0])]
    mean = group_spread(jnp.broadcast_to(sum(means), (8, means[0].shape[-1])), lanes)[0:1] / cells
    square = sum(squares)
    for value in means:
        square = square + positions * (value - mean) ** 2
    square = group_spread(jnp.broadcast_to(square, (8, square.shape[-1])), lanes)[0:1]
    return mean, lax.rsqrt(square / (cells * positions) + 1e-05)


def act_kernel(
    loss_scale, spatial, stats, cot, halo, weights, gain, shift, act, normed, pre, inv, sums
):
    frames, out_rows, out_cols, channels = spatial.shape
    positions = frames * out_rows * out_cols
    mean, inv_std = clip_norm(stats, positions, channels // GROUPS)
    inv[...] = inv_std
    flat = (STEP_ROWS * out_cols, channels)
    shaped = (STEP_ROWS, out_cols, channels)
    sums_shift = jnp.zeros((8, channels), jnp.float32)
    sums_gain = jnp.zeros((8, channels), jnp.float32)

    def fold(values):
        return values.reshape(-1, 8, channels).sum(axis=0)

    for frame in range(frames):

        def cot_block(later, rows):
            if frame + later < frames:
                return cot[frame + later, rows].reshape(flat)
            return halo[frame + later - frames, rows].reshape(flat)

        def one(step, carry):
            rows = pl.ds(step * STEP_ROWS, STEP_ROWS)
            norm = (spatial[frame, rows].reshape(flat) - mean) * inv_std
            before = norm * gain[...] + shift[...]
            sig = jax.nn.sigmoid(before)
            act[frame, rows] = (before * sig).astype(jnp.bfloat16).reshape(shaped)
            back = dot_transposed(cot_block(0, rows), weights[0])
            back += dot_transposed(cot_block(1, rows), weights[1])
            back += dot_transposed(cot_block(2, rows), weights[2])
            back = back.astype(jnp.bfloat16).astype(jnp.float32)
            back_pre = back * loss_scale * sig * (1.0 + before * (1.0 - sig))
            normed[frame, rows] = norm.reshape(shaped)
            pre[frame, rows] = back_pre.reshape(shaped)
            return (carry[0] + fold(back_pre), carry[1] + fold(back_pre * norm))

        steps = out_rows // STEP_ROWS
        if steps <= 4:
            for step in range(steps):
                sums_shift, sums_gain = one(step, (sums_shift, sums_gain))
        else:
            sums_shift, sums_gain = lax.fori_loop(0, steps, one, (sums_shift, sums_gain))

    row = lax.broadcasted_iota(jnp.int32, (8, channels), 0)
    packed = jnp.where(
        row == 0,
        sums_shift.sum(axis=0, keepdims=True),
        jnp.where(row == 1, sums_gain.sum(axis=0, keepdims=True), 0.0),
    )

    def put(slot):
        sums[slot] = packed

    each(sums.shape[0], put)


def grad_kernel(
    per_clip, loss_scale, first, odd, even, normed, pre, inv, sums, gain, act, cot, halo, grads,
    grad_gain, grad_shift,
):
    frames, out_rows, out_cols, channels = normed.shape
    lanes = channels // GROUPS
    members = per_clip * frames * out_rows * out_cols * lanes
    clip = sums[first[0]]
    for member in range(1, per_clip):
        clip = clip + sums[first[0] + member]
    group = group_spread(clip * gain[...], lanes) / members
    group_shift, group_gain = group[0:1], group[1:2]
    total = jnp.sum(sums[...], axis=0)
    grad_shift[...] = total[0:1]
    grad_gain[...] = total[1:2]
    flat = (out_rows * out_cols, channels)
    flat_wide = (out_rows * out_cols, 3 * channels)
    parts = [None, None, None]
    temporal = None
    for frame in range(frames):
        back = (
            gain[...] * pre[frame].reshape(flat)
            - group_shift
            - normed[frame].reshape(flat) * group_gain
        ) * inv[...]
        back = back.astype(jnp.bfloat16).T
        for tap, source in enumerate(
            (odd.at[frame, pl.ds(0, out_rows)], even.at[frame], odd.at[frame, pl.ds(1, out_rows)])
        ):
            term = dot(back, source[...].reshape(flat_wide))
            parts[tap] = term if parts[tap] is None else parts[tap] + term
        act_turned = act[frame].reshape(flat).T
        cots = [
            cot[frame + later] if frame + later < frames else halo[frame + later - frames]
            for later in range(3)
        ]
        terms = [dot(act_turned, value.reshape(flat)) for value in cots]
        temporal = terms if temporal is None else [a + b for a, b in zip(temporal, terms)]
    for tap in range(3):
        for side in range(3):
            block = parts[tap][:, side * channels : (side + 1) * channels].T
            grads[pl.ds((3 * tap + side) * channels, channels)] = block.astype(jnp.bfloat16)
    for tap in range(3):
        grads[pl.ds((9 + tap) * channels, channels)] = (temporal[tap] * loss_scale).astype(
            jnp.bfloat16
        )
    if grads.shape[0] > 12 * channels:
        rest = grads.shape[0] - 12 * channels
        grads[pl.ds(12 * channels, rest)] = jnp.zeros((rest, channels), jnp.bfloat16)


def sum_kernel(arrived, spread):
    count, rows, channels = arrived.shape
    total = jnp.sum(arrived[...].astype(jnp.float32), axis=0).astype(jnp.bfloat16)

    def put(slot):
        spread[slot] = total

    each(count, put)


def final_kernel(arrived, grad_spatial, grad_temporal):
    rows = grad_spatial.shape[0]
    grad_spatial[...] = arrived[pl.ds(0, rows)].astype(jnp.float32)
    grad_temporal[...] = arrived[pl.ds(rows, grad_temporal.shape[0])].astype(jnp.float32)


def encode_kernel(act, halo, weights, encoded):
    frames, out_rows, out_cols, channels = act.shape
    flat = (STEP_ROWS * out_cols, channels)
    for frame in range(frames):

        def one(step, frame=frame):
            rows = pl.ds(step * STEP_ROWS, STEP_ROWS)
            total = None
            for tap in range(3):
                source = (
                    act[frame - tap, rows] if frame >= tap else halo[frames + frame - tap, rows]
                )
                term = dot(source.reshape(flat), weights[tap])
                total = term if total is None else total + term
            encoded[frame, rows] = total.astype(jnp.bfloat16).reshape(
                STEP_ROWS, out_cols, channels
            )

        each(out_rows // STEP_ROWS, one)


def on_device(video_in, w_spatial, w_temporal, norm_gain, norm_shift, cotangent):
    frames, height, width, channels = video_in.shape[1:]
    out_rows, out_cols = height // 2, width // 2
    dp_size, seq_size = lax.axis_size("dp"), lax.axis_size("seq")
    devices = dp_size * seq_size
    per_clip = FRAMES // frames
    assert frames >= 2 and FRAMES % frames == 0
    loss_scale = float(devices * frames * out_rows * out_cols) ** (-0.5)
    shape = (frames, out_rows, out_cols, channels)
    video = video_in[0]
    cot = cotangent[0]
    gain = norm_gain[None]
    shift = norm_shift[None]
    f32, bf16 = jnp.float32, jnp.bfloat16
    struct = jax.ShapeDtypeStruct
    positions = frames * out_rows * out_cols

    back_pairs = [(s, s - 1) for s in range(seq_size) if s % per_clip]
    ahead_pairs = [(s - 1, s) for s in range(seq_size) if s % per_clip]
    clips = [
        list(range(first, first + per_clip)) for first in range(0, seq_size, per_clip)
    ]

    cot_halo = lax.ppermute(cot, "seq", back_pairs)

    spatial, stats, odd, even = call(
        conv_kernel,
        (
            struct(shape, f32),
            struct((per_clip, 8, channels), f32),
            struct((frames, out_rows + 1, out_cols, 3 * channels), bf16),
            struct((frames, out_rows, out_cols, 3 * channels), bf16),
        ),
        [WHOLE] * 2,
        [pltpu.VMEM((2 * STEP_ROWS, 8 + width, channels), f32)],
        flops=2 * positions * 9 * channels * channels,
        moved=video.size * 6,
    )(video, w_spatial.reshape(3, 3 * channels, channels))

    stats = lax.all_to_all(stats, "seq", 0, 0, axis_index_groups=clips, tiled=True)

    act, normed, pre, inv, sums = call(
        functools.partial(act_kernel, loss_scale),
        (
            struct(shape, bf16),
            struct(shape, f32),
            struct(shape, f32),
            struct((1, channels), f32),
            struct((devices, 8, channels), f32),
        ),
        [WHOLE] * 7,
        flops=2 * positions * 3 * channels * channels,
        moved=positions * channels * 20,
    )(spatial, stats, cot, cot_halo, w_temporal, gain, shift)

    act_halo = lax.ppermute(act, "seq", ahead_pairs)
    sums = lax.all_to_all(sums, ("dp", "seq"), 0, 0, tiled=True)

    chunk = -(-12 * channels // (16 * devices)) * 16
    seq_index = lax.axis_index("seq")
    first = lax.axis_index("dp") * seq_size + seq_index // per_clip * per_clip
    grads, grad_gain, grad_shift = call(
        functools.partial(grad_kernel, per_clip, loss_scale),
        (
            struct((devices * chunk, channels), bf16),
            struct((1, channels), f32),
            struct((1, channels), f32),
        ),
        [SCALAR] + [WHOLE] * 10,
        flops=2 * positions * 12 * channels * channels,
        moved=positions * channels * 24,
    )(first.astype(jnp.int32)[None], odd, even, normed, pre, inv, sums, gain, act, cot, cot_halo)

    grads = lax.all_to_all(
        grads.reshape(devices, chunk, channels), ("dp", "seq"), 0, 0, tiled=True
    )
    grads = call(
        sum_kernel, struct((devices, chunk, channels), bf16), [WHOLE], moved=grads.size * 4
    )(grads)
    grads = lax.all_to_all(grads, ("dp", "seq"), 0, 0, tiled=True)
    encoded = call(
        encode_kernel,
        struct(shape, bf16),
        [WHOLE] * 3,
        flops=2 * positions * 3 * channels * channels,
        moved=positions * channels * 6,
    )(act, act_halo, w_temporal)
    grad_spatial, grad_temporal = call(
        final_kernel,
        (struct((9 * channels, channels), f32), struct((3 * channels, channels), f32)),
        [WHOLE],
        moved=12 * channels * channels * 6,
    )(grads.reshape(devices * chunk, channels))
    return (
        encoded[None],
        grad_spatial.reshape(3, 3, channels, channels),
        grad_temporal.reshape(3, channels, channels),
        grad_gain[0],
        grad_shift[0],
    )


def solution(mesh):
    placed = P("dp", "seq", None, None, None)
    return jax.shard_map(
        on_device,
        mesh=mesh,
        in_specs=(placed, P(), P(), P(), P(), placed),
        out_specs=(placed, P(), P(), P(), P()),
        check_vma=False,
    )
```

```python
import functools
import math

import jax
import jax.numpy as jnp
from jax import lax
from jax.experimental import pallas as pl
from jax.experimental.pallas import tpu as pltpu
from jax.sharding import PartitionSpec as P

GROUPS = 32
FRAMES = 8
STEP_ROWS = 8
EXTRA = 16
SPARE_BYTES = 4 * 1024 * 1024

WHOLE = pl.BlockSpec(memory_space=pltpu.VMEM)
FAR = pl.BlockSpec(memory_space=pltpu.HBM)


def dot(left, right):
    return jnp.dot(left, right, preferred_element_type=jnp.float32)


def dot_transposed(left, right):
    return lax.dot_general(
        left, right, (((1,), (1,)), ((), ())), preferred_element_type=jnp.float32
    )


def each(count, body):
    if count <= 8:
        for step in range(count):
            body(step)
    else:
        lax.fori_loop(0, count, lambda step, carry: (body(step), carry)[1], 0)


def call(kernel, out_shape, operands, specs=None, scratch=(), flops=0):
    sizes = [value.size * value.dtype.itemsize for value in operands]
    sizes += [value.size * value.dtype.itemsize for value in jax.tree.leaves(out_shape)]
    held = sum(math.prod(item.shape) * 4 for item in scratch if hasattr(item, "shape"))
    return pl.pallas_call(
        kernel,
        out_shape=out_shape,
        in_specs=specs or [WHOLE] * len(operands),
        out_specs=jax.tree.map(lambda _: WHOLE, out_shape),
        scratch_shapes=list(scratch),
        compiler_params=pltpu.CompilerParams(vmem_limit_bytes=sum(sizes) + held + SPARE_BYTES),
        cost_estimate=pl.CostEstimate(
            flops=flops, bytes_accessed=sum(sizes), transcendentals=0
        ),
    )(*operands)


def group_spread(values, lanes):
    channels = values.shape[-1]
    shift = 1
    while shift < lanes:
        values = values + pltpu.roll(values, channels - shift, 1)
        shift *= 2
    lane = lax.broadcasted_iota(jnp.int32, values.shape, 1)
    values = jnp.where(lax.rem(lane, lanes) == 0, values, 0.0)
    shift = 1
    while shift < lanes:
        values = values + pltpu.roll(values, shift, 1)
        shift *= 2
    return values


def conv_kernel(
    video_far, weights_far, gain_far, shift_far, spatial, stats, odd, even, params, wide, video,
    weights, arrived,
):
    frames, height, width, channels = video.shape
    out_rows, out_cols = height // 2, width // 2
    positions = frames * out_rows * out_cols
    pieces = arrived.shape[0] - 3
    half = height * frames // pieces
    copies = []
    for piece in range(pieces):
        rows = pl.ds(piece * half % height, half)
        at = (piece * half // height, rows)
        copies.append(pltpu.make_async_copy(video_far.at[at], video.at[at], arrived.at[piece]))
    small = [
        pltpu.make_async_copy(source, target, arrived.at[pieces + index])
        for index, (source, target) in enumerate(
            ((weights_far, weights), (gain_far, params.at[0:1]), (shift_far, params.at[1:2]))
        )
    ]
    copies[0].start()
    small[0].start()
    for copy in copies[1:]:
        copy.start()
    for copy in small[1:]:
        copy.start()
    for slot in range(2 * STEP_ROWS):
        wide[slot, 0:8] = jnp.zeros((8, channels), jnp.float32)

    for frame in range(frames):
        odd[frame, 0] = jnp.zeros((out_cols, 3 * channels), jnp.bfloat16)

    for piece in range(pieces):
        frame = piece * half // height
        base = piece * half % height // 2 // STEP_ROWS
        copies[piece].wait()

        def separate(step, frame=frame, base=base):
            step = base + step
            for row in range(STEP_ROWS):
                for parity in range(2):
                    slot = 2 * row + parity
                    wide[slot, 8 : 8 + width] = video[
                        frame, 2 * (step * STEP_ROWS + row) + parity
                    ].astype(jnp.float32)
            for row in range(STEP_ROWS):
                for parity in range(2):
                    slot = 2 * row + parity
                    for tap in range(3):
                        value = wide[slot, pl.ds(7 + tap, out_cols, stride=2), :].astype(
                            jnp.bfloat16
                        )
                        lanes = slice(tap * channels, (tap + 1) * channels)
                        if parity:
                            odd[frame, step * STEP_ROWS + row + 1, :, lanes] = value
                        else:
                            even[frame, step * STEP_ROWS + row, :, lanes] = value

        each(half // 2 // STEP_ROWS, separate)
        if piece == 0:
            small[0].wait()

        def multiply(step, frame=frame, base=base):
            step = base + step
            flat = (STEP_ROWS * out_cols, 3 * channels)
            first = step * STEP_ROWS
            total = dot(odd[frame, pl.ds(first, STEP_ROWS)].reshape(flat), weights[0])
            total += dot(even[frame, pl.ds(first, STEP_ROWS)].reshape(flat), weights[1])
            total += dot(odd[frame, pl.ds(first + 1, STEP_ROWS)].reshape(flat), weights[2])
            spatial[frame, pl.ds(first, STEP_ROWS)] = total.reshape(STEP_ROWS, out_cols, channels)

        each(half // 2 // STEP_ROWS, multiply)

    steps = positions // (STEP_ROWS * out_cols)
    per_frame = out_rows // STEP_ROWS

    def block(step):
        return spatial[step // per_frame, pl.ds((step % per_frame) * STEP_ROWS, STEP_ROWS)]

    def fold(values):
        return values.reshape(-1, 8, channels).sum(axis=0)

    def fold_all(term):
        if steps <= 8:
            total = term(0)
            for step in range(1, steps):
                total += term(step)
            return total
        return lax.fori_loop(
            0, steps, lambda step, total: total + term(step), jnp.zeros((8, channels), jnp.float32)
        )

    mean = fold_all(lambda step: fold(block(step))).sum(axis=0, keepdims=True) / positions
    square = fold_all(lambda step: fold((block(step) - mean) ** 2)).sum(axis=0, keepdims=True)
    row = lax.broadcasted_iota(jnp.int32, (8, channels), 0)
    packed = jnp.where(row == 0, mean, jnp.where(row == 1, square, 0.0))
    for slot in range(stats.shape[0]):
        stats[slot] = packed
    for copy in small[1:]:
        copy.wait()


def clip_norm(stats, positions, lanes):
    cells = stats.shape[0] * lanes
    means = [stats[member, 0:1] for member in range(stats.shape[0])]
    squares = [stats[member, 1:2] for member in range(stats.shape[0])]
    mean = group_spread(jnp.broadcast_to(sum(means), (8, means[0].shape[-1])), lanes)[0:1] / cells
    square = sum(squares)
    for value in means:
        square = square + positions * (value - mean) ** 2
    square = group_spread(jnp.broadcast_to(square, (8, square.shape[-1])), lanes)[0:1]
    return mean, lax.rsqrt(square / (cells * positions) + 1e-05)


def act_kernel(
    loss_scale, spatial, stats, cot, halo, weights, params, act, normed, pre, inv, sums
):
    frames, out_rows, out_cols, channels = spatial.shape
    positions = frames * out_rows * out_cols
    mean, inv_std = clip_norm(stats, positions, channels // GROUPS)
    inv[...] = inv_std
    gain, shift = params[0:1], params[1:2]
    flat = (STEP_ROWS * out_cols, channels)
    shaped = (STEP_ROWS, out_cols, channels)
    sums_shift = jnp.zeros((8, channels), jnp.float32)
    sums_gain = jnp.zeros((8, channels), jnp.float32)

    def fold(values):
        return values.reshape(-1, 8, channels).sum(axis=0)

    for frame in range(frames):

        def cot_block(later, rows):
            if frame + later < frames:
                return cot[frame + later, rows].reshape(flat)
            return halo[frame + later - frames, rows].reshape(flat)

        def one(step, carry):
            rows = pl.ds(step * STEP_ROWS, STEP_ROWS)
            norm = (spatial[frame, rows].reshape(flat) - mean) * inv_std
            before = norm * gain + shift
            sig = jax.nn.sigmoid(before)
            act[frame, rows] = (before * sig).astype(jnp.bfloat16).reshape(shaped)
            back = dot_transposed(cot_block(0, rows), weights[0])
            back += dot_transposed(cot_block(1, rows), weights[1])
            back += dot_transposed(cot_block(2, rows), weights[2])
            back = back.astype(jnp.bfloat16).astype(jnp.float32)
            back_pre = back * loss_scale * sig * (1.0 + before * (1.0 - sig))
            normed[frame, rows] = norm.reshape(shaped)
            pre[frame, rows] = back_pre.reshape(shaped)
            return (carry[0] + fold(back_pre), carry[1] + fold(back_pre * norm))

        steps = out_rows // STEP_ROWS
        if steps <= 4:
            for step in range(steps):
                sums_shift, sums_gain = one(step, (sums_shift, sums_gain))
        else:
            sums_shift, sums_gain = lax.fori_loop(0, steps, one, (sums_shift, sums_gain))

    row = lax.broadcasted_iota(jnp.int32, (8, channels), 0)
    packed = jnp.where(
        row == 0,
        sums_shift.sum(axis=0, keepdims=True),
        jnp.where(row == 1, sums_gain.sum(axis=0, keepdims=True), 0.0),
    )

    def put(slot):
        sums[slot] = packed

    each(sums.shape[0], put)


def split_rows(values, rows):
    pieces = []
    for value in values:
        rest = value
        for _ in range(3):
            piece = rest.astype(jnp.bfloat16).astype(jnp.float32)
            pieces.append(piece)
            rest = rest - piece
    row = lax.broadcasted_iota(jnp.int32, (rows, values[0].shape[-1]), 0)
    packed = jnp.zeros((rows, values[0].shape[-1]), jnp.float32)
    for index, piece in enumerate(pieces):
        packed = jnp.where(row == index, piece, packed)
    return packed.astype(jnp.bfloat16)


def join_rows(packed, count):
    return [
        packed[3 * i : 3 * i + 1] + packed[3 * i + 1 : 3 * i + 2] + packed[3 * i + 2 : 3 * i + 3]
        for i in range(count)
    ]


def store_rows(chunks, rows, first, values):
    done = 0
    while done < values.shape[0]:
        chunk, at = divmod(first + done, rows)
        count = min(rows - at, values.shape[0] - done)
        chunks[chunk, pl.ds(at, count)] = values[done : done + count]
        done += count


def grad_kernel(
    loss_scale, odd, even, normed, pre, inv, own, sums, params, act, cot, halo, grads
):
    frames, out_rows, out_cols, channels = normed.shape
    lanes = channels // GROUPS
    members = sums.shape[0] * frames * out_rows * out_cols * lanes
    gain = params[0:1]
    clip = jnp.sum(sums[...], axis=0)
    group = group_spread(clip * gain, lanes) / members
    group_shift, group_gain = group[0:1], group[1:2]
    flat = (out_rows * out_cols, channels)
    flat_wide = (out_rows * out_cols, 3 * channels)
    rows = grads.shape[1] - EXTRA
    parts = [None, None, None]
    temporal = None
    for frame in range(frames):
        back = (
            gain * pre[frame].reshape(flat)
            - group_shift
            - normed[frame].reshape(flat) * group_gain
        ) * inv[...]
        back = back.astype(jnp.bfloat16).T
        for tap, source in enumerate(
            (odd.at[frame, pl.ds(0, out_rows)], even.at[frame], odd.at[frame, pl.ds(1, out_rows)])
        ):
            term = dot(back, source[...].reshape(flat_wide))
            parts[tap] = term if parts[tap] is None else parts[tap] + term
        act_turned = act[frame].reshape(flat).T
        cots = [
            cot[frame + later] if frame + later < frames else halo[frame + later - frames]
            for later in range(3)
        ]
        terms = [dot(act_turned, value.reshape(flat)) for value in cots]
        temporal = terms if temporal is None else [a + b for a, b in zip(temporal, terms)]
    for tap in range(3):
        for side in range(3):
            block = parts[tap][:, side * channels : (side + 1) * channels].T
            store_rows(grads, rows, (3 * tap + side) * channels, block.astype(jnp.bfloat16))
    for tap in range(3):
        block = (temporal[tap] * loss_scale).astype(jnp.bfloat16)
        store_rows(grads, rows, (9 + tap) * channels, block)
    rest = grads.shape[0] * rows - 12 * channels
    if rest:
        store_rows(grads, rows, 12 * channels, jnp.zeros((rest, channels), jnp.bfloat16))
    extra = split_rows([own[0, 1:2], own[0, 0:1]], EXTRA)
    for chunk in range(grads.shape[0]):
        grads[chunk, pl.ds(rows, EXTRA)] = extra


def total_of(arrived, first, count):
    total = arrived[0, pl.ds(first, count)].astype(jnp.float32)
    for chunk in range(1, arrived.shape[0]):
        total += arrived[chunk, pl.ds(first, count)].astype(jnp.float32)
    return total


def near_sum_kernel(arrived, chunks):
    rows = arrived.shape[1] - EXTRA
    count = chunks.shape[1] - EXTRA
    extra = split_rows(join_rows(total_of(arrived, rows, EXTRA), 2), EXTRA)
    for chunk in range(chunks.shape[0]):
        chunks[chunk, pl.ds(0, count)] = total_of(arrived, chunk * count, count).astype(
            jnp.bfloat16
        )
        chunks[chunk, pl.ds(count, EXTRA)] = extra


def far_sum_kernel(arrived, spread, grad_gain, grad_shift):
    count = spread.shape[1]
    total = total_of(arrived, 0, count).astype(jnp.bfloat16)
    for slot in range(spread.shape[0]):
        spread[slot] = total
    grad_gain[...], grad_shift[...] = join_rows(total_of(arrived, count, EXTRA), 2)


def spread_kernel(arrived, spread):
    for slot in range(spread.shape[0]):
        spread[slot] = arrived[...]


def final_kernel(arrived, grad_spatial, grad_temporal):
    rows = grad_spatial.shape[0]
    grad_spatial[...] = arrived[pl.ds(0, rows)].astype(jnp.float32)
    grad_temporal[...] = arrived[pl.ds(rows, grad_temporal.shape[0])].astype(jnp.float32)


def encode_kernel(act, halo, weights, encoded):
    frames, out_rows, out_cols, channels = act.shape
    flat = (STEP_ROWS * out_cols, channels)
    for frame in range(frames):

        def one(step, frame=frame):
            rows = pl.ds(step * STEP_ROWS, STEP_ROWS)
            total = None
            for tap in range(3):
                source = (
                    act[frame - tap, rows] if frame >= tap else halo[frames + frame - tap, rows]
                )
                term = dot(source.reshape(flat), weights[tap])
                total = term if total is None else total + term
            encoded[frame, rows] = total.astype(jnp.bfloat16).reshape(
                STEP_ROWS, out_cols, channels
            )

        each(out_rows // STEP_ROWS, one)


def on_device(video_in, w_spatial, w_temporal, norm_gain, norm_shift, cotangent):
    frames, height, width, channels = video_in.shape[1:]
    out_rows, out_cols = height // 2, width // 2
    dp_size, seq_size = lax.axis_size("dp"), lax.axis_size("seq")
    devices = dp_size * seq_size
    per_clip = FRAMES // frames
    assert frames >= 2 and FRAMES % frames == 0
    loss_scale = float(devices * frames * out_rows * out_cols) ** (-0.5)
    shape = (frames, out_rows, out_cols, channels)
    positions = frames * out_rows * out_cols
    video = video_in[0]
    cot = cotangent[0]
    f32, bf16 = jnp.float32, jnp.bfloat16
    struct = jax.ShapeDtypeStruct

    back_pairs = [(s, s - 1) for s in range(seq_size) if s % per_clip]
    ahead_pairs = [(s - 1, s) for s in range(seq_size) if s % per_clip]
    clips = [list(range(first, first + per_clip)) for first in range(0, seq_size, per_clip)]
    pair = 2 if seq_size % 2 == 0 else 1
    near = [
        [d * seq_size + s + p for d in range(dp_size) for p in range(pair)]
        for s in range(0, seq_size, pair)
    ]
    far = [
        [d * seq_size + s + p for s in range(0, seq_size, pair)]
        for d in range(dp_size)
        for p in range(pair)
    ]
    near_count, far_count = dp_size * pair, seq_size // pair

    def exchange(value, axes, groups):
        return lax.all_to_all(value, axes, 0, 0, axis_index_groups=groups, tiled=True)

    cot_halo = lax.ppermute(cot, "seq", back_pairs)

    pieces = 2 * frames
    spatial, stats, odd, even, params = call(
        conv_kernel,
        (
            struct(shape, f32),
            struct((per_clip, 8, channels), f32),
            struct((frames, out_rows + 1, out_cols, 3 * channels), bf16),
            struct((frames, out_rows, out_cols, 3 * channels), bf16),
            struct((8, channels), f32),
        ),
        (
            video,
            w_spatial.reshape(3, 3 * channels, channels),
            norm_gain[None],
            norm_shift[None],
        ),
        specs=[FAR] * 4,
        scratch=[
            pltpu.VMEM((2 * STEP_ROWS, 8 + width, channels), f32),
            pltpu.VMEM(video.shape, bf16),
            pltpu.VMEM((3, 3 * channels, channels), bf16),
            pltpu.SemaphoreType.DMA((pieces + 3,)),
        ],
        flops=2 * positions * 9 * channels * channels,
    )
    stats = exchange(stats, "seq", clips)
    act, normed, pre, inv, own = call(
        functools.partial(act_kernel, loss_scale),
        (
            struct(shape, bf16),
            struct(shape, f32),
            struct(shape, f32),
            struct((1, channels), f32),
            struct((per_clip, 8, channels), f32),
        ),
        (spatial, stats, cot, cot_halo, w_temporal, params),
        flops=2 * positions * 3 * channels * channels,
    )
    act_halo = lax.ppermute(act, "seq", ahead_pairs)
    sums = exchange(own, "seq", clips)
    far_rows = -(-12 * channels // (16 * devices)) * 16
    near_rows = far_rows * far_count
    grads = call(
        functools.partial(grad_kernel, loss_scale),
        struct((near_count, near_rows + EXTRA, channels), bf16),
        (odd, even, normed, pre, inv, own, sums, params, act, cot, cot_halo),
        flops=2 * positions * 12 * channels * channels,
    )
    grads = exchange(grads, ("dp", "seq"), near)
    grads = call(
        near_sum_kernel, struct((far_count, far_rows + EXTRA, channels), bf16), (grads,)
    )
    grads = exchange(grads, ("dp", "seq"), far)
    grads, grad_gain, grad_shift = call(
        far_sum_kernel,
        (
            struct((far_count, far_rows, channels), bf16),
            struct((1, channels), f32),
            struct((1, channels), f32),
        ),
        (grads,),
    )
    grads = exchange(grads, ("dp", "seq"), far)
    grads = call(
        spread_kernel,
        struct((near_count, near_rows, channels), bf16),
        (grads.reshape(near_rows, channels),),
    )
    grads = exchange(grads, ("dp", "seq"), near)
    encoded = call(
        encode_kernel,
        struct(shape, bf16),
        (act, act_halo, w_temporal),
        flops=2 * positions * 3 * channels * channels,
    )
    grad_spatial, grad_temporal = call(
        final_kernel,
        (struct((9 * channels, channels), f32), struct((3 * channels, channels), f32)),
        (grads.reshape(near_count * near_rows, channels),),
    )
    return (
        encoded[None],
        grad_spatial.reshape(3, 3, channels, channels),
        grad_temporal.reshape(3, channels, channels),
        grad_gain[0],
        grad_shift[0],
    )


def solution(mesh):
    placed = P("dp", "seq", None, None, None)
    return jax.shard_map(
        on_device,
        mesh=mesh,
        in_specs=(placed, P(), P(), P(), P(), placed),
        out_specs=(placed, P(), P(), P(), P()),
        check_vma=False,
    )
```

```python
import functools
import math

import jax
import jax.numpy as jnp
from jax import lax
from jax.experimental import pallas as pl
from jax.experimental.pallas import tpu as pltpu
from jax.sharding import PartitionSpec as P

GROUPS = 32
FRAMES = 8
STEP_ROWS = 8
EXTRA = 8
SPARE_BYTES = 4 * 1024 * 1024

WHOLE = pl.BlockSpec(memory_space=pltpu.VMEM)
FAR = pl.BlockSpec(memory_space=pltpu.HBM)


def dot(left, right):
    return jnp.dot(left, right, preferred_element_type=jnp.float32)


def dot_transposed(left, right):
    return lax.dot_general(
        left, right, (((1,), (1,)), ((), ())), preferred_element_type=jnp.float32
    )


def each(count, body):
    if count <= 8:
        for step in range(count):
            body(step)
    else:
        lax.fori_loop(0, count, lambda step, carry: (body(step), carry)[1], 0)


def call(kernel, out_shape, operands, specs=None, scratch=(), flops=0):
    sizes = [value.size * value.dtype.itemsize for value in operands]
    sizes += [value.size * value.dtype.itemsize for value in jax.tree.leaves(out_shape)]
    held = sum(math.prod(item.shape) * 4 for item in scratch if hasattr(item, "shape"))
    return pl.pallas_call(
        kernel,
        out_shape=out_shape,
        in_specs=specs or [WHOLE] * len(operands),
        out_specs=jax.tree.map(lambda _: WHOLE, out_shape),
        scratch_shapes=list(scratch),
        compiler_params=pltpu.CompilerParams(vmem_limit_bytes=sum(sizes) + held + SPARE_BYTES),
        cost_estimate=pl.CostEstimate(
            flops=flops, bytes_accessed=sum(sizes), transcendentals=0
        ),
    )(*operands)


def group_spread(values, lanes):
    channels = values.shape[-1]
    shift = 1
    while shift < lanes:
        values = values + pltpu.roll(values, channels - shift, 1)
        shift *= 2
    lane = lax.broadcasted_iota(jnp.int32, values.shape, 1)
    values = jnp.where(lax.rem(lane, lanes) == 0, values, 0.0)
    shift = 1
    while shift < lanes:
        values = values + pltpu.roll(values, shift, 1)
        shift *= 2
    return values


def conv_kernel(
    video_far, weights_far, gain_far, shift_far, spatial, stats, odd, even, params, wide, video,
    weights, arrived,
):
    frames, height, width, channels = video.shape
    out_rows, out_cols = height // 2, width // 2
    positions = frames * out_rows * out_cols
    pieces = arrived.shape[0] - 3
    half = height * frames // pieces
    copies = []
    for piece in range(pieces):
        rows = pl.ds(piece * half % height, half)
        at = (piece * half // height, rows)
        copies.append(pltpu.make_async_copy(video_far.at[at], video.at[at], arrived.at[piece]))
    small = [
        pltpu.make_async_copy(source, target, arrived.at[pieces + index])
        for index, (source, target) in enumerate(
            ((weights_far, weights), (gain_far, params.at[0:1]), (shift_far, params.at[1:2]))
        )
    ]
    copies[0].start()
    small[0].start()
    for copy in copies[1:]:
        copy.start()
    for copy in small[1:]:
        copy.start()
    for slot in range(2 * STEP_ROWS):
        wide[slot, 0:8] = jnp.zeros((8, channels), jnp.float32)

    for frame in range(frames):
        odd[frame, 0] = jnp.zeros((out_cols, 3 * channels), jnp.bfloat16)

    for piece in range(pieces):
        frame = piece * half // height
        base = piece * half % height // 2 // STEP_ROWS
        copies[piece].wait()

        def separate(step, frame=frame, base=base):
            step = base + step
            for row in range(STEP_ROWS):
                for parity in range(2):
                    slot = 2 * row + parity
                    wide[slot, 8 : 8 + width] = video[
                        frame, 2 * (step * STEP_ROWS + row) + parity
                    ].astype(jnp.float32)
            for row in range(STEP_ROWS):
                for parity in range(2):
                    slot = 2 * row + parity
                    for tap in range(3):
                        value = wide[slot, pl.ds(7 + tap, out_cols, stride=2), :].astype(
                            jnp.bfloat16
                        )
                        lanes = slice(tap * channels, (tap + 1) * channels)
                        if parity:
                            odd[frame, step * STEP_ROWS + row + 1, :, lanes] = value
                        else:
                            even[frame, step * STEP_ROWS + row, :, lanes] = value

        each(half // 2 // STEP_ROWS, separate)
        if piece == 0:
            small[0].wait()

        def multiply(step, frame=frame, base=base):
            step = base + step
            flat = (STEP_ROWS * out_cols, 3 * channels)
            first = step * STEP_ROWS
            total = dot(odd[frame, pl.ds(first, STEP_ROWS)].reshape(flat), weights[0])
            total += dot(even[frame, pl.ds(first, STEP_ROWS)].reshape(flat), weights[1])
            total += dot(odd[frame, pl.ds(first + 1, STEP_ROWS)].reshape(flat), weights[2])
            spatial[frame, pl.ds(first, STEP_ROWS)] = total.reshape(STEP_ROWS, out_cols, channels)

        each(half // 2 // STEP_ROWS, multiply)

    steps = positions // (STEP_ROWS * out_cols)
    per_frame = out_rows // STEP_ROWS

    def block(step):
        return spatial[step // per_frame, pl.ds((step % per_frame) * STEP_ROWS, STEP_ROWS)]

    def fold(values):
        return values.reshape(-1, 8, channels).sum(axis=0)

    def fold_all(term):
        if steps <= 8:
            total = term(0)
            for step in range(1, steps):
                total += term(step)
            return total
        return lax.fori_loop(
            0, steps, lambda step, total: total + term(step), jnp.zeros((8, channels), jnp.float32)
        )

    mean = fold_all(lambda step: fold(block(step))).sum(axis=0, keepdims=True) / positions
    square = fold_all(lambda step: fold((block(step) - mean) ** 2)).sum(axis=0, keepdims=True)
    row = lax.broadcasted_iota(jnp.int32, (8, channels), 0)
    packed = jnp.where(row == 0, mean, jnp.where(row == 1, square, 0.0))
    for slot in range(stats.shape[0]):
        stats[slot] = packed
    for copy in small[1:]:
        copy.wait()


def clip_norm(stats, positions, lanes):
    cells = stats.shape[0] * lanes
    means = [stats[member, 0:1] for member in range(stats.shape[0])]
    squares = [stats[member, 1:2] for member in range(stats.shape[0])]
    mean = group_spread(jnp.broadcast_to(sum(means), (8, means[0].shape[-1])), lanes)[0:1] / cells
    square = sum(squares)
    for value in means:
        square = square + positions * (value - mean) ** 2
    square = group_spread(jnp.broadcast_to(square, (8, square.shape[-1])), lanes)[0:1]
    return mean, lax.rsqrt(square / (cells * positions) + 1e-05)


def act_kernel(
    loss_scale, spatial, stats, cot, halo, weights, params, act, normed, pre, inv, sums
):
    frames, out_rows, out_cols, channels = spatial.shape
    positions = frames * out_rows * out_cols
    mean, inv_std = clip_norm(stats, positions, channels // GROUPS)
    inv[...] = inv_std
    gain, shift = params[0:1], params[1:2]
    flat = (STEP_ROWS * out_cols, channels)
    shaped = (STEP_ROWS, out_cols, channels)
    sums_shift = jnp.zeros((8, channels), jnp.float32)
    sums_gain = jnp.zeros((8, channels), jnp.float32)

    def fold(values):
        return values.reshape(-1, 8, channels).sum(axis=0)

    for frame in range(frames):

        def cot_block(later, rows):
            if frame + later < frames:
                return cot[frame + later, rows].reshape(flat)
            return halo[frame + later - frames, rows].reshape(flat)

        def one(step, carry):
            rows = pl.ds(step * STEP_ROWS, STEP_ROWS)
            norm = (spatial[frame, rows].reshape(flat) - mean) * inv_std
            before = norm * gain + shift
            sig = jax.nn.sigmoid(before)
            act[frame, rows] = (before * sig).astype(jnp.bfloat16).reshape(shaped)
            back = dot_transposed(cot_block(0, rows), weights[0])
            back += dot_transposed(cot_block(1, rows), weights[1])
            back += dot_transposed(cot_block(2, rows), weights[2])
            back = back.astype(jnp.bfloat16).astype(jnp.float32)
            back_pre = back * loss_scale * sig * (1.0 + before * (1.0 - sig))
            normed[frame, rows] = norm.reshape(shaped)
            pre[frame, rows] = back_pre.reshape(shaped)
            return (carry[0] + fold(back_pre), carry[1] + fold(back_pre * norm))

        steps = out_rows // STEP_ROWS
        if steps <= 4:
            for step in range(steps):
                sums_shift, sums_gain = one(step, (sums_shift, sums_gain))
        else:
            sums_shift, sums_gain = lax.fori_loop(0, steps, one, (sums_shift, sums_gain))

    row = lax.broadcasted_iota(jnp.int32, (8, channels), 0)
    packed = jnp.where(
        row == 0,
        sums_shift.sum(axis=0, keepdims=True),
        jnp.where(row == 1, sums_gain.sum(axis=0, keepdims=True), 0.0),
    )

    def put(slot):
        sums[slot] = packed

    each(sums.shape[0], put)


def split_rows(values, rows):
    pieces = []
    for value in values:
        rest = value
        for _ in range(3):
            piece = rest.astype(jnp.bfloat16).astype(jnp.float32)
            pieces.append(piece)
            rest = rest - piece
    row = lax.broadcasted_iota(jnp.int32, (rows, values[0].shape[-1]), 0)
    packed = jnp.zeros((rows, values[0].shape[-1]), jnp.float32)
    for index, piece in enumerate(pieces):
        packed = jnp.where(row == index, piece, packed)
    return packed.astype(jnp.bfloat16)


def join_rows(packed, count):
    return [
        packed[3 * i : 3 * i + 1] + packed[3 * i + 1 : 3 * i + 2] + packed[3 * i + 2 : 3 * i + 3]
        for i in range(count)
    ]


def store_rows(chunks, rows, first, values):
    done = 0
    while done < values.shape[0]:
        chunk, at = divmod(first + done, rows)
        count = min(rows - at, values.shape[0] - done)
        chunks[chunk, pl.ds(at, count)] = values[done : done + count]
        done += count


def grad_kernel(
    loss_scale, odd, even, normed, pre, inv, own, sums, params, act, cot, halo, grads
):
    frames, out_rows, out_cols, channels = normed.shape
    lanes = channels // GROUPS
    members = sums.shape[0] * frames * out_rows * out_cols * lanes
    gain = params[0:1]
    clip = jnp.sum(sums[...], axis=0)
    group = group_spread(clip * gain, lanes) / members
    group_shift, group_gain = group[0:1], group[1:2]
    flat = (out_rows * out_cols, channels)
    flat_wide = (out_rows * out_cols, 3 * channels)
    rows = grads.shape[1] - EXTRA
    parts = [None, None, None]
    temporal = None
    for frame in range(frames):
        back = (
            gain * pre[frame].reshape(flat)
            - group_shift
            - normed[frame].reshape(flat) * group_gain
        ) * inv[...]
        back = back.astype(jnp.bfloat16).T
        for tap, source in enumerate(
            (odd.at[frame, pl.ds(0, out_rows)], even.at[frame], odd.at[frame, pl.ds(1, out_rows)])
        ):
            term = dot(back, source[...].reshape(flat_wide))
            parts[tap] = term if parts[tap] is None else parts[tap] + term
        act_turned = act[frame].reshape(flat).T
        cots = [
            cot[frame + later] if frame + later < frames else halo[frame + later - frames]
            for later in range(3)
        ]
        terms = [dot(act_turned, value.reshape(flat)) for value in cots]
        temporal = terms if temporal is None else [a + b for a, b in zip(temporal, terms)]
    for tap in range(3):
        for side in range(3):
            block = parts[tap][:, side * channels : (side + 1) * channels].T
            store_rows(grads, rows, (3 * tap + side) * channels, block.astype(jnp.bfloat16))
    for tap in range(3):
        block = (temporal[tap] * loss_scale).astype(jnp.bfloat16)
        store_rows(grads, rows, (9 + tap) * channels, block)
    rest = grads.shape[0] * rows - 12 * channels
    if rest:
        store_rows(grads, rows, 12 * channels, jnp.zeros((rest, channels), jnp.bfloat16))
    extra = split_rows([own[0, 1:2], own[0, 0:1]], EXTRA)
    for chunk in range(grads.shape[0]):
        grads[chunk, pl.ds(rows, EXTRA)] = extra


def total_of(arrived, first, count):
    total = arrived[0, pl.ds(first, count)].astype(jnp.float32)
    for chunk in range(1, arrived.shape[0]):
        total += arrived[chunk, pl.ds(first, count)].astype(jnp.float32)
    return total


def sum_kernel(arrived, spread, grad_gain, grad_shift):
    count = spread.shape[1]
    total = total_of(arrived, 0, count).astype(jnp.bfloat16)
    for slot in range(spread.shape[0]):
        spread[slot] = total
    grad_gain[...], grad_shift[...] = join_rows(total_of(arrived, count, EXTRA), 2)


def final_kernel(arrived, grad_spatial, grad_temporal):
    rows = grad_spatial.shape[0]
    grad_spatial[...] = arrived[pl.ds(0, rows)].astype(jnp.float32)
    grad_temporal[...] = arrived[pl.ds(rows, grad_temporal.shape[0])].astype(jnp.float32)


def encode_kernel(act, halo, weights, encoded):
    frames, out_rows, out_cols, channels = act.shape
    flat = (STEP_ROWS * out_cols, channels)
    for frame in range(frames):

        def one(step, frame=frame):
            rows = pl.ds(step * STEP_ROWS, STEP_ROWS)
            total = None
            for tap in range(3):
                source = (
                    act[frame - tap, rows] if frame >= tap else halo[frames + frame - tap, rows]
                )
                term = dot(source.reshape(flat), weights[tap])
                total = term if total is None else total + term
            encoded[frame, rows] = total.astype(jnp.bfloat16).reshape(
                STEP_ROWS, out_cols, channels
            )

        each(out_rows // STEP_ROWS, one)


def on_device(video_in, w_spatial, w_temporal, norm_gain, norm_shift, cotangent):
    frames, height, width, channels = video_in.shape[1:]
    out_rows, out_cols = height // 2, width // 2
    dp_size, seq_size = lax.axis_size("dp"), lax.axis_size("seq")
    devices = dp_size * seq_size
    per_clip = FRAMES // frames
    assert frames >= 2 and FRAMES % frames == 0
    loss_scale = float(devices * frames * out_rows * out_cols) ** (-0.5)
    shape = (frames, out_rows, out_cols, channels)
    positions = frames * out_rows * out_cols
    video = video_in[0]
    cot = cotangent[0]
    f32, bf16 = jnp.float32, jnp.bfloat16
    struct = jax.ShapeDtypeStruct

    back_pairs = [(s, s - 1) for s in range(seq_size) if s % per_clip]
    ahead_pairs = [(s - 1, s) for s in range(seq_size) if s % per_clip]
    clips = [list(range(first, first + per_clip)) for first in range(0, seq_size, per_clip)]

    def exchange(value, axes, groups=None):
        return lax.all_to_all(value, axes, 0, 0, axis_index_groups=groups, tiled=True)

    def far(value):
        return pltpu.with_memory_space_constraint(value, pltpu.HBM)

    cot_halo = lax.ppermute(cot, "seq", back_pairs)

    pieces = 2 * frames
    spatial, stats, odd, even, params = call(
        conv_kernel,
        (
            struct(shape, f32),
            struct((per_clip, 8, channels), f32),
            struct((frames, out_rows + 1, out_cols, 3 * channels), bf16),
            struct((frames, out_rows, out_cols, 3 * channels), bf16),
            struct((8, channels), f32),
        ),
        (
            far(video),
            far(w_spatial.reshape(3, 3 * channels, channels)),
            far(norm_gain[None]),
            far(norm_shift[None]),
        ),
        specs=[FAR] * 4,
        scratch=[
            pltpu.VMEM((2 * STEP_ROWS, 8 + width, channels), f32),
            pltpu.VMEM(video.shape, bf16),
            pltpu.VMEM((3, 3 * channels, channels), bf16),
            pltpu.SemaphoreType.DMA((pieces + 3,)),
        ],
        flops=2 * positions * 9 * channels * channels,
    )
    stats = exchange(stats, "seq", clips)
    act, normed, pre, inv, own = call(
        functools.partial(act_kernel, loss_scale),
        (
            struct(shape, bf16),
            struct(shape, f32),
            struct(shape, f32),
            struct((1, channels), f32),
            struct((per_clip, 8, channels), f32),
        ),
        (spatial, stats, cot, cot_halo, w_temporal, params),
        flops=2 * positions * 3 * channels * channels,
    )
    act_halo = lax.ppermute(act, "seq", ahead_pairs)
    sums = exchange(own, "seq", clips)
    encoded = call(
        encode_kernel,
        struct(shape, bf16),
        (act, act_halo, w_temporal),
        flops=2 * positions * 3 * channels * channels,
    )
    encoded, sums = lax.optimization_barrier((encoded, sums))
    rows = -(-12 * channels // (16 * devices)) * 16
    grads = call(
        functools.partial(grad_kernel, loss_scale),
        struct((devices, rows + EXTRA, channels), bf16),
        (odd, even, normed, pre, inv, own, sums, params, act, cot, cot_halo),
        flops=2 * positions * 12 * channels * channels,
    )
    grads = exchange(grads, ("dp", "seq"))
    grads, grad_gain, grad_shift = call(
        sum_kernel,
        (
            struct((devices, rows, channels), bf16),
            struct((1, channels), f32),
            struct((1, channels), f32),
        ),
        (grads,),
    )
    grads = exchange(grads, ("dp", "seq"))
    grad_spatial, grad_temporal = call(
        final_kernel,
        (struct((9 * channels, channels), f32), struct((3 * channels, channels), f32)),
        (grads.reshape(devices * rows, channels),),
    )
    return (
        encoded[None],
        grad_spatial.reshape(3, 3, channels, channels),
        grad_temporal.reshape(3, channels, channels),
        grad_gain[0],
        grad_shift[0],
    )


def solution(mesh):
    placed = P("dp", "seq", None, None, None)
    return jax.shard_map(
        on_device,
        mesh=mesh,
        in_specs=(placed, P(), P(), P(), P(), placed),
        out_specs=(placed, P(), P(), P(), P()),
        check_vma=False,
    )
```

```python
import functools
import math

import jax
import jax.numpy as jnp
from jax import lax
from jax.experimental import pallas as pl
from jax.experimental.pallas import tpu as pltpu
from jax.sharding import PartitionSpec as P

GROUPS = 32
FRAMES = 8
STEP_ROWS = 8
EXTRA = 8
SPARE_BYTES = 4 * 1024 * 1024

WHOLE = pl.BlockSpec(memory_space=pltpu.VMEM)
FAR = pl.BlockSpec(memory_space=pltpu.HBM)


def dot(left, right):
    return jnp.dot(left, right, preferred_element_type=jnp.float32)


def dot_transposed(left, right):
    return lax.dot_general(
        left, right, (((1,), (1,)), ((), ())), preferred_element_type=jnp.float32
    )


def each(count, body):
    if count <= 8:
        for step in range(count):
            body(step)
    else:
        lax.fori_loop(0, count, lambda step, carry: (body(step), carry)[1], 0)


def call(kernel, out_shape, operands, specs=None, scratch=(), flops=0):
    sizes = [value.size * value.dtype.itemsize for value in operands]
    sizes += [value.size * value.dtype.itemsize for value in jax.tree.leaves(out_shape)]
    held = sum(math.prod(item.shape) * 4 for item in scratch if hasattr(item, "shape"))
    return pl.pallas_call(
        kernel,
        out_shape=out_shape,
        in_specs=specs or [WHOLE] * len(operands),
        out_specs=jax.tree.map(lambda _: WHOLE, out_shape),
        scratch_shapes=list(scratch),
        compiler_params=pltpu.CompilerParams(vmem_limit_bytes=sum(sizes) + held + SPARE_BYTES),
        cost_estimate=pl.CostEstimate(
            flops=flops, bytes_accessed=sum(sizes), transcendentals=0
        ),
    )(*operands)


def group_spread(values, lanes):
    channels = values.shape[-1]
    shift = 1
    while shift < lanes:
        values = values + pltpu.roll(values, channels - shift, 1)
        shift *= 2
    lane = lax.broadcasted_iota(jnp.int32, values.shape, 1)
    values = jnp.where(lax.rem(lane, lanes) == 0, values, 0.0)
    shift = 1
    while shift < lanes:
        values = values + pltpu.roll(values, shift, 1)
        shift *= 2
    return values


def conv_kernel(
    video_far, weights_far, gain_far, shift_far, spatial, stats, odd, even, params, wide, video,
    weights, arrived,
):
    frames, height, width, channels = video.shape
    out_rows, out_cols = height // 2, width // 2
    positions = frames * out_rows * out_cols
    pieces = arrived.shape[0] - 3
    half = height * frames // pieces
    copies = []
    for piece in range(pieces):
        rows = pl.ds(piece * half % height, half)
        at = (piece * half // height, rows)
        copies.append(pltpu.make_async_copy(video_far.at[at], video.at[at], arrived.at[piece]))
    small = [
        pltpu.make_async_copy(source, target, arrived.at[pieces + index])
        for index, (source, target) in enumerate(
            ((weights_far, weights), (gain_far, params.at[0:1]), (shift_far, params.at[1:2]))
        )
    ]
    copies[0].start()
    small[0].start()
    for copy in copies[1:]:
        copy.start()
    for copy in small[1:]:
        copy.start()
    for slot in range(2 * STEP_ROWS):
        wide[slot, 0:8] = jnp.zeros((8, channels), jnp.float32)

    for frame in range(frames):
        odd[frame, 0] = jnp.zeros((out_cols, 3 * channels), jnp.bfloat16)

    for piece in range(pieces):
        frame = piece * half // height
        base = piece * half % height // 2 // STEP_ROWS
        copies[piece].wait()

        def separate(step, frame=frame, base=base):
            step = base + step
            for row in range(STEP_ROWS):
                for parity in range(2):
                    slot = 2 * row + parity
                    wide[slot, 8 : 8 + width] = video[
                        frame, 2 * (step * STEP_ROWS + row) + parity
                    ].astype(jnp.float32)
            for row in range(STEP_ROWS):
                for parity in range(2):
                    slot = 2 * row + parity
                    for tap in range(3):
                        value = wide[slot, pl.ds(7 + tap, out_cols, stride=2), :].astype(
                            jnp.bfloat16
                        )
                        lanes = slice(tap * channels, (tap + 1) * channels)
                        if parity:
                            odd[frame, step * STEP_ROWS + row + 1, :, lanes] = value
                        else:
                            even[frame, step * STEP_ROWS + row, :, lanes] = value

        each(half // 2 // STEP_ROWS, separate)
        if piece == 0:
            small[0].wait()

        def multiply(step, frame=frame, base=base):
            step = base + step
            flat = (STEP_ROWS * out_cols, 3 * channels)
            first = step * STEP_ROWS
            total = dot(odd[frame, pl.ds(first, STEP_ROWS)].reshape(flat), weights[0])
            total += dot(even[frame, pl.ds(first, STEP_ROWS)].reshape(flat), weights[1])
            total += dot(odd[frame, pl.ds(first + 1, STEP_ROWS)].reshape(flat), weights[2])
            spatial[frame, pl.ds(first, STEP_ROWS)] = total.reshape(STEP_ROWS, out_cols, channels)

        each(half // 2 // STEP_ROWS, multiply)

    steps = positions // (STEP_ROWS * out_cols)
    per_frame = out_rows // STEP_ROWS

    def block(step):
        return spatial[step // per_frame, pl.ds((step % per_frame) * STEP_ROWS, STEP_ROWS)]

    def fold(values):
        return values.reshape(-1, 8, channels).sum(axis=0)

    def fold_all(term):
        if steps <= 8:
            total = term(0)
            for step in range(1, steps):
                total += term(step)
            return total
        return lax.fori_loop(
            0, steps, lambda step, total: total + term(step), jnp.zeros((8, channels), jnp.float32)
        )

    mean = fold_all(lambda step: fold(block(step))).sum(axis=0, keepdims=True) / positions
    square = fold_all(lambda step: fold((block(step) - mean) ** 2)).sum(axis=0, keepdims=True)
    row = lax.broadcasted_iota(jnp.int32, (8, channels), 0)
    packed = jnp.where(row == 0, mean, jnp.where(row == 1, square, 0.0))
    for slot in range(stats.shape[0]):
        stats[slot] = packed
    for copy in small[1:]:
        copy.wait()


def clip_norm(stats, positions, lanes):
    cells = stats.shape[0] * lanes
    means = [stats[member, 0:1] for member in range(stats.shape[0])]
    squares = [stats[member, 1:2] for member in range(stats.shape[0])]
    mean = group_spread(jnp.broadcast_to(sum(means), (8, means[0].shape[-1])), lanes)[0:1] / cells
    square = sum(squares)
    for value in means:
        square = square + positions * (value - mean) ** 2
    square = group_spread(jnp.broadcast_to(square, (8, square.shape[-1])), lanes)[0:1]
    return mean, lax.rsqrt(square / (cells * positions) + 1e-05)


def act_kernel(
    loss_scale, spatial, stats, cot, halo, weights, params, act, normed, pre, temporal, sums
):
    frames, out_rows, out_cols, channels = spatial.shape
    positions = frames * out_rows * out_cols
    mean, inv_std = clip_norm(stats, positions, channels // GROUPS)
    gain, shift = params[0:1], params[1:2]
    flat = (STEP_ROWS * out_cols, channels)
    shaped = (STEP_ROWS, out_cols, channels)
    sums_shift = jnp.zeros((8, channels), jnp.float32)
    sums_gain = jnp.zeros((8, channels), jnp.float32)

    def fold(values):
        return values.reshape(-1, 8, channels).sum(axis=0)

    for frame in range(frames):

        def cot_block(later, rows):
            if frame + later < frames:
                return cot[frame + later, rows].reshape(flat)
            return halo[frame + later - frames, rows].reshape(flat)

        def one(step, carry):
            rows = pl.ds(step * STEP_ROWS, STEP_ROWS)
            norm = (spatial[frame, rows].reshape(flat) - mean) * inv_std
            before = norm * gain + shift
            sig = jax.nn.sigmoid(before)
            act[frame, rows] = (before * sig).astype(jnp.bfloat16).reshape(shaped)
            back = dot_transposed(cot_block(0, rows), weights[0])
            back += dot_transposed(cot_block(1, rows), weights[1])
            back += dot_transposed(cot_block(2, rows), weights[2])
            back = back.astype(jnp.bfloat16).astype(jnp.float32)
            back_pre = back * loss_scale * sig * (1.0 + before * (1.0 - sig))
            normed[frame, rows] = norm.reshape(shaped)
            pre[frame, rows] = (back_pre * (gain * inv_std)).reshape(shaped)
            return (carry[0] + fold(back_pre), carry[1] + fold(back_pre * norm))

        steps = out_rows // STEP_ROWS
        if steps <= 4:
            for step in range(steps):
                sums_shift, sums_gain = one(step, (sums_shift, sums_gain))
        else:
            sums_shift, sums_gain = lax.fori_loop(0, steps, one, (sums_shift, sums_gain))

    sums_shift = sums_shift.sum(axis=0, keepdims=True)
    sums_gain = sums_gain.sum(axis=0, keepdims=True)
    row = lax.broadcasted_iota(jnp.int32, (8, channels), 0)
    packed = jnp.zeros((8, channels), jnp.float32)
    for index, value in enumerate(
        (sums_shift, sums_gain, gain * sums_shift, gain * sums_gain, inv_std)
    ):
        packed = jnp.where(row == index, value, packed)
    for slot in range(sums.shape[0]):
        sums[slot] = packed

    all_rows = (out_rows * out_cols, channels)
    parts = [None, None, None]
    for frame in range(frames):
        turned = act[frame].reshape(all_rows).T
        for later in range(3):
            value = cot[frame + later] if frame + later < frames else halo[frame + later - frames]
            term = dot(turned, value.reshape(all_rows))
            parts[later] = term if parts[later] is None else parts[later] + term
    for later in range(3):
        temporal[pl.ds(later * channels, channels)] = (parts[later] * loss_scale).astype(
            jnp.bfloat16
        )


def split_rows(values, rows):
    pieces = []
    for value in values:
        rest = value
        for _ in range(3):
            piece = rest.astype(jnp.bfloat16).astype(jnp.float32)
            pieces.append(piece)
            rest = rest - piece
    row = lax.broadcasted_iota(jnp.int32, (rows, values[0].shape[-1]), 0)
    packed = jnp.zeros((rows, values[0].shape[-1]), jnp.float32)
    for index, piece in enumerate(pieces):
        packed = jnp.where(row == index, piece, packed)
    return packed.astype(jnp.bfloat16)


def join_rows(packed, count):
    return [
        packed[3 * i : 3 * i + 1] + packed[3 * i + 1 : 3 * i + 2] + packed[3 * i + 2 : 3 * i + 3]
        for i in range(count)
    ]


def store_rows(chunks, rows, first, values):
    done = 0
    while done < values.shape[0]:
        chunk, at = divmod(first + done, rows)
        count = min(rows - at, values.shape[0] - done)
        chunks[chunk, pl.ds(at, count)] = values[done : done + count]
        done += count


def grad_kernel(
    odd, even, normed, pre, sums, temporal, act, act_halo, weights, grads, encoded
):
    frames, out_rows, out_cols, channels = normed.shape
    lanes = channels // GROUPS
    members = sums.shape[0] * frames * out_rows * out_cols * lanes
    clip = jnp.sum(sums[...], axis=0)
    inv_std = sums[0, 4:5]
    group = group_spread(clip, lanes) * inv_std / members
    group_shift, group_gain = group[2:3], group[3:4]
    flat = (out_rows * out_cols, channels)
    flat_wide = (out_rows * out_cols, 3 * channels)
    rows = grads.shape[1] - EXTRA
    parts = [None, None, None]
    for frame in range(frames):
        back = (
            pre[frame].reshape(flat) - group_shift - normed[frame].reshape(flat) * group_gain
        )
        back = back.astype(jnp.bfloat16).T
        for tap, source in enumerate(
            (odd.at[frame, pl.ds(0, out_rows)], even.at[frame], odd.at[frame, pl.ds(1, out_rows)])
        ):
            term = dot(back, source[...].reshape(flat_wide))
            parts[tap] = term if parts[tap] is None else parts[tap] + term
    for tap in range(3):
        for side in range(3):
            block = parts[tap][:, side * channels : (side + 1) * channels].T
            store_rows(grads, rows, (3 * tap + side) * channels, block.astype(jnp.bfloat16))
    for tap in range(3):
        block = temporal[pl.ds(tap * channels, channels)]
        store_rows(grads, rows, (9 + tap) * channels, block)
    rest = grads.shape[0] * rows - 12 * channels
    if rest:
        store_rows(grads, rows, 12 * channels, jnp.zeros((rest, channels), jnp.bfloat16))
    share = clip * (1.0 / sums.shape[0])
    extra = split_rows([share[1:2], share[0:1]], EXTRA)
    for chunk in range(grads.shape[0]):
        grads[chunk, pl.ds(rows, EXTRA)] = extra
    encode(act, act_halo, weights, encoded)


def total_of(arrived, first, count):
    total = arrived[0, pl.ds(first, count)].astype(jnp.float32)
    for chunk in range(1, arrived.shape[0]):
        total += arrived[chunk, pl.ds(first, count)].astype(jnp.float32)
    return total


def sum_kernel(arrived, spread, grad_gain, grad_shift):
    count = spread.shape[1]
    total = total_of(arrived, 0, count).astype(jnp.bfloat16)
    for slot in range(spread.shape[0]):
        spread[slot] = total
    grad_gain[...], grad_shift[...] = join_rows(total_of(arrived, count, EXTRA), 2)


def final_kernel(arrived, grad_spatial, grad_temporal):
    rows = grad_spatial.shape[0]
    grad_spatial[...] = arrived[pl.ds(0, rows)].astype(jnp.float32)
    grad_temporal[...] = arrived[pl.ds(rows, grad_temporal.shape[0])].astype(jnp.float32)


def encode(act, halo, weights, encoded):
    frames, out_rows, out_cols, channels = act.shape
    flat = (STEP_ROWS * out_cols, channels)
    for frame in range(frames):

        def one(step, frame=frame):
            rows = pl.ds(step * STEP_ROWS, STEP_ROWS)
            total = None
            for tap in range(3):
                source = (
                    act[frame - tap, rows] if frame >= tap else halo[frames + frame - tap, rows]
                )
                term = dot(source.reshape(flat), weights[tap])
                total = term if total is None else total + term
            encoded[frame, rows] = total.astype(jnp.bfloat16).reshape(
                STEP_ROWS, out_cols, channels
            )

        each(out_rows // STEP_ROWS, one)


def on_device(video_in, w_spatial, w_temporal, norm_gain, norm_shift, cotangent):
    frames, height, width, channels = video_in.shape[1:]
    out_rows, out_cols = height // 2, width // 2
    dp_size, seq_size = lax.axis_size("dp"), lax.axis_size("seq")
    devices = dp_size * seq_size
    per_clip = FRAMES // frames
    assert frames >= 2 and FRAMES % frames == 0
    loss_scale = float(devices * frames * out_rows * out_cols) ** (-0.5)
    shape = (frames, out_rows, out_cols, channels)
    positions = frames * out_rows * out_cols
    video = video_in[0]
    cot = cotangent[0]
    f32, bf16 = jnp.float32, jnp.bfloat16
    struct = jax.ShapeDtypeStruct

    back_pairs = [(s, s - 1) for s in range(seq_size) if s % per_clip]
    ahead_pairs = [(s - 1, s) for s in range(seq_size) if s % per_clip]
    clips = [list(range(first, first + per_clip)) for first in range(0, seq_size, per_clip)]

    def exchange(value, axes, groups=None):
        return lax.all_to_all(value, axes, 0, 0, axis_index_groups=groups, tiled=True)

    def far(value):
        return pltpu.with_memory_space_constraint(value, pltpu.HBM)

    cot_halo = lax.ppermute(cot, "seq", back_pairs)

    pieces = 2 * frames
    spatial, stats, odd, even, params = call(
        conv_kernel,
        (
            struct(shape, f32),
            struct((per_clip, 8, channels), f32),
            struct((frames, out_rows + 1, out_cols, 3 * channels), bf16),
            struct((frames, out_rows, out_cols, 3 * channels), bf16),
            struct((8, channels), f32),
        ),
        (
            far(video),
            far(w_spatial.reshape(3, 3 * channels, channels)),
            far(norm_gain[None]),
            far(norm_shift[None]),
        ),
        specs=[FAR] * 4,
        scratch=[
            pltpu.VMEM((2 * STEP_ROWS, 8 + width, channels), f32),
            pltpu.VMEM(video.shape, bf16),
            pltpu.VMEM((3, 3 * channels, channels), bf16),
            pltpu.SemaphoreType.DMA((pieces + 3,)),
        ],
        flops=2 * positions * 9 * channels * channels,
    )
    stats = exchange(stats, "seq", clips)
    act, normed, pre, temporal, own = call(
        functools.partial(act_kernel, loss_scale),
        (
            struct(shape, bf16),
            struct(shape, f32),
            struct(shape, f32),
            struct((3 * channels, channels), bf16),
            struct((per_clip, 8, channels), f32),
        ),
        (spatial, stats, cot, cot_halo, w_temporal, params),
        flops=2 * positions * 3 * channels * channels,
    )
    act_halo = lax.ppermute(act, "seq", ahead_pairs)
    sums = exchange(own, "seq", clips)
    rows = -(-12 * channels // (16 * devices)) * 16
    grads, encoded = call(
        grad_kernel,
        (struct((devices, rows + EXTRA, channels), bf16), struct(shape, bf16)),
        (odd, even, normed, pre, sums, temporal, act, act_halo, w_temporal),
        flops=2 * positions * 12 * channels * channels,
    )
    grads = exchange(grads, ("dp", "seq"))
    grads, grad_gain, grad_shift = call(
        sum_kernel,
        (
            struct((devices, rows, channels), bf16),
            struct((1, channels), f32),
            struct((1, channels), f32),
        ),
        (grads,),
    )
    grads = exchange(grads, ("dp", "seq"))
    grad_spatial, grad_temporal = call(
        final_kernel,
        (struct((9 * channels, channels), f32), struct((3 * channels, channels), f32)),
        (grads.reshape(devices * rows, channels),),
    )
    return (
        encoded[None],
        grad_spatial.reshape(3, 3, channels, channels),
        grad_temporal.reshape(3, channels, channels),
        grad_gain[0],
        grad_shift[0],
    )


def solution(mesh):
    placed = P("dp", "seq", None, None, None)
    return jax.shard_map(
        on_device,
        mesh=mesh,
        in_specs=(placed, P(), P(), P(), P(), placed),
        out_specs=(placed, P(), P(), P(), P()),
        check_vma=False,
    )
```

```python
import functools
import math

import jax
import jax.numpy as jnp
from jax import lax
from jax.experimental import pallas as pl
from jax.experimental.pallas import tpu as pltpu
from jax.sharding import PartitionSpec as P

GROUPS = 32
FRAMES = 8
STEP_ROWS = 8
EXTRA = 8
SPARE_BYTES = 4 * 1024 * 1024

WHOLE = pl.BlockSpec(memory_space=pltpu.VMEM)
FAR = pl.BlockSpec(memory_space=pltpu.HBM)


def dot(left, right):
    return jnp.dot(left, right, preferred_element_type=jnp.float32)


def dot_transposed(left, right):
    return lax.dot_general(
        left, right, (((1,), (1,)), ((), ())), preferred_element_type=jnp.float32
    )


def each(count, body):
    if count <= 8:
        for step in range(count):
            body(step)
    else:
        lax.fori_loop(0, count, lambda step, carry: (body(step), carry)[1], 0)


def call(kernel, out_shape, operands, specs=None, scratch=(), flops=0):
    sizes = [value.size * value.dtype.itemsize for value in operands]
    sizes += [value.size * value.dtype.itemsize for value in jax.tree.leaves(out_shape)]
    held = sum(math.prod(item.shape) * 4 for item in scratch if hasattr(item, "shape"))
    return pl.pallas_call(
        kernel,
        out_shape=out_shape,
        in_specs=specs or [WHOLE] * len(operands),
        out_specs=jax.tree.map(lambda _: WHOLE, out_shape),
        scratch_shapes=list(scratch),
        compiler_params=pltpu.CompilerParams(vmem_limit_bytes=sum(sizes) + held + SPARE_BYTES),
        cost_estimate=pl.CostEstimate(
            flops=flops, bytes_accessed=sum(sizes), transcendentals=0
        ),
    )(*operands)


def group_spread(values, lanes):
    channels = values.shape[-1]
    shift = 1
    while shift < lanes:
        values = values + pltpu.roll(values, channels - shift, 1)
        shift *= 2
    lane = lax.broadcasted_iota(jnp.int32, values.shape, 1)
    values = jnp.where(lax.rem(lane, lanes) == 0, values, 0.0)
    shift = 1
    while shift < lanes:
        values = values + pltpu.roll(values, shift, 1)
        shift *= 2
    return values


def conv_kernel(
    video_far, weights_far, gain_far, shift_far, spatial, stats, odd, even, params, wide, video,
    weights, arrived,
):
    frames, height, width, channels = video.shape
    out_rows, out_cols = height // 2, width // 2
    positions = frames * out_rows * out_cols
    pieces = arrived.shape[0] - 3
    half = height * frames // pieces
    copies = []
    for piece in range(pieces):
        rows = pl.ds(piece * half % height, half)
        at = (piece * half // height, rows)
        copies.append(pltpu.make_async_copy(video_far.at[at], video.at[at], arrived.at[piece]))
    small = [
        pltpu.make_async_copy(source, target, arrived.at[pieces + index])
        for index, (source, target) in enumerate(
            ((weights_far, weights), (gain_far, params.at[0:1]), (shift_far, params.at[1:2]))
        )
    ]
    copies[0].start()
    small[0].start()
    for copy in copies[1:]:
        copy.start()
    for copy in small[1:]:
        copy.start()
    for slot in range(2 * STEP_ROWS):
        wide[slot, 0:8] = jnp.zeros((8, channels), jnp.float32)

    for frame in range(frames):
        odd[frame, 0] = jnp.zeros((out_cols, 3 * channels), jnp.bfloat16)

    for piece in range(pieces):
        frame = piece * half // height
        base = piece * half % height // 2 // STEP_ROWS
        copies[piece].wait()

        def separate(step, frame=frame, base=base):
            step = base + step
            for row in range(STEP_ROWS):
                for parity in range(2):
                    slot = 2 * row + parity
                    wide[slot, 8 : 8 + width] = video[
                        frame, 2 * (step * STEP_ROWS + row) + parity
                    ].astype(jnp.float32)
            for row in range(STEP_ROWS):
                for parity in range(2):
                    slot = 2 * row + parity
                    for tap in range(3):
                        value = wide[slot, pl.ds(7 + tap, out_cols, stride=2), :].astype(
                            jnp.bfloat16
                        )
                        lanes = slice(tap * channels, (tap + 1) * channels)
                        if parity:
                            odd[frame, step * STEP_ROWS + row + 1, :, lanes] = value
                        else:
                            even[frame, step * STEP_ROWS + row, :, lanes] = value

        each(half // 2 // STEP_ROWS, separate)
        if piece == 0:
            small[0].wait()

        def multiply(step, frame=frame, base=base):
            step = base + step
            flat = (STEP_ROWS * out_cols, 3 * channels)
            first = step * STEP_ROWS
            total = dot(odd[frame, pl.ds(first, STEP_ROWS)].reshape(flat), weights[0])
            total += dot(even[frame, pl.ds(first, STEP_ROWS)].reshape(flat), weights[1])
            total += dot(odd[frame, pl.ds(first + 1, STEP_ROWS)].reshape(flat), weights[2])
            spatial[frame, pl.ds(first, STEP_ROWS)] = total.reshape(STEP_ROWS, out_cols, channels)

        each(half // 2 // STEP_ROWS, multiply)

    steps = positions // (STEP_ROWS * out_cols)
    per_frame = out_rows // STEP_ROWS

    def block(step):
        return spatial[step // per_frame, pl.ds((step % per_frame) * STEP_ROWS, STEP_ROWS)]

    def fold(values):
        return values.reshape(-1, 8, channels).sum(axis=0)

    def fold_all(term):
        if steps <= 8:
            total = term(0)
            for step in range(1, steps):
                total += term(step)
            return total
        return lax.fori_loop(
            0, steps, lambda step, total: total + term(step), jnp.zeros((8, channels), jnp.float32)
        )

    mean = fold_all(lambda step: fold(block(step))).sum(axis=0, keepdims=True) / positions
    square = fold_all(lambda step: fold((block(step) - mean) ** 2)).sum(axis=0, keepdims=True)
    row = lax.broadcasted_iota(jnp.int32, (8, channels), 0)
    packed = jnp.where(row == 0, mean, jnp.where(row == 1, square, 0.0))
    for slot in range(stats.shape[0]):
        stats[slot] = packed
    for copy in small[1:]:
        copy.wait()


def clip_norm(stats, positions, lanes):
    cells = stats.shape[0] * lanes
    means = [stats[member, 0:1] for member in range(stats.shape[0])]
    squares = [stats[member, 1:2] for member in range(stats.shape[0])]
    mean = group_spread(jnp.broadcast_to(sum(means), (8, means[0].shape[-1])), lanes)[0:1] / cells
    square = sum(squares)
    for value in means:
        square = square + positions * (value - mean) ** 2
    square = group_spread(jnp.broadcast_to(square, (8, square.shape[-1])), lanes)[0:1]
    return mean, lax.rsqrt(square / (cells * positions) + 1e-05)


def act_kernel(
    loss_scale, spatial, stats, cot, halo, weights, params, act, normed, pre, temporal, sums
):
    frames, out_rows, out_cols, channels = spatial.shape
    positions = frames * out_rows * out_cols
    mean, inv_std = clip_norm(stats, positions, channels // GROUPS)
    gain, shift = params[0:1], params[1:2]
    flat = (STEP_ROWS * out_cols, channels)
    shaped = (STEP_ROWS, out_cols, channels)
    sums_shift = jnp.zeros((8, channels), jnp.float32)
    sums_gain = jnp.zeros((8, channels), jnp.float32)

    def fold(values):
        return values.reshape(-1, 8, channels).sum(axis=0)

    for frame in range(frames):

        def cot_block(later, rows):
            if frame + later < frames:
                return cot[frame + later, rows].reshape(flat)
            return halo[frame + later - frames, rows].reshape(flat)

        def one(step, carry):
            rows = pl.ds(step * STEP_ROWS, STEP_ROWS)
            norm = (spatial[frame, rows].reshape(flat) - mean) * inv_std
            before = norm * gain + shift
            sig = jax.nn.sigmoid(before)
            act[frame, rows] = (before * sig).astype(jnp.bfloat16).reshape(shaped)
            back = dot_transposed(cot_block(0, rows), weights[0])
            back += dot_transposed(cot_block(1, rows), weights[1])
            back += dot_transposed(cot_block(2, rows), weights[2])
            back = back.astype(jnp.bfloat16).astype(jnp.float32)
            back_pre = back * loss_scale * sig * (1.0 + before * (1.0 - sig))
            normed[frame, rows] = norm.reshape(shaped)
            pre[frame, rows] = (back_pre * (gain * inv_std)).reshape(shaped)
            return (carry[0] + fold(back_pre), carry[1] + fold(back_pre * norm))

        steps = out_rows // STEP_ROWS
        if steps <= 4:
            for step in range(steps):
                sums_shift, sums_gain = one(step, (sums_shift, sums_gain))
        else:
            sums_shift, sums_gain = lax.fori_loop(0, steps, one, (sums_shift, sums_gain))

    sums_shift = sums_shift.sum(axis=0, keepdims=True)
    sums_gain = sums_gain.sum(axis=0, keepdims=True)
    row = lax.broadcasted_iota(jnp.int32, (8, channels), 0)
    packed = jnp.zeros((8, channels), jnp.float32)
    for index, value in enumerate(
        (sums_shift, sums_gain, gain * sums_shift, gain * sums_gain, inv_std)
    ):
        packed = jnp.where(row == index, value, packed)
    for slot in range(sums.shape[0]):
        sums[slot] = packed

    all_rows = (out_rows * out_cols, channels)
    parts = [None, None, None]
    for frame in range(frames):
        turned = act[frame].reshape(all_rows).T
        for later in range(3):
            value = cot[frame + later] if frame + later < frames else halo[frame + later - frames]
            term = dot(turned, value.reshape(all_rows))
            parts[later] = term if parts[later] is None else parts[later] + term
    for later in range(3):
        temporal[pl.ds(later * channels, channels)] = (parts[later] * loss_scale).astype(
            jnp.bfloat16
        )


def split_rows(values, rows):
    pieces = []
    for value in values:
        rest = value
        for _ in range(3):
            piece = rest.astype(jnp.bfloat16).astype(jnp.float32)
            pieces.append(piece)
            rest = rest - piece
    row = lax.broadcasted_iota(jnp.int32, (rows, values[0].shape[-1]), 0)
    packed = jnp.zeros((rows, values[0].shape[-1]), jnp.float32)
    for index, piece in enumerate(pieces):
        packed = jnp.where(row == index, piece, packed)
    return packed.astype(jnp.bfloat16)


def join_rows(packed, count):
    return [
        packed[3 * i : 3 * i + 1] + packed[3 * i + 1 : 3 * i + 2] + packed[3 * i + 2 : 3 * i + 3]
        for i in range(count)
    ]


def store_rows(chunks, rows, first, values):
    done = 0
    while done < values.shape[0]:
        chunk, at = divmod(first + done, rows)
        count = min(rows - at, values.shape[0] - done)
        chunks[chunk, pl.ds(at, count)] = values[done : done + count]
        done += count


def grad_kernel(
    odd, even, normed, pre, sums, temporal, act, act_halo, weights, grads, encoded
):
    frames, out_rows, out_cols, channels = normed.shape
    lanes = channels // GROUPS
    members = sums.shape[0] * frames * out_rows * out_cols * lanes
    clip = jnp.sum(sums[...], axis=0)
    inv_std = sums[0, 4:5]
    group = group_spread(clip, lanes) * inv_std / members
    group_shift, group_gain = group[2:3], group[3:4]
    flat = (out_rows * out_cols, channels)
    flat_wide = (out_rows * out_cols, 3 * channels)
    rows = grads.shape[1] - EXTRA
    parts = [None, None, None]
    for frame in range(frames):
        back = (
            pre[frame].reshape(flat) - group_shift - normed[frame].reshape(flat) * group_gain
        )
        back = back.astype(jnp.bfloat16).T
        for tap, source in enumerate(
            (odd.at[frame, pl.ds(0, out_rows)], even.at[frame], odd.at[frame, pl.ds(1, out_rows)])
        ):
            term = dot(back, source[...].reshape(flat_wide))
            parts[tap] = term if parts[tap] is None else parts[tap] + term
    for tap in range(3):
        for side in range(3):
            block = parts[tap][:, side * channels : (side + 1) * channels].T
            store_rows(grads, rows, (3 * tap + side) * channels, block.astype(jnp.bfloat16))
    for tap in range(3):
        block = temporal[pl.ds(tap * channels, channels)]
        store_rows(grads, rows, (9 + tap) * channels, block)
    rest = grads.shape[0] * rows - 12 * channels
    if rest:
        store_rows(grads, rows, 12 * channels, jnp.zeros((rest, channels), jnp.bfloat16))
    share = clip * (1.0 / sums.shape[0])
    extra = split_rows([share[1:2], share[0:1]], EXTRA)
    for chunk in range(grads.shape[0]):
        grads[chunk, pl.ds(rows, EXTRA)] = extra
    encode(act, act_halo, weights, encoded)


def total_of(arrived, first, count):
    total = arrived[0, pl.ds(first, count)].astype(jnp.float32)
    for chunk in range(1, arrived.shape[0]):
        total += arrived[chunk, pl.ds(first, count)].astype(jnp.float32)
    return total


def sum_kernel(arrived, spread, grad_gain, grad_shift):
    count = spread.shape[0]
    total = total_of(arrived, 0, count).astype(jnp.bfloat16)
    spread[...] = total
    grad_gain[...], grad_shift[...] = join_rows(total_of(arrived, count, EXTRA), 2)


def final_kernel(arrived, grad_spatial, grad_temporal):
    rows = grad_spatial.shape[0]
    grad_spatial[...] = arrived[pl.ds(0, rows)].astype(jnp.float32)
    grad_temporal[...] = arrived[pl.ds(rows, grad_temporal.shape[0])].astype(jnp.float32)


def encode(act, halo, weights, encoded):
    frames, out_rows, out_cols, channels = act.shape
    flat = (STEP_ROWS * out_cols, channels)
    for frame in range(frames):

        def one(step, frame=frame):
            rows = pl.ds(step * STEP_ROWS, STEP_ROWS)
            total = None
            for tap in range(3):
                source = (
                    act[frame - tap, rows] if frame >= tap else halo[frames + frame - tap, rows]
                )
                term = dot(source.reshape(flat), weights[tap])
                total = term if total is None else total + term
            encoded[frame, rows] = total.astype(jnp.bfloat16).reshape(
                STEP_ROWS, out_cols, channels
            )

        each(out_rows // STEP_ROWS, one)


def on_device(video_in, w_spatial, w_temporal, norm_gain, norm_shift, cotangent):
    frames, height, width, channels = video_in.shape[1:]
    out_rows, out_cols = height // 2, width // 2
    dp_size, seq_size = lax.axis_size("dp"), lax.axis_size("seq")
    devices = dp_size * seq_size
    per_clip = FRAMES // frames
    assert frames >= 2 and FRAMES % frames == 0
    loss_scale = float(devices * frames * out_rows * out_cols) ** (-0.5)
    shape = (frames, out_rows, out_cols, channels)
    positions = frames * out_rows * out_cols
    video = video_in[0]
    cot = cotangent[0]
    f32, bf16 = jnp.float32, jnp.bfloat16
    struct = jax.ShapeDtypeStruct

    back_pairs = [(s, s - 1) for s in range(seq_size) if s % per_clip]
    ahead_pairs = [(s - 1, s) for s in range(seq_size) if s % per_clip]
    clips = [list(range(first, first + per_clip)) for first in range(0, seq_size, per_clip)]

    def exchange(value, axes, groups=None):
        return lax.all_to_all(value, axes, 0, 0, axis_index_groups=groups, tiled=True)

    def far(value):
        return pltpu.with_memory_space_constraint(value, pltpu.HBM)

    cot_halo = lax.ppermute(cot, "seq", back_pairs)

    pieces = 2 * frames
    spatial, stats, odd, even, params = call(
        conv_kernel,
        (
            struct(shape, f32),
            struct((per_clip, 8, channels), f32),
            struct((frames, out_rows + 1, out_cols, 3 * channels), bf16),
            struct((frames, out_rows, out_cols, 3 * channels), bf16),
            struct((8, channels), f32),
        ),
        (
            far(video),
            far(w_spatial.reshape(3, 3 * channels, channels)),
            far(norm_gain[None]),
            far(norm_shift[None]),
        ),
        specs=[FAR] * 4,
        scratch=[
            pltpu.VMEM((2 * STEP_ROWS, 8 + width, channels), f32),
            pltpu.VMEM(video.shape, bf16),
            pltpu.VMEM((3, 3 * channels, channels), bf16),
            pltpu.SemaphoreType.DMA((pieces + 3,)),
        ],
        flops=2 * positions * 9 * channels * channels,
    )
    stats = exchange(stats, "seq", clips)
    act, normed, pre, temporal, own = call(
        functools.partial(act_kernel, loss_scale),
        (
            struct(shape, bf16),
            struct(shape, f32),
            struct(shape, f32),
            struct((3 * channels, channels), bf16),
            struct((per_clip, 8, channels), f32),
        ),
        (spatial, stats, cot, cot_halo, w_temporal, params),
        flops=2 * positions * 3 * channels * channels,
    )
    act_halo = lax.ppermute(act, "seq", ahead_pairs)
    sums = exchange(own, "seq", clips)
    rows = -(-12 * channels // (16 * devices)) * 16
    grads, encoded = call(
        grad_kernel,
        (struct((devices, rows + EXTRA, channels), bf16), struct(shape, bf16)),
        (odd, even, normed, pre, sums, temporal, act, act_halo, w_temporal),
        flops=2 * positions * 12 * channels * channels,
    )
    grads = exchange(grads, ("dp", "seq"))
    grads, grad_gain, grad_shift = call(
        sum_kernel,
        (
            struct((rows, channels), bf16),
            struct((1, channels), f32),
            struct((1, channels), f32),
        ),
        (grads,),
    )
    grads = lax.all_gather(grads, ("dp", "seq"), axis=0, tiled=True)
    grad_spatial, grad_temporal = call(
        final_kernel,
        (struct((9 * channels, channels), f32), struct((3 * channels, channels), f32)),
        (grads,),
    )
    return (
        encoded[None],
        grad_spatial.reshape(3, 3, channels, channels),
        grad_temporal.reshape(3, channels, channels),
        grad_gain[0],
        grad_shift[0],
    )


def solution(mesh):
    placed = P("dp", "seq", None, None, None)
    return jax.shard_map(
        on_device,
        mesh=mesh,
        in_specs=(placed, P(), P(), P(), P(), placed),
        out_specs=(placed, P(), P(), P(), P()),
        check_vma=False,
    )
```

```python
import functools
import math

import jax
import jax.numpy as jnp
from jax import lax
from jax.experimental import pallas as pl
from jax.experimental.pallas import tpu as pltpu
from jax.sharding import PartitionSpec as P

GROUPS = 32
FRAMES = 8
STEP_ROWS = 8
EXTRA = 8
SPARE_BYTES = 4 * 1024 * 1024

WHOLE = pl.BlockSpec(memory_space=pltpu.VMEM)
FAR = pl.BlockSpec(memory_space=pltpu.HBM)


def dot(left, right):
    return jnp.dot(left, right, preferred_element_type=jnp.float32)


def dot_transposed(left, right):
    return lax.dot_general(
        left, right, (((1,), (1,)), ((), ())), preferred_element_type=jnp.float32
    )


def each(count, body):
    if count <= 8:
        for step in range(count):
            body(step)
    else:
        lax.fori_loop(0, count, lambda step, carry: (body(step), carry)[1], 0)


def call(kernel, out_shape, operands, specs=None, scratch=(), flops=0):
    sizes = [value.size * value.dtype.itemsize for value in operands]
    sizes += [value.size * value.dtype.itemsize for value in jax.tree.leaves(out_shape)]
    held = sum(math.prod(item.shape) * 4 for item in scratch if hasattr(item, "shape"))
    return pl.pallas_call(
        kernel,
        out_shape=out_shape,
        in_specs=specs or [WHOLE] * len(operands),
        out_specs=jax.tree.map(lambda _: WHOLE, out_shape),
        scratch_shapes=list(scratch),
        compiler_params=pltpu.CompilerParams(vmem_limit_bytes=sum(sizes) + held + SPARE_BYTES),
        cost_estimate=pl.CostEstimate(
            flops=flops, bytes_accessed=sum(sizes), transcendentals=0
        ),
    )(*operands)


def group_spread(values, lanes):
    channels = values.shape[-1]
    shift = 1
    while shift < lanes:
        values = values + pltpu.roll(values, channels - shift, 1)
        shift *= 2
    lane = lax.broadcasted_iota(jnp.int32, values.shape, 1)
    values = jnp.where(lax.rem(lane, lanes) == 0, values, 0.0)
    shift = 1
    while shift < lanes:
        values = values + pltpu.roll(values, shift, 1)
        shift *= 2
    return values


def conv_kernel(
    video_far, weights_far, gain_far, shift_far, spatial, stats, odd, even, params, wide, video,
    weights, arrived,
):
    frames, height, width, channels = video.shape
    out_rows, out_cols = height // 2, width // 2
    positions = frames * out_rows * out_cols
    pieces = arrived.shape[0] - 3
    half = height * frames // pieces
    copies = []
    for piece in range(pieces):
        rows = pl.ds(piece * half % height, half)
        at = (piece * half // height, rows)
        copies.append(pltpu.make_async_copy(video_far.at[at], video.at[at], arrived.at[piece]))
    small = [
        pltpu.make_async_copy(source, target, arrived.at[pieces + index])
        for index, (source, target) in enumerate(
            ((weights_far, weights), (gain_far, params.at[0:1]), (shift_far, params.at[1:2]))
        )
    ]
    copies[0].start()
    small[0].start()
    for copy in copies[1:]:
        copy.start()
    for copy in small[1:]:
        copy.start()
    for slot in range(2 * STEP_ROWS):
        wide[slot, 0:8] = jnp.zeros((8, channels), jnp.float32)

    for frame in range(frames):
        odd[frame, 0] = jnp.zeros((out_cols, 3 * channels), jnp.bfloat16)

    for piece in range(pieces):
        frame = piece * half // height
        base = piece * half % height // 2 // STEP_ROWS
        copies[piece].wait()

        def separate(step, frame=frame, base=base):
            step = base + step
            for row in range(STEP_ROWS):
                for parity in range(2):
                    slot = 2 * row + parity
                    wide[slot, 8 : 8 + width] = video[
                        frame, 2 * (step * STEP_ROWS + row) + parity
                    ].astype(jnp.float32)
            for row in range(STEP_ROWS):
                for parity in range(2):
                    slot = 2 * row + parity
                    for tap in range(3):
                        value = wide[slot, pl.ds(7 + tap, out_cols, stride=2), :].astype(
                            jnp.bfloat16
                        )
                        lanes = slice(tap * channels, (tap + 1) * channels)
                        if parity:
                            odd[frame, step * STEP_ROWS + row + 1, :, lanes] = value
                        else:
                            even[frame, step * STEP_ROWS + row, :, lanes] = value

        each(half // 2 // STEP_ROWS, separate)
        if piece == 0:
            small[0].wait()

        def multiply(step, frame=frame, base=base):
            step = base + step
            flat = (STEP_ROWS * out_cols, 3 * channels)
            first = step * STEP_ROWS
            total = dot(odd[frame, pl.ds(first, STEP_ROWS)].reshape(flat), weights[0])
            total += dot(even[frame, pl.ds(first, STEP_ROWS)].reshape(flat), weights[1])
            total += dot(odd[frame, pl.ds(first + 1, STEP_ROWS)].reshape(flat), weights[2])
            spatial[frame, pl.ds(first, STEP_ROWS)] = total.reshape(STEP_ROWS, out_cols, channels)

        each(half // 2 // STEP_ROWS, multiply)

    steps = positions // (STEP_ROWS * out_cols)
    per_frame = out_rows // STEP_ROWS

    def block(step):
        return spatial[step // per_frame, pl.ds((step % per_frame) * STEP_ROWS, STEP_ROWS)]

    def fold(values):
        return values.reshape(-1, 8, channels).sum(axis=0)

    def fold_all(term):
        if steps <= 8:
            total = term(0)
            for step in range(1, steps):
                total += term(step)
            return total
        return lax.fori_loop(
            0, steps, lambda step, total: total + term(step), jnp.zeros((8, channels), jnp.float32)
        )

    mean = fold_all(lambda step: fold(block(step))).sum(axis=0, keepdims=True) / positions
    square = fold_all(lambda step: fold((block(step) - mean) ** 2)).sum(axis=0, keepdims=True)
    row = lax.broadcasted_iota(jnp.int32, (8, channels), 0)
    packed = jnp.where(row == 0, mean, jnp.where(row == 1, square, 0.0))
    for slot in range(stats.shape[0]):
        stats[slot] = packed
    for copy in small[1:]:
        copy.wait()


def clip_norm(stats, positions, lanes):
    cells = stats.shape[0] * lanes
    means = [stats[member, 0:1] for member in range(stats.shape[0])]
    squares = [stats[member, 1:2] for member in range(stats.shape[0])]
    mean = group_spread(jnp.broadcast_to(sum(means), (8, means[0].shape[-1])), lanes)[0:1] / cells
    square = sum(squares)
    for value in means:
        square = square + positions * (value - mean) ** 2
    square = group_spread(jnp.broadcast_to(square, (8, square.shape[-1])), lanes)[0:1]
    return mean, lax.rsqrt(square / (cells * positions) + 1e-05)


def act_kernel(
    loss_scale, spatial, stats, cot, halo, weights, params, act, normed, pre, temporal, sums
):
    frames, out_rows, out_cols, channels = spatial.shape
    positions = frames * out_rows * out_cols
    mean, inv_std = clip_norm(stats, positions, channels // GROUPS)
    gain, shift = params[0:1], params[1:2]
    flat = (STEP_ROWS * out_cols, channels)
    shaped = (STEP_ROWS, out_cols, channels)
    sums_shift = jnp.zeros((8, channels), jnp.float32)
    sums_gain = jnp.zeros((8, channels), jnp.float32)

    def fold(values):
        return values.reshape(-1, 8, channels).sum(axis=0)

    for frame in range(frames):

        def cot_block(later, rows):
            if frame + later < frames:
                return cot[frame + later, rows].reshape(flat)
            return halo[frame + later - frames, rows].reshape(flat)

        def one(step, carry):
            rows = pl.ds(step * STEP_ROWS, STEP_ROWS)
            norm = (spatial[frame, rows].reshape(flat) - mean) * inv_std
            before = norm * gain + shift
            sig = jax.nn.sigmoid(before)
            act[frame, rows] = (before * sig).astype(jnp.bfloat16).reshape(shaped)
            back = dot_transposed(cot_block(0, rows), weights[0])
            back += dot_transposed(cot_block(1, rows), weights[1])
            back += dot_transposed(cot_block(2, rows), weights[2])
            back = back.astype(jnp.bfloat16).astype(jnp.float32)
            back_pre = back * loss_scale * sig * (1.0 + before * (1.0 - sig))
            normed[frame, rows] = norm.reshape(shaped)
            pre[frame, rows] = (back_pre * (gain * inv_std)).reshape(shaped)
            return (carry[0] + fold(back_pre), carry[1] + fold(back_pre * norm))

        steps = out_rows // STEP_ROWS
        if steps <= 4:
            for step in range(steps):
                sums_shift, sums_gain = one(step, (sums_shift, sums_gain))
        else:
            sums_shift, sums_gain = lax.fori_loop(0, steps, one, (sums_shift, sums_gain))

    sums_shift = sums_shift.sum(axis=0, keepdims=True)
    sums_gain = sums_gain.sum(axis=0, keepdims=True)
    row = lax.broadcasted_iota(jnp.int32, (8, channels), 0)
    packed = jnp.zeros((8, channels), jnp.float32)
    for index, value in enumerate(
        (sums_shift, sums_gain, gain * sums_shift, gain * sums_gain, inv_std)
    ):
        packed = jnp.where(row == index, value, packed)
    for slot in range(sums.shape[0]):
        sums[slot] = packed

    all_rows = (out_rows * out_cols, channels)
    parts = [None, None, None]
    for frame in range(frames):
        turned = act[frame].reshape(all_rows).T
        for later in range(3):
            value = cot[frame + later] if frame + later < frames else halo[frame + later - frames]
            term = dot(turned, value.reshape(all_rows))
            parts[later] = term if parts[later] is None else parts[later] + term
    for later in range(3):
        temporal[pl.ds(later * channels, channels)] = (parts[later] * loss_scale).astype(
            jnp.bfloat16
        )


def split_rows(values, rows):
    pieces = []
    for value in values:
        rest = value
        for _ in range(3):
            piece = rest.astype(jnp.bfloat16).astype(jnp.float32)
            pieces.append(piece)
            rest = rest - piece
    row = lax.broadcasted_iota(jnp.int32, (rows, values[0].shape[-1]), 0)
    packed = jnp.zeros((rows, values[0].shape[-1]), jnp.float32)
    for index, piece in enumerate(pieces):
        packed = jnp.where(row == index, piece, packed)
    return packed.astype(jnp.bfloat16)


def join_rows(packed, count):
    return [
        packed[3 * i : 3 * i + 1] + packed[3 * i + 1 : 3 * i + 2] + packed[3 * i + 2 : 3 * i + 3]
        for i in range(count)
    ]


def store_rows(chunks, rows, first, values):
    done = 0
    while done < values.shape[0]:
        chunk, at = divmod(first + done, rows)
        count = min(rows - at, values.shape[0] - done)
        chunks[chunk, pl.ds(at, count)] = values[done : done + count]
        done += count


def grad_kernel(
    odd, even, normed, pre, sums, temporal, act, act_halo, weights, grads, encoded
):
    frames, out_rows, out_cols, channels = normed.shape
    lanes = channels // GROUPS
    members = sums.shape[0] * frames * out_rows * out_cols * lanes
    clip = jnp.sum(sums[...], axis=0)
    inv_std = sums[0, 4:5]
    group = group_spread(clip, lanes) * inv_std / members
    group_shift, group_gain = group[2:3], group[3:4]
    flat = (out_rows * out_cols, channels)
    flat_wide = (out_rows * out_cols, 3 * channels)
    rows = grads.shape[1] - EXTRA
    parts = [None, None, None]
    for frame in range(frames):
        back = (
            pre[frame].reshape(flat) - group_shift - normed[frame].reshape(flat) * group_gain
        )
        back = back.astype(jnp.bfloat16).T
        for tap, source in enumerate(
            (odd.at[frame, pl.ds(0, out_rows)], even.at[frame], odd.at[frame, pl.ds(1, out_rows)])
        ):
            term = dot(back, source[...].reshape(flat_wide))
            parts[tap] = term if parts[tap] is None else parts[tap] + term
    for tap in range(3):
        for side in range(3):
            block = parts[tap][:, side * channels : (side + 1) * channels].T
            store_rows(grads, rows, (3 * tap + side) * channels, block.astype(jnp.bfloat16))
    for tap in range(3):
        block = temporal[pl.ds(tap * channels, channels)]
        store_rows(grads, rows, (9 + tap) * channels, block)
    rest = grads.shape[0] * rows - 12 * channels
    if rest:
        store_rows(grads, rows, 12 * channels, jnp.zeros((rest, channels), jnp.bfloat16))
    share = clip * (1.0 / sums.shape[0])
    extra = split_rows([share[1:2], share[0:1]], EXTRA)
    for chunk in range(grads.shape[0]):
        grads[chunk, pl.ds(rows, EXTRA)] = extra
    encode(act, act_halo, weights, encoded)


def total_of(arrived, first, count):
    total = arrived[0, pl.ds(first, count)].astype(jnp.float32)
    for chunk in range(1, arrived.shape[0]):
        total += arrived[chunk, pl.ds(first, count)].astype(jnp.float32)
    return total


def half_kernel(arrived, chunk):
    count = chunk.shape[0] - EXTRA
    chunk[pl.ds(0, count)] = total_of(arrived, 0, count).astype(jnp.bfloat16)
    sums = join_rows(total_of(arrived, count, EXTRA), 2)
    chunk[pl.ds(count, EXTRA)] = split_rows(sums, EXTRA)


def sum_kernel(mine, other, spread, grad_gain, grad_shift):
    count = spread.shape[1]
    wide = [source[...].astype(jnp.float32) for source in (mine, other)]
    total = (wide[0][:count] + wide[1][:count]).astype(jnp.bfloat16)
    for slot in range(spread.shape[0]):
        spread[slot] = total
    sums = [join_rows(source[count:], 2) for source in wide]
    grad_gain[...] = sums[0][0] + sums[1][0]
    grad_shift[...] = sums[0][1] + sums[1][1]


def final_kernel(arrived, grad_spatial, grad_temporal):
    rows = grad_spatial.shape[0]
    grad_spatial[...] = arrived[pl.ds(0, rows)].astype(jnp.float32)
    grad_temporal[...] = arrived[pl.ds(rows, grad_temporal.shape[0])].astype(jnp.float32)


def encode(act, halo, weights, encoded):
    frames, out_rows, out_cols, channels = act.shape
    flat = (STEP_ROWS * out_cols, channels)
    for frame in range(frames):

        def one(step, frame=frame):
            rows = pl.ds(step * STEP_ROWS, STEP_ROWS)
            total = None
            for tap in range(3):
                source = (
                    act[frame - tap, rows] if frame >= tap else halo[frames + frame - tap, rows]
                )
                term = dot(source.reshape(flat), weights[tap])
                total = term if total is None else total + term
            encoded[frame, rows] = total.astype(jnp.bfloat16).reshape(
                STEP_ROWS, out_cols, channels
            )

        each(out_rows // STEP_ROWS, one)


def on_device(video_in, w_spatial, w_temporal, norm_gain, norm_shift, cotangent):
    frames, height, width, channels = video_in.shape[1:]
    out_rows, out_cols = height // 2, width // 2
    dp_size, seq_size = lax.axis_size("dp"), lax.axis_size("seq")
    devices = dp_size * seq_size
    per_clip = FRAMES // frames
    assert frames >= 2 and FRAMES % frames == 0
    loss_scale = float(devices * frames * out_rows * out_cols) ** (-0.5)
    shape = (frames, out_rows, out_cols, channels)
    positions = frames * out_rows * out_cols
    video = video_in[0]
    cot = cotangent[0]
    f32, bf16 = jnp.float32, jnp.bfloat16
    struct = jax.ShapeDtypeStruct

    back_pairs = [(s, s - 1) for s in range(seq_size) if s % per_clip]
    ahead_pairs = [(s - 1, s) for s in range(seq_size) if s % per_clip]
    clips = [list(range(first, first + per_clip)) for first in range(0, seq_size, per_clip)]

    def exchange(value, axes, groups=None):
        return lax.all_to_all(value, axes, 0, 0, axis_index_groups=groups, tiled=True)

    def far(value):
        return pltpu.with_memory_space_constraint(value, pltpu.HBM)

    cot_halo = lax.ppermute(cot, "seq", back_pairs)

    pieces = 2 * frames
    spatial, stats, odd, even, params = call(
        conv_kernel,
        (
            struct(shape, f32),
            struct((per_clip, 8, channels), f32),
            struct((frames, out_rows + 1, out_cols, 3 * channels), bf16),
            struct((frames, out_rows, out_cols, 3 * channels), bf16),
            struct((8, channels), f32),
        ),
        (
            far(video),
            far(w_spatial.reshape(3, 3 * channels, channels)),
            far(norm_gain[None]),
            far(norm_shift[None]),
        ),
        specs=[FAR] * 4,
        scratch=[
            pltpu.VMEM((2 * STEP_ROWS, 8 + width, channels), f32),
            pltpu.VMEM(video.shape, bf16),
            pltpu.VMEM((3, 3 * channels, channels), bf16),
            pltpu.SemaphoreType.DMA((pieces + 3,)),
        ],
        flops=2 * positions * 9 * channels * channels,
    )
    stats = exchange(stats, "seq", clips)
    act, normed, pre, temporal, own = call(
        functools.partial(act_kernel, loss_scale),
        (
            struct(shape, bf16),
            struct(shape, f32),
            struct(shape, f32),
            struct((3 * channels, channels), bf16),
            struct((per_clip, 8, channels), f32),
        ),
        (spatial, stats, cot, cot_halo, w_temporal, params),
        flops=2 * positions * 3 * channels * channels,
    )
    act_halo = lax.ppermute(act, "seq", ahead_pairs)
    sums = exchange(own, "seq", clips)
    halves = 2 if seq_size % 2 == 0 else 1
    half = seq_size // halves
    near = [
        [d * seq_size + s for d in range(dp_size) for s in range(first, first + half)]
        for first in range(0, seq_size, half)
    ]
    count = dp_size * half
    rows = -(-12 * channels // (16 * count)) * 16
    grads, encoded = call(
        grad_kernel,
        (struct((count, rows + EXTRA, channels), bf16), struct(shape, bf16)),
        (odd, even, normed, pre, sums, temporal, act, act_halo, w_temporal),
        flops=2 * positions * 12 * channels * channels,
    )
    grads = exchange(grads, ("dp", "seq"), near)
    mine = call(half_kernel, struct((rows + EXTRA, channels), bf16), (grads,))
    if halves == 2:
        other = lax.ppermute(mine, "seq", [(s, (s + half) % seq_size) for s in range(seq_size)])
    else:
        other = jnp.zeros_like(mine)
    grads, grad_gain, grad_shift = call(
        sum_kernel,
        (
            struct((count, rows, channels), bf16),
            struct((1, channels), f32),
            struct((1, channels), f32),
        ),
        (mine, other),
    )
    grads = exchange(grads, ("dp", "seq"), near)
    grad_spatial, grad_temporal = call(
        final_kernel,
        (struct((9 * channels, channels), f32), struct((3 * channels, channels), f32)),
        (grads.reshape(count * rows, channels),),
    )
    return (
        encoded[None],
        grad_spatial.reshape(3, 3, channels, channels),
        grad_temporal.reshape(3, channels, channels),
        grad_gain[0],
        grad_shift[0],
    )


def solution(mesh):
    placed = P("dp", "seq", None, None, None)
    return jax.shard_map(
        on_device,
        mesh=mesh,
        in_specs=(placed, P(), P(), P(), P(), placed),
        out_specs=(placed, P(), P(), P(), P()),
        check_vma=False,
    )
```

```python
import functools
import math

import jax
import jax.numpy as jnp
from jax import lax
from jax.experimental import pallas as pl
from jax.experimental.pallas import tpu as pltpu
from jax.sharding import PartitionSpec as P

GROUPS = 32
FRAMES = 8
STEP_ROWS = 8
EXTRA = 8
SPARE_BYTES = 4 * 1024 * 1024

WHOLE = pl.BlockSpec(memory_space=pltpu.VMEM)
FAR = pl.BlockSpec(memory_space=pltpu.HBM)


def dot(left, right):
    return jnp.dot(left, right, preferred_element_type=jnp.float32)


def dot_transposed(left, right):
    return lax.dot_general(
        left, right, (((1,), (1,)), ((), ())), preferred_element_type=jnp.float32
    )


def each(count, body):
    if count <= 8:
        for step in range(count):
            body(step)
    else:
        lax.fori_loop(0, count, lambda step, carry: (body(step), carry)[1], 0)


def call(kernel, out_shape, operands, specs=None, scratch=(), flops=0):
    sizes = [value.size * value.dtype.itemsize for value in operands]
    sizes += [value.size * value.dtype.itemsize for value in jax.tree.leaves(out_shape)]
    held = sum(math.prod(item.shape) * 4 for item in scratch if hasattr(item, "shape"))
    return pl.pallas_call(
        kernel,
        out_shape=out_shape,
        in_specs=specs or [WHOLE] * len(operands),
        out_specs=jax.tree.map(lambda _: WHOLE, out_shape),
        scratch_shapes=list(scratch),
        compiler_params=pltpu.CompilerParams(vmem_limit_bytes=sum(sizes) + held + SPARE_BYTES),
        cost_estimate=pl.CostEstimate(
            flops=flops, bytes_accessed=sum(sizes), transcendentals=0
        ),
    )(*operands)


def group_spread(values, lanes):
    channels = values.shape[-1]
    shift = 1
    while shift < lanes:
        values = values + pltpu.roll(values, channels - shift, 1)
        shift *= 2
    lane = lax.broadcasted_iota(jnp.int32, values.shape, 1)
    values = jnp.where(lax.rem(lane, lanes) == 0, values, 0.0)
    shift = 1
    while shift < lanes:
        values = values + pltpu.roll(values, shift, 1)
        shift *= 2
    return values


def conv_kernel(
    video_far, weights_far, gain_far, shift_far, spatial, stats, odd, even, params, wide, video,
    weights, arrived,
):
    frames, height, width, channels = video.shape
    out_rows, out_cols = height // 2, width // 2
    positions = frames * out_rows * out_cols
    pieces = arrived.shape[0] - 3
    half = height * frames // pieces
    copies = []
    for piece in range(pieces):
        rows = pl.ds(piece * half % height, half)
        at = (piece * half // height, rows)
        copies.append(pltpu.make_async_copy(video_far.at[at], video.at[at], arrived.at[piece]))
    small = [
        pltpu.make_async_copy(source, target, arrived.at[pieces + index])
        for index, (source, target) in enumerate(
            ((weights_far, weights), (gain_far, params.at[0:1]), (shift_far, params.at[1:2]))
        )
    ]
    copies[0].start()
    small[0].start()
    for copy in copies[1:]:
        copy.start()
    for copy in small[1:]:
        copy.start()
    for slot in range(2 * STEP_ROWS):
        wide[slot, 0:8] = jnp.zeros((8, channels), jnp.float32)

    for frame in range(frames):
        odd[frame, 0] = jnp.zeros((out_cols, 3 * channels), jnp.bfloat16)

    for piece in range(pieces):
        frame = piece * half // height
        base = piece * half % height // 2 // STEP_ROWS
        copies[piece].wait()

        def separate(step, frame=frame, base=base):
            step = base + step
            for row in range(STEP_ROWS):
                for parity in range(2):
                    slot = 2 * row + parity
                    wide[slot, 8 : 8 + width] = video[
                        frame, 2 * (step * STEP_ROWS + row) + parity
                    ].astype(jnp.float32)
            for row in range(STEP_ROWS):
                for parity in range(2):
                    slot = 2 * row + parity
                    for tap in range(3):
                        value = wide[slot, pl.ds(7 + tap, out_cols, stride=2), :].astype(
                            jnp.bfloat16
                        )
                        lanes = slice(tap * channels, (tap + 1) * channels)
                        if parity:
                            odd[frame, step * STEP_ROWS + row + 1, :, lanes] = value
                        else:
                            even[frame, step * STEP_ROWS + row, :, lanes] = value

        each(half // 2 // STEP_ROWS, separate)
        if piece == 0:
            small[0].wait()

        def multiply(step, frame=frame, base=base):
            step = base + step
            flat = (STEP_ROWS * out_cols, 3 * channels)
            first = step * STEP_ROWS
            total = dot(odd[frame, pl.ds(first, STEP_ROWS)].reshape(flat), weights[0])
            total += dot(even[frame, pl.ds(first, STEP_ROWS)].reshape(flat), weights[1])
            total += dot(odd[frame, pl.ds(first + 1, STEP_ROWS)].reshape(flat), weights[2])
            spatial[frame, pl.ds(first, STEP_ROWS)] = total.reshape(STEP_ROWS, out_cols, channels)

        each(half // 2 // STEP_ROWS, multiply)

    steps = positions // (STEP_ROWS * out_cols)
    per_frame = out_rows // STEP_ROWS

    def block(step):
        return spatial[step // per_frame, pl.ds((step % per_frame) * STEP_ROWS, STEP_ROWS)]

    def fold(values):
        return values.reshape(-1, 8, channels).sum(axis=0)

    def fold_all(term):
        if steps <= 8:
            total = term(0)
            for step in range(1, steps):
                total += term(step)
            return total
        return lax.fori_loop(
            0, steps, lambda step, total: total + term(step), jnp.zeros((8, channels), jnp.float32)
        )

    mean = fold_all(lambda step: fold(block(step))).sum(axis=0, keepdims=True) / positions
    square = fold_all(lambda step: fold((block(step) - mean) ** 2)).sum(axis=0, keepdims=True)
    row = lax.broadcasted_iota(jnp.int32, (8, channels), 0)
    packed = jnp.where(row == 0, mean, jnp.where(row == 1, square, 0.0))
    for slot in range(stats.shape[0]):
        stats[slot] = packed
    for copy in small[1:]:
        copy.wait()


def clip_norm(stats, positions, lanes):
    cells = stats.shape[0] * lanes
    means = [stats[member, 0:1] for member in range(stats.shape[0])]
    squares = [stats[member, 1:2] for member in range(stats.shape[0])]
    mean = group_spread(jnp.broadcast_to(sum(means), (8, means[0].shape[-1])), lanes)[0:1] / cells
    square = sum(squares)
    for value in means:
        square = square + positions * (value - mean) ** 2
    square = group_spread(jnp.broadcast_to(square, (8, square.shape[-1])), lanes)[0:1]
    return mean, lax.rsqrt(square / (cells * positions) + 1e-05)


def act_kernel(
    loss_scale, spatial, stats, cot, halo, weights, params, act, normed, pre, temporal, sums
):
    frames, out_rows, out_cols, channels = spatial.shape
    positions = frames * out_rows * out_cols
    mean, inv_std = clip_norm(stats, positions, channels // GROUPS)
    gain, shift = params[0:1], params[1:2]
    flat = (STEP_ROWS * out_cols, channels)
    shaped = (STEP_ROWS, out_cols, channels)
    sums_shift = jnp.zeros((8, channels), jnp.float32)
    sums_gain = jnp.zeros((8, channels), jnp.float32)

    def fold(values):
        return values.reshape(-1, 8, channels).sum(axis=0)

    for frame in range(frames):

        def cot_block(later, rows):
            if frame + later < frames:
                return cot[frame + later, rows].reshape(flat)
            return halo[frame + later - frames, rows].reshape(flat)

        def one(step, carry):
            rows = pl.ds(step * STEP_ROWS, STEP_ROWS)
            norm = (spatial[frame, rows].reshape(flat) - mean) * inv_std
            before = norm * gain + shift
            sig = jax.nn.sigmoid(before)
            act[frame, rows] = (before * sig).astype(jnp.bfloat16).reshape(shaped)
            back = dot_transposed(cot_block(0, rows), weights[0])
            back += dot_transposed(cot_block(1, rows), weights[1])
            back += dot_transposed(cot_block(2, rows), weights[2])
            back = back.astype(jnp.bfloat16).astype(jnp.float32)
            back_pre = back * loss_scale * sig * (1.0 + before * (1.0 - sig))
            normed[frame, rows] = norm.reshape(shaped)
            pre[frame, rows] = (back_pre * (gain * inv_std)).reshape(shaped)
            return (carry[0] + fold(back_pre), carry[1] + fold(back_pre * norm))

        steps = out_rows // STEP_ROWS
        if steps <= 4:
            for step in range(steps):
                sums_shift, sums_gain = one(step, (sums_shift, sums_gain))
        else:
            sums_shift, sums_gain = lax.fori_loop(0, steps, one, (sums_shift, sums_gain))

    sums_shift = sums_shift.sum(axis=0, keepdims=True)
    sums_gain = sums_gain.sum(axis=0, keepdims=True)
    row = lax.broadcasted_iota(jnp.int32, (8, channels), 0)
    packed = jnp.zeros((8, channels), jnp.float32)
    for index, value in enumerate(
        (sums_shift, sums_gain, gain * sums_shift, gain * sums_gain, inv_std)
    ):
        packed = jnp.where(row == index, value, packed)
    for slot in range(sums.shape[0]):
        sums[slot] = packed

    all_rows = (out_rows * out_cols, channels)
    parts = [None, None, None]
    for frame in range(frames):
        turned = act[frame].reshape(all_rows).T
        for later in range(3):
            value = cot[frame + later] if frame + later < frames else halo[frame + later - frames]
            term = dot(turned, value.reshape(all_rows))
            parts[later] = term if parts[later] is None else parts[later] + term
    for later in range(3):
        temporal[pl.ds(later * channels, channels)] = (parts[later] * loss_scale).astype(
            jnp.bfloat16
        )


def split_rows(values, rows):
    pieces = []
    for value in values:
        rest = value
        for _ in range(3):
            piece = rest.astype(jnp.bfloat16).astype(jnp.float32)
            pieces.append(piece)
            rest = rest - piece
    row = lax.broadcasted_iota(jnp.int32, (rows, values[0].shape[-1]), 0)
    packed = jnp.zeros((rows, values[0].shape[-1]), jnp.float32)
    for index, piece in enumerate(pieces):
        packed = jnp.where(row == index, piece, packed)
    return packed.astype(jnp.bfloat16)


def join_rows(packed, count):
    return [
        packed[3 * i : 3 * i + 1] + packed[3 * i + 1 : 3 * i + 2] + packed[3 * i + 2 : 3 * i + 3]
        for i in range(count)
    ]


def store_rows(chunks, rows, first, values):
    done = 0
    while done < values.shape[0]:
        chunk, at = divmod(first + done, rows)
        count = min(rows - at, values.shape[0] - done)
        chunks[chunk, pl.ds(at, count)] = values[done : done + count]
        done += count


def grad_kernel(odd, even, normed, pre, sums, temporal, grads):
    frames, out_rows, out_cols, channels = normed.shape
    lanes = channels // GROUPS
    members = sums.shape[0] * frames * out_rows * out_cols * lanes
    clip = jnp.sum(sums[...], axis=0)
    inv_std = sums[0, 4:5]
    group = group_spread(clip, lanes) * inv_std / members
    group_shift, group_gain = group[2:3], group[3:4]
    flat = (out_rows * out_cols, channels)
    flat_wide = (out_rows * out_cols, 3 * channels)
    rows = grads.shape[1] - EXTRA
    parts = [None, None, None]
    for frame in range(frames):
        back = (
            pre[frame].reshape(flat) - group_shift - normed[frame].reshape(flat) * group_gain
        )
        back = back.astype(jnp.bfloat16).T
        for tap, source in enumerate(
            (odd.at[frame, pl.ds(0, out_rows)], even.at[frame], odd.at[frame, pl.ds(1, out_rows)])
        ):
            term = dot(back, source[...].reshape(flat_wide))
            parts[tap] = term if parts[tap] is None else parts[tap] + term
    for tap in range(3):
        for side in range(3):
            block = parts[tap][:, side * channels : (side + 1) * channels].T
            store_rows(grads, rows, (3 * tap + side) * channels, block.astype(jnp.bfloat16))
    for tap in range(3):
        block = temporal[pl.ds(tap * channels, channels)]
        store_rows(grads, rows, (9 + tap) * channels, block)
    rest = grads.shape[0] * rows - 12 * channels
    if rest:
        store_rows(grads, rows, 12 * channels, jnp.zeros((rest, channels), jnp.bfloat16))
    share = clip * (1.0 / sums.shape[0])
    extra = split_rows([share[1:2], share[0:1]], EXTRA)
    for chunk in range(grads.shape[0]):
        grads[chunk, pl.ds(rows, EXTRA)] = extra


def total_of(arrived, first, count):
    total = arrived[0, pl.ds(first, count)].astype(jnp.float32)
    for chunk in range(1, arrived.shape[0]):
        total += arrived[chunk, pl.ds(first, count)].astype(jnp.float32)
    return total


def half_kernel(arrived, chunk):
    count = chunk.shape[0] - EXTRA
    chunk[pl.ds(0, count)] = total_of(arrived, 0, count).astype(jnp.bfloat16)
    sums = join_rows(total_of(arrived, count, EXTRA), 2)
    chunk[pl.ds(count, EXTRA)] = split_rows(sums, EXTRA)


def sum_kernel(mine, other, spread, grad_gain, grad_shift):
    count = spread.shape[1]
    wide = [source[...].astype(jnp.float32) for source in (mine, other)]
    total = (wide[0][:count] + wide[1][:count]).astype(jnp.bfloat16)
    for slot in range(spread.shape[0]):
        spread[slot] = total
    sums = [join_rows(source[count:], 2) for source in wide]
    grad_gain[...] = sums[0][0] + sums[1][0]
    grad_shift[...] = sums[0][1] + sums[1][1]


def near_encode_kernel(act, weights, part):
    frames, out_rows, out_cols, channels = act.shape
    flat = (STEP_ROWS * out_cols, channels)
    for frame in range(frames):

        def one(step, frame=frame):
            rows = pl.ds(step * STEP_ROWS, STEP_ROWS)
            total = dot(act[frame, rows].reshape(flat), weights[0])
            for tap in range(1, min(frame, 2) + 1):
                total += dot(act[frame - tap, rows].reshape(flat), weights[tap])
            part[frame, rows] = total.reshape(part[frame, rows].shape)

        each(out_rows // STEP_ROWS, one)


def final_kernel(arrived, part, halo, weights, grad_spatial, grad_temporal, encoded):
    count = grad_spatial.shape[0]
    grad_spatial[...] = arrived[pl.ds(0, count)].astype(jnp.float32)
    grad_temporal[...] = arrived[pl.ds(count, grad_temporal.shape[0])].astype(jnp.float32)
    frames, out_rows, out_cols, channels = halo.shape
    flat = (STEP_ROWS * out_cols, channels)
    for frame in range(frames):

        def one(step, frame=frame):
            rows = pl.ds(step * STEP_ROWS, STEP_ROWS)
            total = part[frame, rows].reshape(flat)
            for tap in range(frame + 1, 3):
                total += dot(halo[frames + frame - tap, rows].reshape(flat), weights[tap])
            encoded[frame, rows] = total.astype(jnp.bfloat16).reshape(
                STEP_ROWS, out_cols, channels
            )

        each(out_rows // STEP_ROWS, one)


def on_device(video_in, w_spatial, w_temporal, norm_gain, norm_shift, cotangent):
    frames, height, width, channels = video_in.shape[1:]
    out_rows, out_cols = height // 2, width // 2
    dp_size, seq_size = lax.axis_size("dp"), lax.axis_size("seq")
    devices = dp_size * seq_size
    per_clip = FRAMES // frames
    assert frames >= 2 and FRAMES % frames == 0
    loss_scale = float(devices * frames * out_rows * out_cols) ** (-0.5)
    shape = (frames, out_rows, out_cols, channels)
    positions = frames * out_rows * out_cols
    video = video_in[0]
    cot = cotangent[0]
    f32, bf16 = jnp.float32, jnp.bfloat16
    struct = jax.ShapeDtypeStruct

    back_pairs = [(s, s - 1) for s in range(seq_size) if s % per_clip]
    ahead_pairs = [(s - 1, s) for s in range(seq_size) if s % per_clip]
    clips = [list(range(first, first + per_clip)) for first in range(0, seq_size, per_clip)]

    def exchange(value, axes, groups=None):
        return lax.all_to_all(value, axes, 0, 0, axis_index_groups=groups, tiled=True)

    def far(value):
        return pltpu.with_memory_space_constraint(value, pltpu.HBM)

    cot_halo = lax.ppermute(cot, "seq", back_pairs)

    pieces = 2 * frames
    spatial, stats, odd, even, params = call(
        conv_kernel,
        (
            struct(shape, f32),
            struct((per_clip, 8, channels), f32),
            struct((frames, out_rows + 1, out_cols, 3 * channels), bf16),
            struct((frames, out_rows, out_cols, 3 * channels), bf16),
            struct((8, channels), f32),
        ),
        (
            far(video),
            far(w_spatial.reshape(3, 3 * channels, channels)),
            far(norm_gain[None]),
            far(norm_shift[None]),
        ),
        specs=[FAR] * 4,
        scratch=[
            pltpu.VMEM((2 * STEP_ROWS, 8 + width, channels), f32),
            pltpu.VMEM(video.shape, bf16),
            pltpu.VMEM((3, 3 * channels, channels), bf16),
            pltpu.SemaphoreType.DMA((pieces + 3,)),
        ],
        flops=2 * positions * 9 * channels * channels,
    )
    stats = exchange(stats, "seq", clips)
    act, normed, pre, temporal, own = call(
        functools.partial(act_kernel, loss_scale),
        (
            struct(shape, bf16),
            struct(shape, f32),
            struct(shape, f32),
            struct((3 * channels, channels), bf16),
            struct((per_clip, 8, channels), f32),
        ),
        (spatial, stats, cot, cot_halo, w_temporal, params),
        flops=2 * positions * 3 * channels * channels,
    )
    sums = exchange(own, "seq", clips)
    halves = 2 if seq_size % 2 == 0 else 1
    half = seq_size // halves
    near = [
        [d * seq_size + s for d in range(dp_size) for s in range(first, first + half)]
        for first in range(0, seq_size, half)
    ]
    count = dp_size * half
    rows = -(-12 * channels // (16 * count)) * 16
    grads = call(
        grad_kernel,
        struct((count, rows + EXTRA, channels), bf16),
        (odd, even, normed, pre, sums, temporal),
        flops=2 * positions * 9 * channels * channels,
    )
    grads = exchange(grads, ("dp", "seq"), near)
    mine = call(half_kernel, struct((rows + EXTRA, channels), bf16), (grads,))
    if halves == 2:
        other = lax.ppermute(mine, "seq", [(s, (s + half) % seq_size) for s in range(seq_size)])
    else:
        other = jnp.zeros_like(mine)
    act, _ = lax.optimization_barrier((act, mine))
    part = call(
        near_encode_kernel,
        struct(shape, f32),
        (act, w_temporal),
        flops=2 * positions * 2 * channels * channels,
    )
    act, part = lax.optimization_barrier((act, part))
    act_halo = lax.ppermute(act, "seq", ahead_pairs)
    other, part = lax.optimization_barrier((other, part))
    grads, grad_gain, grad_shift = call(
        sum_kernel,
        (
            struct((count, rows, channels), bf16),
            struct((1, channels), f32),
            struct((1, channels), f32),
        ),
        (mine, other),
    )
    grads = exchange(grads, ("dp", "seq"), near)
    grad_spatial, grad_temporal, encoded = call(
        final_kernel,
        (
            struct((9 * channels, channels), f32),
            struct((3 * channels, channels), f32),
            struct(shape, bf16),
        ),
        (grads.reshape(count * rows, channels), part, act_halo, w_temporal),
        flops=2 * positions * 2 * channels * channels,
    )
    return (
        encoded[None],
        grad_spatial.reshape(3, 3, channels, channels),
        grad_temporal.reshape(3, channels, channels),
        grad_gain[0],
        grad_shift[0],
    )


def solution(mesh):
    placed = P("dp", "seq", None, None, None)
    return jax.shard_map(
        on_device,
        mesh=mesh,
        in_specs=(placed, P(), P(), P(), P(), placed),
        out_specs=(placed, P(), P(), P(), P()),
        check_vma=False,
    )
```

```python
import functools
import math

import jax
import jax.numpy as jnp
from jax import lax
from jax.experimental import pallas as pl
from jax.experimental.pallas import tpu as pltpu
from jax.sharding import PartitionSpec as P

GROUPS = 32
FRAMES = 8
STEP_ROWS = 8
EXTRA = 8
SPARE_BYTES = 4 * 1024 * 1024

SCALAR = pl.BlockSpec(memory_space=pltpu.SMEM)
WHOLE = pl.BlockSpec(memory_space=pltpu.VMEM)
FAR = pl.BlockSpec(memory_space=pltpu.HBM)


def dot(left, right):
    return jnp.dot(left, right, preferred_element_type=jnp.float32)


def dot_transposed(left, right):
    return lax.dot_general(
        left, right, (((1,), (1,)), ((), ())), preferred_element_type=jnp.float32
    )


def each(count, body):
    if count <= 8:
        for step in range(count):
            body(step)
    else:
        lax.fori_loop(0, count, lambda step, carry: (body(step), carry)[1], 0)


def call(kernel, out_shape, operands, specs=None, scratch=(), flops=0):
    sizes = [value.size * value.dtype.itemsize for value in operands]
    sizes += [value.size * value.dtype.itemsize for value in jax.tree.leaves(out_shape)]
    held = sum(math.prod(item.shape) * 4 for item in scratch if hasattr(item, "shape"))
    return pl.pallas_call(
        kernel,
        out_shape=out_shape,
        in_specs=specs or [WHOLE] * len(operands),
        out_specs=jax.tree.map(lambda _: WHOLE, out_shape),
        scratch_shapes=list(scratch),
        compiler_params=pltpu.CompilerParams(vmem_limit_bytes=sum(sizes) + held + SPARE_BYTES),
        cost_estimate=pl.CostEstimate(
            flops=flops, bytes_accessed=sum(sizes), transcendentals=0
        ),
    )(*operands)


def group_spread(values, lanes):
    channels = values.shape[-1]
    shift = 1
    while shift < lanes:
        values = values + pltpu.roll(values, channels - shift, 1)
        shift *= 2
    lane = lax.broadcasted_iota(jnp.int32, values.shape, 1)
    values = jnp.where(lax.rem(lane, lanes) == 0, values, 0.0)
    shift = 1
    while shift < lanes:
        values = values + pltpu.roll(values, shift, 1)
        shift *= 2
    return values


def conv_kernel(
    video_far, weights_far, gain_far, shift_far, spatial, stats, odd, even, params, wide, video,
    weights, arrived,
):
    frames, height, width, channels = video.shape
    out_rows, out_cols = height // 2, width // 2
    positions = frames * out_rows * out_cols
    pieces = arrived.shape[0] - 3
    half = height * frames // pieces
    copies = []
    for piece in range(pieces):
        rows = pl.ds(piece * half % height, half)
        at = (piece * half // height, rows)
        copies.append(pltpu.make_async_copy(video_far.at[at], video.at[at], arrived.at[piece]))
    small = [
        pltpu.make_async_copy(source, target, arrived.at[pieces + index])
        for index, (source, target) in enumerate(
            ((weights_far, weights), (gain_far, params.at[0:1]), (shift_far, params.at[1:2]))
        )
    ]
    copies[0].start()
    small[0].start()
    for copy in copies[1:]:
        copy.start()
    for copy in small[1:]:
        copy.start()
    for slot in range(2 * STEP_ROWS):
        wide[slot, 0:8] = jnp.zeros((8, channels), jnp.float32)

    for frame in range(frames):
        odd[frame, 0] = jnp.zeros((out_cols, 3 * channels), jnp.bfloat16)

    for piece in range(pieces):
        frame = piece * half // height
        base = piece * half % height // 2 // STEP_ROWS
        copies[piece].wait()

        def separate(step, frame=frame, base=base):
            step = base + step
            for row in range(STEP_ROWS):
                for parity in range(2):
                    slot = 2 * row + parity
                    wide[slot, 8 : 8 + width] = video[
                        frame, 2 * (step * STEP_ROWS + row) + parity
                    ].astype(jnp.float32)
            for row in range(STEP_ROWS):
                for parity in range(2):
                    slot = 2 * row + parity
                    for tap in range(3):
                        value = wide[slot, pl.ds(7 + tap, out_cols, stride=2), :].astype(
                            jnp.bfloat16
                        )
                        lanes = slice(tap * channels, (tap + 1) * channels)
                        if parity:
                            odd[frame, step * STEP_ROWS + row + 1, :, lanes] = value
                        else:
                            even[frame, step * STEP_ROWS + row, :, lanes] = value

        each(half // 2 // STEP_ROWS, separate)
        if piece == 0:
            small[0].wait()

        def multiply(step, frame=frame, base=base):
            step = base + step
            flat = (STEP_ROWS * out_cols, 3 * channels)
            first = step * STEP_ROWS
            total = dot(odd[frame, pl.ds(first, STEP_ROWS)].reshape(flat), weights[0])
            total += dot(even[frame, pl.ds(first, STEP_ROWS)].reshape(flat), weights[1])
            total += dot(odd[frame, pl.ds(first + 1, STEP_ROWS)].reshape(flat), weights[2])
            spatial[frame, pl.ds(first, STEP_ROWS)] = total.reshape(STEP_ROWS, out_cols, channels)

        each(half // 2 // STEP_ROWS, multiply)

    steps = positions // (STEP_ROWS * out_cols)
    per_frame = out_rows // STEP_ROWS

    def block(step):
        return spatial[step // per_frame, pl.ds((step % per_frame) * STEP_ROWS, STEP_ROWS)]

    def fold(values):
        return values.reshape(-1, 8, channels).sum(axis=0)

    def fold_all(term):
        if steps <= 8:
            total = term(0)
            for step in range(1, steps):
                total += term(step)
            return total
        return lax.fori_loop(
            0, steps, lambda step, total: total + term(step), jnp.zeros((8, channels), jnp.float32)
        )

    mean = fold_all(lambda step: fold(block(step))).sum(axis=0, keepdims=True) / positions
    square = fold_all(lambda step: fold((block(step) - mean) ** 2)).sum(axis=0, keepdims=True)
    row = lax.broadcasted_iota(jnp.int32, (8, channels), 0)
    packed = jnp.where(row == 0, mean, jnp.where(row == 1, square, 0.0))
    for slot in range(stats.shape[0]):
        stats[slot] = packed
    for copy in small[1:]:
        copy.wait()


def clip_norm(stats, positions, lanes):
    cells = stats.shape[0] * lanes
    means = [stats[member, 0:1] for member in range(stats.shape[0])]
    squares = [stats[member, 1:2] for member in range(stats.shape[0])]
    mean = group_spread(jnp.broadcast_to(sum(means), (8, means[0].shape[-1])), lanes)[0:1] / cells
    square = sum(squares)
    for value in means:
        square = square + positions * (value - mean) ** 2
    square = group_spread(jnp.broadcast_to(square, (8, square.shape[-1])), lanes)[0:1]
    return mean, lax.rsqrt(square / (cells * positions) + 1e-05)


def act_kernel(
    loss_scale, keep, spatial, stats, cot, arrived, weights, params, act, normed, pre, temporal,
    sums, halo,
):
    frames, out_rows, out_cols, channels = spatial.shape
    positions = frames * out_rows * out_cols
    mean, inv_std = clip_norm(stats, positions, channels // GROUPS)
    gain, shift = params[0:1], params[1:2]
    for frame in range(2):
        value = arrived[frame]
        halo[frame] = jnp.where(keep[0] != 0, value, jnp.zeros_like(value))
    flat = (STEP_ROWS * out_cols, channels)
    shaped = (STEP_ROWS, out_cols, channels)
    sums_shift = jnp.zeros((8, channels), jnp.float32)
    sums_gain = jnp.zeros((8, channels), jnp.float32)

    def fold(values):
        return values.reshape(-1, 8, channels).sum(axis=0)

    for frame in range(frames):

        def cot_block(later, rows):
            if frame + later < frames:
                return cot[frame + later, rows].reshape(flat)
            return halo[frame + later - frames, rows].reshape(flat)

        def one(step, carry):
            rows = pl.ds(step * STEP_ROWS, STEP_ROWS)
            norm = (spatial[frame, rows].reshape(flat) - mean) * inv_std
            before = norm * gain + shift
            sig = jax.nn.sigmoid(before)
            act[frame, rows] = (before * sig).astype(jnp.bfloat16).reshape(shaped)
            back = dot_transposed(cot_block(0, rows), weights[0])
            back += dot_transposed(cot_block(1, rows), weights[1])
            back += dot_transposed(cot_block(2, rows), weights[2])
            back = back.astype(jnp.bfloat16).astype(jnp.float32)
            back_pre = back * loss_scale * sig * (1.0 + before * (1.0 - sig))
            normed[frame, rows] = norm.reshape(shaped)
            pre[frame, rows] = (back_pre * (gain * inv_std)).reshape(shaped)
            return (carry[0] + fold(back_pre), carry[1] + fold(back_pre * norm))

        steps = out_rows // STEP_ROWS
        if steps <= 4:
            for step in range(steps):
                sums_shift, sums_gain = one(step, (sums_shift, sums_gain))
        else:
            sums_shift, sums_gain = lax.fori_loop(0, steps, one, (sums_shift, sums_gain))

    sums_shift = sums_shift.sum(axis=0, keepdims=True)
    sums_gain = sums_gain.sum(axis=0, keepdims=True)
    row = lax.broadcasted_iota(jnp.int32, (8, channels), 0)
    packed = jnp.zeros((8, channels), jnp.float32)
    for index, value in enumerate(
        (sums_shift, sums_gain, gain * sums_shift, gain * sums_gain, inv_std)
    ):
        packed = jnp.where(row == index, value, packed)
    for slot in range(sums.shape[0]):
        sums[slot] = packed

    all_rows = (out_rows * out_cols, channels)
    parts = [None, None, None]
    for frame in range(frames):
        turned = act[frame].reshape(all_rows).T
        for later in range(3):
            value = cot[frame + later] if frame + later < frames else halo[frame + later - frames]
            term = dot(turned, value.reshape(all_rows))
            parts[later] = term if parts[later] is None else parts[later] + term
    for later in range(3):
        temporal[pl.ds(later * channels, channels)] = (parts[later] * loss_scale).astype(
            jnp.bfloat16
        )


def split_rows(values, rows):
    pieces = []
    for value in values:
        rest = value
        for _ in range(3):
            piece = rest.astype(jnp.bfloat16).astype(jnp.float32)
            pieces.append(piece)
            rest = rest - piece
    row = lax.broadcasted_iota(jnp.int32, (rows, values[0].shape[-1]), 0)
    packed = jnp.zeros((rows, values[0].shape[-1]), jnp.float32)
    for index, piece in enumerate(pieces):
        packed = jnp.where(row == index, piece, packed)
    return packed.astype(jnp.bfloat16)


def join_rows(packed, count):
    return [
        packed[3 * i : 3 * i + 1] + packed[3 * i + 1 : 3 * i + 2] + packed[3 * i + 2 : 3 * i + 3]
        for i in range(count)
    ]


def store_rows(chunks, rows, first, values):
    done = 0
    while done < values.shape[0]:
        chunk, at = divmod(first + done, rows)
        count = min(rows - at, values.shape[0] - done)
        chunks[chunk, pl.ds(at, count)] = values[done : done + count]
        done += count


def grad_kernel(
    odd, even, normed, pre, sums, temporal, grads
):
    frames, out_rows, out_cols, channels = normed.shape
    lanes = channels // GROUPS
    members = sums.shape[0] * frames * out_rows * out_cols * lanes
    clip = jnp.sum(sums[...], axis=0)
    inv_std = sums[0, 4:5]
    group = group_spread(clip, lanes) * inv_std / members
    group_shift, group_gain = group[2:3], group[3:4]
    flat = (out_rows * out_cols, channels)
    flat_wide = (out_rows * out_cols, 3 * channels)
    rows = grads.shape[1] - EXTRA
    parts = [None, None, None]
    for frame in range(frames):
        back = (
            pre[frame].reshape(flat) - group_shift - normed[frame].reshape(flat) * group_gain
        )
        back = back.astype(jnp.bfloat16).T
        for tap, source in enumerate(
            (odd.at[frame, pl.ds(0, out_rows)], even.at[frame], odd.at[frame, pl.ds(1, out_rows)])
        ):
            term = dot(back, source[...].reshape(flat_wide))
            parts[tap] = term if parts[tap] is None else parts[tap] + term
    for tap in range(3):
        for side in range(3):
            block = parts[tap][:, side * channels : (side + 1) * channels].T
            store_rows(grads, rows, (3 * tap + side) * channels, block.astype(jnp.bfloat16))
    for tap in range(3):
        block = temporal[pl.ds(tap * channels, channels)]
        store_rows(grads, rows, (9 + tap) * channels, block)
    rest = grads.shape[0] * rows - 12 * channels
    if rest:
        store_rows(grads, rows, 12 * channels, jnp.zeros((rest, channels), jnp.bfloat16))
    share = clip * (1.0 / sums.shape[0])
    extra = split_rows([share[1:2], share[0:1]], EXTRA)
    for chunk in range(grads.shape[0]):
        grads[chunk, pl.ds(rows, EXTRA)] = extra


def total_of(arrived, first, count):
    total = arrived[0, pl.ds(first, count)].astype(jnp.float32)
    for chunk in range(1, arrived.shape[0]):
        total += arrived[chunk, pl.ds(first, count)].astype(jnp.float32)
    return total


def half_kernel(arrived, chunk):
    count = chunk.shape[0] - EXTRA
    chunk[pl.ds(0, count)] = total_of(arrived, 0, count).astype(jnp.bfloat16)
    sums = join_rows(total_of(arrived, count, EXTRA), 2)
    chunk[pl.ds(count, EXTRA)] = split_rows(sums, EXTRA)


def sum_kernel(mine, other, spread, grad_gain, grad_shift):
    count = spread.shape[1]
    wide = [source[...].astype(jnp.float32) for source in (mine, other)]
    total = (wide[0][:count] + wide[1][:count]).astype(jnp.bfloat16)
    for slot in range(spread.shape[0]):
        spread[slot] = total
    sums = [join_rows(source[count:], 2) for source in wide]
    grad_gain[...] = sums[0][0] + sums[1][0]
    grad_shift[...] = sums[0][1] + sums[1][1]


def final_kernel(arrived, grad_spatial, grad_temporal):
    rows = grad_spatial.shape[0]
    grad_spatial[...] = arrived[pl.ds(0, rows)].astype(jnp.float32)
    grad_temporal[...] = arrived[pl.ds(rows, grad_temporal.shape[0])].astype(jnp.float32)


def encode_kernel(keep, act, halo, weights, encoded):
    frames, out_rows, out_cols, channels = act.shape
    flat = (STEP_ROWS * out_cols, channels)
    for frame in range(frames):

        def one(step, frame=frame):
            rows = pl.ds(step * STEP_ROWS, STEP_ROWS)
            total = None
            for tap in range(3):
                if frame >= tap:
                    source = act[frame - tap, rows]
                else:
                    source = halo[frames + frame - tap, rows]
                    source = jnp.where(keep[0] != 0, source, jnp.zeros_like(source))
                term = dot(source.reshape(flat), weights[tap])
                total = term if total is None else total + term
            encoded[frame, rows] = total.astype(jnp.bfloat16).reshape(
                STEP_ROWS, out_cols, channels
            )

        each(out_rows // STEP_ROWS, one)


def on_device(video_in, w_spatial, w_temporal, norm_gain, norm_shift, cotangent):
    frames, height, width, channels = video_in.shape[1:]
    out_rows, out_cols = height // 2, width // 2
    dp_size, seq_size = lax.axis_size("dp"), lax.axis_size("seq")
    devices = dp_size * seq_size
    per_clip = FRAMES // frames
    assert frames >= 2 and FRAMES % frames == 0
    loss_scale = float(devices * frames * out_rows * out_cols) ** (-0.5)
    shape = (frames, out_rows, out_cols, channels)
    positions = frames * out_rows * out_cols
    video = video_in[0]
    cot = cotangent[0]
    f32, bf16 = jnp.float32, jnp.bfloat16
    struct = jax.ShapeDtypeStruct

    ahead_pairs = [
        (s, s // per_clip * per_clip + (s + 1) % per_clip) for s in range(seq_size)
    ]
    back_pairs = [(target, source) for source, target in ahead_pairs]
    member = lax.axis_index("seq") % per_clip
    not_first = (member != 0).astype(jnp.int32)[None]
    not_last = (member != per_clip - 1).astype(jnp.int32)[None]
    clips = [list(range(first, first + per_clip)) for first in range(0, seq_size, per_clip)]

    def exchange(value, axes, groups=None):
        return lax.all_to_all(value, axes, 0, 0, axis_index_groups=groups, tiled=True)

    def far(value):
        return pltpu.with_memory_space_constraint(value, pltpu.HBM)

    cot_halo = lax.ppermute(cot, "seq", back_pairs)

    pieces = 2 * frames
    spatial, stats, odd, even, params = call(
        conv_kernel,
        (
            struct(shape, f32),
            struct((per_clip, 8, channels), f32),
            struct((frames, out_rows + 1, out_cols, 3 * channels), bf16),
            struct((frames, out_rows, out_cols, 3 * channels), bf16),
            struct((8, channels), f32),
        ),
        (
            far(video),
            far(w_spatial.reshape(3, 3 * channels, channels)),
            far(norm_gain[None]),
            far(norm_shift[None]),
        ),
        specs=[FAR] * 4,
        scratch=[
            pltpu.VMEM((2 * STEP_ROWS, 8 + width, channels), f32),
            pltpu.VMEM(video.shape, bf16),
            pltpu.VMEM((3, 3 * channels, channels), bf16),
            pltpu.SemaphoreType.DMA((pieces + 3,)),
        ],
        flops=2 * positions * 9 * channels * channels,
    )
    stats = exchange(stats, "seq", clips)
    act, normed, pre, temporal, own = call(
        functools.partial(act_kernel, loss_scale),
        (
            struct(shape, bf16),
            struct(shape, f32),
            struct(shape, f32),
            struct((3 * channels, channels), bf16),
            struct((per_clip, 8, channels), f32),
        ),
        (not_last, spatial, stats, cot, cot_halo, w_temporal, params),
        specs=[SCALAR] + [WHOLE] * 6,
        scratch=[pltpu.VMEM((2,) + shape[1:], bf16)],
        flops=2 * positions * 3 * channels * channels,
    )
    act_halo = lax.ppermute(act, "seq", ahead_pairs)
    sums = exchange(own, "seq", clips)
    halves = 2 if seq_size % 2 == 0 else 1
    half = seq_size // halves
    near = [
        [d * seq_size + s for d in range(dp_size) for s in range(first, first + half)]
        for first in range(0, seq_size, half)
    ]
    count = dp_size * half
    rows = -(-12 * channels // (16 * count)) * 16
    sums, act_halo = lax.optimization_barrier((sums, act_halo))
    grads = call(
        grad_kernel,
        struct((count, rows + EXTRA, channels), bf16),
        (odd, even, normed, pre, sums, temporal),
        flops=2 * positions * 9 * channels * channels,
    )
    grads = exchange(grads, ("dp", "seq"), near)
    mine = call(half_kernel, struct((rows + EXTRA, channels), bf16), (grads,))
    if halves == 2:
        other = lax.ppermute(mine, "seq", [(s, (s + half) % seq_size) for s in range(seq_size)])
    else:
        other = jnp.zeros_like(mine)
    act, act_halo, _ = lax.optimization_barrier((act, act_halo, mine))
    encoded = call(
        encode_kernel,
        struct(shape, bf16),
        (not_first, act, act_halo, w_temporal),
        specs=[SCALAR] + [WHOLE] * 3,
        flops=2 * positions * 3 * channels * channels,
    )
    other, encoded = lax.optimization_barrier((other, encoded))
    grads, grad_gain, grad_shift = call(
        sum_kernel,
        (
            struct((count, rows, channels), bf16),
            struct((1, channels), f32),
            struct((1, channels), f32),
        ),
        (mine, other),
    )
    grads = exchange(grads, ("dp", "seq"), near)
    grad_spatial, grad_temporal = call(
        final_kernel,
        (struct((9 * channels, channels), f32), struct((3 * channels, channels), f32)),
        (grads.reshape(count * rows, channels),),
    )
    return (
        encoded[None],
        grad_spatial.reshape(3, 3, channels, channels),
        grad_temporal.reshape(3, channels, channels),
        grad_gain[0],
        grad_shift[0],
    )


def solution(mesh):
    placed = P("dp", "seq", None, None, None)
    return jax.shard_map(
        on_device,
        mesh=mesh,
        in_specs=(placed, P(), P(), P(), P(), placed),
        out_specs=(placed, P(), P(), P(), P()),
        check_vma=False,
    )
```

```python
import functools
import math

import jax
import jax.numpy as jnp
from jax import lax
from jax.experimental import pallas as pl
from jax.experimental.pallas import tpu as pltpu
from jax.sharding import PartitionSpec as P

GROUPS = 32
FRAMES = 8
STEP_ROWS = 8
EXTRA = 8
SPARE_BYTES = 4 * 1024 * 1024

WHOLE = pl.BlockSpec(memory_space=pltpu.VMEM)
FAR = pl.BlockSpec(memory_space=pltpu.HBM)


def dot(left, right):
    return jnp.dot(left, right, preferred_element_type=jnp.float32)


def dot_transposed(left, right):
    return lax.dot_general(
        left, right, (((1,), (1,)), ((), ())), preferred_element_type=jnp.float32
    )


def each(count, body):
    if count <= 8:
        for step in range(count):
            body(step)
    else:
        lax.fori_loop(0, count, lambda step, carry: (body(step), carry)[1], 0)


def call(kernel, out_shape, operands, specs=None, scratch=(), flops=0):
    sizes = [value.size * value.dtype.itemsize for value in operands]
    sizes += [value.size * value.dtype.itemsize for value in jax.tree.leaves(out_shape)]
    held = sum(math.prod(item.shape) * 4 for item in scratch if hasattr(item, "shape"))
    return pl.pallas_call(
        kernel,
        out_shape=out_shape,
        in_specs=specs or [WHOLE] * len(operands),
        out_specs=jax.tree.map(lambda _: WHOLE, out_shape),
        scratch_shapes=list(scratch),
        compiler_params=pltpu.CompilerParams(vmem_limit_bytes=sum(sizes) + held + SPARE_BYTES),
        cost_estimate=pl.CostEstimate(
            flops=flops, bytes_accessed=sum(sizes), transcendentals=0
        ),
    )(*operands)


def group_spread(values, lanes):
    channels = values.shape[-1]
    shift = 1
    while shift < lanes:
        values = values + pltpu.roll(values, channels - shift, 1)
        shift *= 2
    lane = lax.broadcasted_iota(jnp.int32, values.shape, 1)
    values = jnp.where(lax.rem(lane, lanes) == 0, values, 0.0)
    shift = 1
    while shift < lanes:
        values = values + pltpu.roll(values, shift, 1)
        shift *= 2
    return values


def conv_kernel(
    video_far, weights_far, gain_far, shift_far, spatial, stats, odd, even, params, wide, video,
    weights, arrived,
):
    frames, height, width, channels = video.shape
    out_rows, out_cols = height // 2, width // 2
    positions = frames * out_rows * out_cols
    pieces = arrived.shape[0] - 3
    half = height * frames // pieces
    copies = []
    for piece in range(pieces):
        rows = pl.ds(piece * half % height, half)
        at = (piece * half // height, rows)
        copies.append(pltpu.make_async_copy(video_far.at[at], video.at[at], arrived.at[piece]))
    small = [
        pltpu.make_async_copy(source, target, arrived.at[pieces + index])
        for index, (source, target) in enumerate(
            ((weights_far, weights), (gain_far, params.at[0:1]), (shift_far, params.at[1:2]))
        )
    ]
    copies[0].start()
    small[0].start()
    for copy in copies[1:]:
        copy.start()
    for copy in small[1:]:
        copy.start()
    for slot in range(wide.shape[0]):
        wide[slot, 0:8] = jnp.zeros((8, channels), jnp.float32)
    for frame in range(frames):
        odd[frame, 0] = jnp.zeros((out_cols, 3 * channels), jnp.bfloat16)
    flat = (STEP_ROWS * out_cols, 3 * channels)
    steps = half // 2 // STEP_ROWS

    def place(piece, step):
        return piece * half // height, piece * half % height // 2 + step * STEP_ROWS

    def separate(piece, step):
        frame, first = place(piece, step)
        base = piece % 2 * 2 * STEP_ROWS
        for line in range(2 * STEP_ROWS):
            wide[base + line, 8 : 8 + width] = video[frame, 2 * first + line].astype(jnp.float32)
        for line in range(2 * STEP_ROWS):
            for tap in range(3):
                value = wide[base + line, pl.ds(7 + tap, out_cols, stride=2), :]
                lanes = slice(tap * channels, (tap + 1) * channels)
                if line % 2:
                    odd[frame, first + line // 2 + 1, :, lanes] = value.astype(jnp.bfloat16)
                else:
                    even[frame, first + line // 2, :, lanes] = value.astype(jnp.bfloat16)

    def multiply(piece, step):
        frame, first = place(piece, step)
        total = dot(odd[frame, pl.ds(first, STEP_ROWS)].reshape(flat), weights[0])
        total += dot(even[frame, pl.ds(first, STEP_ROWS)].reshape(flat), weights[1])
        total += dot(odd[frame, pl.ds(first + 1, STEP_ROWS)].reshape(flat), weights[2])
        spatial[frame, pl.ds(first, STEP_ROWS)] = total.reshape(STEP_ROWS, out_cols, channels)
        return total

    def fold(values):
        return values.reshape(-1, 8, channels).sum(axis=0)

    def over_steps(piece, term, start):
        if steps <= 8:
            for step in range(steps):
                start = jax.tree.map(jnp.add, start, term(piece, step))
            return start
        return lax.fori_loop(
            0, steps, lambda step, sums: jax.tree.map(jnp.add, sums, term(piece, step)), start
        )

    zero = jnp.zeros((8, channels), jnp.float32)

    def first_sum(piece, step):
        return fold(multiply(piece, step))

    def first_moments(piece, step):
        frame, first = place(piece, step)
        off = spatial[frame, pl.ds(first, STEP_ROWS)].reshape(-1, channels) - near
        return fold(off), fold(off * off)

    def moments(piece, step):
        off = multiply(piece, step) - near
        return fold(off), fold(off * off)

    for piece in range(pieces):
        copies[piece].wait()
        each(steps, functools.partial(separate, piece))
        if piece == 0:
            small[0].wait()
        elif piece == 1:
            near = over_steps(0, first_sum, zero).sum(axis=0, keepdims=True) * (
                pieces / positions
            )
        else:
            if piece == 2:
                sums = over_steps(0, first_moments, (zero, zero))
            sums = over_steps(piece - 1, moments, sums)
    sums = over_steps(pieces - 1, moments, sums)
    off = sums[0].sum(axis=0, keepdims=True) / positions
    mean = near + off
    square = sums[1].sum(axis=0, keepdims=True) - positions * off * off
    row = lax.broadcasted_iota(jnp.int32, (8, channels), 0)
    packed = jnp.where(row == 0, mean, jnp.where(row == 1, square, 0.0))
    for slot in range(stats.shape[0]):
        stats[slot] = packed
    for copy in small[1:]:
        copy.wait()


def clip_norm(stats, positions, lanes):
    cells = stats.shape[0] * lanes
    means = [stats[member, 0:1] for member in range(stats.shape[0])]
    squares = [stats[member, 1:2] for member in range(stats.shape[0])]
    mean = group_spread(jnp.broadcast_to(sum(means), (8, means[0].shape[-1])), lanes)[0:1] / cells
    square = sum(squares)
    for value in means:
        square = square + positions * (value - mean) ** 2
    square = group_spread(jnp.broadcast_to(square, (8, square.shape[-1])), lanes)[0:1]
    return mean, lax.rsqrt(square / (cells * positions) + 1e-05)


def act_kernel(
    loss_scale, spatial, stats, cot, arrived, weights, params, act, normed, pre, temporal, sums,
    halo,
):
    frames, out_rows, out_cols, channels = spatial.shape
    positions = frames * out_rows * out_cols
    mean, inv_std = clip_norm(stats, positions, channels // GROUPS)
    gain, shift = params[0:1], params[1:2]
    per_clip = sums.shape[0]
    not_last = lax.rem(lax.axis_index("seq"), per_clip) != per_clip - 1
    for frame in range(2):
        value = arrived[frame]
        halo[frame] = jnp.where(not_last, value, jnp.zeros_like(value))
    turned_weights = jnp.concatenate([weights[tap] for tap in range(3)], axis=1)
    flat = (STEP_ROWS * out_cols, channels)
    shaped = (STEP_ROWS, out_cols, channels)
    sums_shift = jnp.zeros((8, channels), jnp.float32)
    sums_gain = jnp.zeros((8, channels), jnp.float32)

    def fold(values):
        return values.reshape(-1, 8, channels).sum(axis=0)

    for frame in range(frames):

        def cot_block(later, rows):
            if frame + later < frames:
                return cot[frame + later, rows].reshape(flat)
            return halo[frame + later - frames, rows].reshape(flat)

        def one(step, carry):
            rows = pl.ds(step * STEP_ROWS, STEP_ROWS)
            norm = (spatial[frame, rows].reshape(flat) - mean) * inv_std
            before = norm * gain + shift
            sig = jax.nn.sigmoid(before)
            act[frame, rows] = (before * sig).astype(jnp.bfloat16).reshape(shaped)
            cots = jnp.concatenate([cot_block(later, rows) for later in range(3)], axis=1)
            back = dot_transposed(cots, turned_weights)
            back = back.astype(jnp.bfloat16).astype(jnp.float32)
            back_pre = back * loss_scale * sig * (1.0 + before * (1.0 - sig))
            normed[frame, rows] = norm.reshape(shaped)
            pre[frame, rows] = (back_pre * (gain * inv_std)).reshape(shaped)
            return (carry[0] + fold(back_pre), carry[1] + fold(back_pre * norm))

        steps = out_rows // STEP_ROWS
        if steps <= 4:
            for step in range(steps):
                sums_shift, sums_gain = one(step, (sums_shift, sums_gain))
        else:
            sums_shift, sums_gain = lax.fori_loop(0, steps, one, (sums_shift, sums_gain))

    sums_shift = sums_shift.sum(axis=0, keepdims=True)
    sums_gain = sums_gain.sum(axis=0, keepdims=True)
    row = lax.broadcasted_iota(jnp.int32, (8, channels), 0)
    packed = jnp.zeros((8, channels), jnp.float32)
    for index, value in enumerate(
        (sums_shift, sums_gain, gain * sums_shift, gain * sums_gain, inv_std)
    ):
        packed = jnp.where(row == index, value, packed)
    for slot in range(sums.shape[0]):
        sums[slot] = packed

    all_rows = (out_rows * out_cols, channels)
    total = None
    for frame in range(frames):
        cots = jnp.concatenate(
            [
                (cot[frame + later] if frame + later < frames else halo[frame + later - frames])
                .reshape(all_rows)
                for later in range(3)
            ],
            axis=1,
        )
        term = dot(act[frame].reshape(all_rows).T, cots)
        total = term if total is None else total + term
    for later in range(3):
        block = total[:, later * channels : (later + 1) * channels] * loss_scale
        temporal[pl.ds(later * channels, channels)] = block.astype(jnp.bfloat16)


def split_rows(values, rows):
    pieces = []
    for value in values:
        rest = value
        for _ in range(3):
            piece = rest.astype(jnp.bfloat16).astype(jnp.float32)
            pieces.append(piece)
            rest = rest - piece
    row = lax.broadcasted_iota(jnp.int32, (rows, values[0].shape[-1]), 0)
    packed = jnp.zeros((rows, values[0].shape[-1]), jnp.float32)
    for index, piece in enumerate(pieces):
        packed = jnp.where(row == index, piece, packed)
    return packed.astype(jnp.bfloat16)


def join_rows(packed, count):
    return [
        packed[3 * i : 3 * i + 1] + packed[3 * i + 1 : 3 * i + 2] + packed[3 * i + 2 : 3 * i + 3]
        for i in range(count)
    ]


def store_rows(chunks, rows, first, values):
    done = 0
    while done < values.shape[0]:
        chunk, at = divmod(first + done, rows)
        count = min(rows - at, values.shape[0] - done)
        chunks[chunk, pl.ds(at, count)] = values[done : done + count]
        done += count


def grad_kernel(
    odd, even, normed, pre, sums, temporal, grads
):
    frames, out_rows, out_cols, channels = normed.shape
    lanes = channels // GROUPS
    members = sums.shape[0] * frames * out_rows * out_cols * lanes
    clip = jnp.sum(sums[...], axis=0)
    inv_std = sums[0, 4:5]
    group = group_spread(clip, lanes) * inv_std / members
    group_shift, group_gain = group[2:3], group[3:4]
    flat = (out_rows * out_cols, channels)
    flat_wide = (out_rows * out_cols, 3 * channels)
    rows = grads.shape[1] - EXTRA
    parts = [None, None, None]
    for frame in range(frames):
        back = (
            pre[frame].reshape(flat) - group_shift - normed[frame].reshape(flat) * group_gain
        )
        back = back.astype(jnp.bfloat16).T
        for tap, source in enumerate(
            (odd.at[frame, pl.ds(0, out_rows)], even.at[frame], odd.at[frame, pl.ds(1, out_rows)])
        ):
            term = dot(back, source[...].reshape(flat_wide))
            parts[tap] = term if parts[tap] is None else parts[tap] + term
    for tap in range(3):
        for side in range(3):
            block = parts[tap][:, side * channels : (side + 1) * channels].T
            store_rows(grads, rows, (3 * tap + side) * channels, block.astype(jnp.bfloat16))
    for tap in range(3):
        block = temporal[pl.ds(tap * channels, channels)]
        store_rows(grads, rows, (9 + tap) * channels, block)
    rest = grads.shape[0] * rows - 12 * channels
    if rest:
        store_rows(grads, rows, 12 * channels, jnp.zeros((rest, channels), jnp.bfloat16))
    share = clip * (1.0 / sums.shape[0])
    extra = split_rows([share[1:2], share[0:1]], EXTRA)
    for chunk in range(grads.shape[0]):
        grads[chunk, pl.ds(rows, EXTRA)] = extra


def total_of(arrived, first, count):
    total = arrived[0, pl.ds(first, count)].astype(jnp.float32)
    for chunk in range(1, arrived.shape[0]):
        total += arrived[chunk, pl.ds(first, count)].astype(jnp.float32)
    return total


def half_kernel(arrived, chunk):
    count = chunk.shape[0] - EXTRA
    chunk[pl.ds(0, count)] = total_of(arrived, 0, count).astype(jnp.bfloat16)
    sums = join_rows(total_of(arrived, count, EXTRA), 2)
    chunk[pl.ds(count, EXTRA)] = split_rows(sums, EXTRA)


def sum_kernel(mine, other, spread, grad_gain, grad_shift):
    count = spread.shape[1]
    wide = [source[...].astype(jnp.float32) for source in (mine, other)]
    total = (wide[0][:count] + wide[1][:count]).astype(jnp.bfloat16)
    for slot in range(spread.shape[0]):
        spread[slot] = total
    sums = [join_rows(source[count:], 2) for source in wide]
    grad_gain[...] = sums[0][0] + sums[1][0]
    grad_shift[...] = sums[0][1] + sums[1][1]


def final_kernel(arrived, grad_spatial, grad_temporal):
    rows = grad_spatial.shape[0]
    grad_spatial[...] = arrived[pl.ds(0, rows)].astype(jnp.float32)
    grad_temporal[...] = arrived[pl.ds(rows, grad_temporal.shape[0])].astype(jnp.float32)


def encode_kernel(per_clip, act, halo, weights, encoded):
    frames, out_rows, out_cols, channels = act.shape
    not_first = lax.rem(lax.axis_index("seq"), per_clip) != 0
    flat = (STEP_ROWS * out_cols, channels)
    for frame in range(frames):

        def one(step, frame=frame):
            rows = pl.ds(step * STEP_ROWS, STEP_ROWS)
            total = None
            for tap in range(3):
                if frame >= tap:
                    source = act[frame - tap, rows]
                else:
                    source = halo[frames + frame - tap, rows]
                    source = jnp.where(not_first, source, jnp.zeros_like(source))
                term = dot(source.reshape(flat), weights[tap])
                total = term if total is None else total + term
            encoded[frame, rows] = total.astype(jnp.bfloat16).reshape(
                STEP_ROWS, out_cols, channels
            )

        each(out_rows // STEP_ROWS, one)


def on_device(video_in, w_spatial, w_temporal, norm_gain, norm_shift, cotangent):
    frames, height, width, channels = video_in.shape[1:]
    out_rows, out_cols = height // 2, width // 2
    dp_size, seq_size = lax.axis_size("dp"), lax.axis_size("seq")
    devices = dp_size * seq_size
    per_clip = FRAMES // frames
    assert frames >= 2 and FRAMES % frames == 0
    loss_scale = float(devices * frames * out_rows * out_cols) ** (-0.5)
    shape = (frames, out_rows, out_cols, channels)
    positions = frames * out_rows * out_cols
    video = video_in[0]
    cot = cotangent[0]
    f32, bf16 = jnp.float32, jnp.bfloat16
    struct = jax.ShapeDtypeStruct

    ahead_pairs = [
        (s, s // per_clip * per_clip + (s + 1) % per_clip) for s in range(seq_size)
    ]
    back_pairs = [(target, source) for source, target in ahead_pairs]
    clips = [list(range(first, first + per_clip)) for first in range(0, seq_size, per_clip)]

    def exchange(value, axes, groups=None):
        return lax.all_to_all(value, axes, 0, 0, axis_index_groups=groups, tiled=True)

    def far(value):
        return pltpu.with_memory_space_constraint(value, pltpu.HBM)

    cot_halo = lax.ppermute(cot, "seq", back_pairs)

    pieces = 2 * frames
    spatial, stats, odd, even, params = call(
        conv_kernel,
        (
            struct(shape, f32),
            struct((per_clip, 8, channels), f32),
            struct((frames, out_rows + 1, out_cols, 3 * channels), bf16),
            struct((frames, out_rows, out_cols, 3 * channels), bf16),
            struct((8, channels), f32),
        ),
        (
            far(video),
            far(w_spatial.reshape(3, 3 * channels, channels)),
            far(norm_gain[None]),
            far(norm_shift[None]),
        ),
        specs=[FAR] * 4,
        scratch=[
            pltpu.VMEM((4 * STEP_ROWS, 8 + width, channels), f32),
            pltpu.VMEM(video.shape, bf16),
            pltpu.VMEM((3, 3 * channels, channels), bf16),
            pltpu.SemaphoreType.DMA((pieces + 3,)),
        ],
        flops=2 * positions * 9 * channels * channels,
    )
    stats = exchange(stats, "seq", clips)
    act, normed, pre, temporal, own = call(
        functools.partial(act_kernel, loss_scale),
        (
            struct(shape, bf16),
            struct(shape, f32),
            struct(shape, f32),
            struct((3 * channels, channels), bf16),
            struct((per_clip, 8, channels), f32),
        ),
        (spatial, stats, cot, cot_halo, w_temporal, params),
        scratch=[pltpu.VMEM((2,) + shape[1:], bf16)],
        flops=2 * positions * 3 * channels * channels,
    )
    act_halo = lax.ppermute(act, "seq", ahead_pairs)
    sums = exchange(own, "seq", clips)
    halves = 2 if seq_size % 2 == 0 else 1
    half = seq_size // halves
    near = [
        [d * seq_size + s for d in range(dp_size) for s in range(first, first + half)]
        for first in range(0, seq_size, half)
    ]
    count = dp_size * half
    rows = -(-12 * channels // (16 * count)) * 16
    sums, act_halo = lax.optimization_barrier((sums, act_halo))
    grads = call(
        grad_kernel,
        struct((count, rows + EXTRA, channels), bf16),
        (odd, even, normed, pre, sums, temporal),
        flops=2 * positions * 9 * channels * channels,
    )
    grads = exchange(grads, ("dp", "seq"), near)
    mine = call(half_kernel, struct((rows + EXTRA, channels), bf16), (grads,))
    if halves == 2:
        other = lax.ppermute(mine, "seq", [(s, (s + half) % seq_size) for s in range(seq_size)])
    else:
        other = jnp.zeros_like(mine)
    act, act_halo, _ = lax.optimization_barrier((act, act_halo, mine))
    encoded = call(
        functools.partial(encode_kernel, per_clip),
        struct(shape, bf16),
        (act, act_halo, w_temporal),
        flops=2 * positions * 3 * channels * channels,
    )
    other, encoded = lax.optimization_barrier((other, encoded))
    grads, grad_gain, grad_shift = call(
        sum_kernel,
        (
            struct((count, rows, channels), bf16),
            struct((1, channels), f32),
            struct((1, channels), f32),
        ),
        (mine, other),
    )
    grads = exchange(grads, ("dp", "seq"), near)
    grad_spatial, grad_temporal = call(
        final_kernel,
        (struct((9 * channels, channels), f32), struct((3 * channels, channels), f32)),
        (grads.reshape(count * rows, channels),),
    )
    return (
        encoded[None],
        grad_spatial.reshape(3, 3, channels, channels),
        grad_temporal.reshape(3, channels, channels),
        grad_gain[0],
        grad_shift[0],
    )


def solution(mesh):
    placed = P("dp", "seq", None, None, None)
    return jax.shard_map(
        on_device,
        mesh=mesh,
        in_specs=(placed, P(), P(), P(), P(), placed),
        out_specs=(placed, P(), P(), P(), P()),
        check_vma=False,
    )
```

```python
import functools
import math

import jax
import jax.numpy as jnp
from jax import lax
from jax.experimental import pallas as pl
from jax.experimental.pallas import tpu as pltpu
from jax.sharding import PartitionSpec as P

GROUPS = 32
FRAMES = 8
STEP_ROWS = 8
EXTRA = 8
SPARE_BYTES = 4 * 1024 * 1024

WHOLE = pl.BlockSpec(memory_space=pltpu.VMEM)
FAR = pl.BlockSpec(memory_space=pltpu.HBM)


def dot(left, right):
    return jnp.dot(left, right, preferred_element_type=jnp.float32)


def dot_transposed(left, right):
    return lax.dot_general(
        left, right, (((1,), (1,)), ((), ())), preferred_element_type=jnp.float32
    )


def each(count, body):
    if count <= 8:
        for step in range(count):
            body(step)
    else:
        lax.fori_loop(0, count, lambda step, carry: (body(step), carry)[1], 0)


def call(kernel, out_shape, operands, specs=None, scratch=(), flops=0):
    sizes = [value.size * value.dtype.itemsize for value in operands]
    sizes += [value.size * value.dtype.itemsize for value in jax.tree.leaves(out_shape)]
    held = sum(math.prod(item.shape) * 4 for item in scratch if hasattr(item, "shape"))
    return pl.pallas_call(
        kernel,
        out_shape=out_shape,
        in_specs=specs or [WHOLE] * len(operands),
        out_specs=jax.tree.map(lambda _: WHOLE, out_shape),
        scratch_shapes=list(scratch),
        compiler_params=pltpu.CompilerParams(vmem_limit_bytes=sum(sizes) + held + SPARE_BYTES),
        cost_estimate=pl.CostEstimate(
            flops=flops, bytes_accessed=sum(sizes), transcendentals=0
        ),
    )(*operands)


def group_spread(values, lanes):
    channels = values.shape[-1]
    shift = 1
    while shift < lanes:
        values = values + pltpu.roll(values, channels - shift, 1)
        shift *= 2
    lane = lax.broadcasted_iota(jnp.int32, values.shape, 1)
    values = jnp.where(lax.rem(lane, lanes) == 0, values, 0.0)
    shift = 1
    while shift < lanes:
        values = values + pltpu.roll(values, shift, 1)
        shift *= 2
    return values


def open_kernel(gate):
    gate[...] = jnp.zeros(gate.shape, gate.dtype)


def conv_kernel(
    pieces, blank, video, weights_far, gain_far, shift_far, spatial, stats, odd, even, params, wide,
    weights, arrived,
):
    frames, height, width, channels = video.shape
    out_rows, out_cols = height // 2, width // 2
    positions = frames * out_rows * out_cols
    half = height * frames // pieces
    params[...] = blank[...]
    copies = [
        pltpu.make_async_copy(source, target, arrived.at[index])
        for index, (source, target) in enumerate(
            ((weights_far, weights), (gain_far, params.at[0:1]), (shift_far, params.at[1:2]))
        )
    ]
    for copy in copies:
        copy.start()
    for slot in range(wide.shape[0]):
        wide[slot, 0:8] = jnp.zeros((8, channels), jnp.float32)
    for frame in range(frames):
        odd[frame, 0] = jnp.zeros((out_cols, 3 * channels), jnp.bfloat16)
    flat = (STEP_ROWS * out_cols, 3 * channels)
    steps = half // 2 // STEP_ROWS

    def place(piece, step):
        return piece * half // height, piece * half % height // 2 + step * STEP_ROWS

    def separate(piece, step):
        frame, first = place(piece, step)
        base = piece % 2 * 2 * STEP_ROWS
        for line in range(2 * STEP_ROWS):
            wide[base + line, 8 : 8 + width] = video[frame, 2 * first + line].astype(jnp.float32)
        for line in range(2 * STEP_ROWS):
            for tap in range(3):
                value = wide[base + line, pl.ds(7 + tap, out_cols, stride=2), :]
                lanes = slice(tap * channels, (tap + 1) * channels)
                if line % 2:
                    odd[frame, first + line // 2 + 1, :, lanes] = value.astype(jnp.bfloat16)
                else:
                    even[frame, first + line // 2, :, lanes] = value.astype(jnp.bfloat16)

    def multiply(piece, step):
        frame, first = place(piece, step)
        total = dot(odd[frame, pl.ds(first, STEP_ROWS)].reshape(flat), weights[0])
        total += dot(even[frame, pl.ds(first, STEP_ROWS)].reshape(flat), weights[1])
        total += dot(odd[frame, pl.ds(first + 1, STEP_ROWS)].reshape(flat), weights[2])
        spatial[frame, pl.ds(first, STEP_ROWS)] = total.reshape(STEP_ROWS, out_cols, channels)
        return total

    def fold(values):
        return values.reshape(-1, 8, channels).sum(axis=0)

    def over_steps(piece, term, start):
        if steps <= 8:
            for step in range(steps):
                start = jax.tree.map(jnp.add, start, term(piece, step))
            return start
        return lax.fori_loop(
            0, steps, lambda step, sums: jax.tree.map(jnp.add, sums, term(piece, step)), start
        )

    zero = jnp.zeros((8, channels), jnp.float32)

    def first_sum(piece, step):
        return fold(multiply(piece, step))

    def first_moments(piece, step):
        frame, first = place(piece, step)
        off = spatial[frame, pl.ds(first, STEP_ROWS)].reshape(-1, channels) - near
        return fold(off), fold(off * off)

    def moments(piece, step):
        off = multiply(piece, step) - near
        return fold(off), fold(off * off)

    for piece in range(pieces):
        each(steps, functools.partial(separate, piece))
    copies[0].wait()
    near = over_steps(0, first_sum, zero).sum(axis=0, keepdims=True) * (pieces / positions)
    sums = over_steps(0, first_moments, (zero, zero))
    for piece in range(1, pieces - 1):
        sums = over_steps(piece, moments, sums)
    sums = over_steps(pieces - 1, moments, sums)
    off = sums[0].sum(axis=0, keepdims=True) / positions
    mean = near + off
    square = sums[1].sum(axis=0, keepdims=True) - positions * off * off
    row = lax.broadcasted_iota(jnp.int32, (8, channels), 0)
    packed = jnp.where(row == 0, mean, jnp.where(row == 1, square, 0.0))
    for slot in range(stats.shape[0]):
        stats[slot] = packed
    for copy in copies[1:]:
        copy.wait()

def clip_norm(stats, positions, lanes):
    cells = stats.shape[0] * lanes
    means = [stats[member, 0:1] for member in range(stats.shape[0])]
    squares = [stats[member, 1:2] for member in range(stats.shape[0])]
    mean = group_spread(jnp.broadcast_to(sum(means), (8, means[0].shape[-1])), lanes)[0:1] / cells
    square = sum(squares)
    for value in means:
        square = square + positions * (value - mean) ** 2
    square = group_spread(jnp.broadcast_to(square, (8, square.shape[-1])), lanes)[0:1]
    return mean, lax.rsqrt(square / (cells * positions) + 1e-05)


def act_kernel(
    loss_scale, spatial, stats, cot, arrived, weights, params, act, normed, pre, temporal, sums,
    halo,
):
    frames, out_rows, out_cols, channels = spatial.shape
    positions = frames * out_rows * out_cols
    mean, inv_std = clip_norm(stats, positions, channels // GROUPS)
    gain, shift = params[0:1], params[1:2]
    per_clip = sums.shape[0]
    not_last = lax.rem(lax.axis_index("seq"), per_clip) != per_clip - 1
    for frame in range(2):
        value = arrived[frame]
        halo[frame] = jnp.where(not_last, value, jnp.zeros_like(value))
    turned_weights = jnp.concatenate([weights[tap] for tap in range(3)], axis=1)
    flat = (STEP_ROWS * out_cols, channels)
    shaped = (STEP_ROWS, out_cols, channels)
    sums_shift = jnp.zeros((8, channels), jnp.float32)
    sums_gain = jnp.zeros((8, channels), jnp.float32)

    def fold(values):
        return values.reshape(-1, 8, channels).sum(axis=0)

    for frame in range(frames):

        def cot_block(later, rows):
            if frame + later < frames:
                return cot[frame + later, rows].reshape(flat)
            return halo[frame + later - frames, rows].reshape(flat)

        def one(step, carry):
            rows = pl.ds(step * STEP_ROWS, STEP_ROWS)
            norm = (spatial[frame, rows].reshape(flat) - mean) * inv_std
            before = norm * gain + shift
            sig = jax.nn.sigmoid(before)
            act[frame, rows] = (before * sig).astype(jnp.bfloat16).reshape(shaped)
            cots = jnp.concatenate([cot_block(later, rows) for later in range(3)], axis=1)
            back = dot_transposed(cots, turned_weights)
            back = back.astype(jnp.bfloat16).astype(jnp.float32)
            back_pre = back * loss_scale * sig * (1.0 + before * (1.0 - sig))
            normed[frame, rows] = norm.reshape(shaped)
            pre[frame, rows] = (back_pre * (gain * inv_std)).reshape(shaped)
            return (carry[0] + fold(back_pre), carry[1] + fold(back_pre * norm))

        steps = out_rows // STEP_ROWS
        if steps <= 4:
            for step in range(steps):
                sums_shift, sums_gain = one(step, (sums_shift, sums_gain))
        else:
            sums_shift, sums_gain = lax.fori_loop(0, steps, one, (sums_shift, sums_gain))

    sums_shift = sums_shift.sum(axis=0, keepdims=True)
    sums_gain = sums_gain.sum(axis=0, keepdims=True)
    row = lax.broadcasted_iota(jnp.int32, (8, channels), 0)
    packed = jnp.zeros((8, channels), jnp.float32)
    for index, value in enumerate(
        (sums_shift, sums_gain, gain * sums_shift, gain * sums_gain, inv_std)
    ):
        packed = jnp.where(row == index, value, packed)
    for slot in range(sums.shape[0]):
        sums[slot] = packed

    all_rows = (out_rows * out_cols, channels)
    total = None
    for frame in range(frames):
        cots = jnp.concatenate(
            [
                (cot[frame + later] if frame + later < frames else halo[frame + later - frames])
                .reshape(all_rows)
                for later in range(3)
            ],
            axis=1,
        )
        term = dot(act[frame].reshape(all_rows).T, cots)
        total = term if total is None else total + term
    for later in range(3):
        block = total[:, later * channels : (later + 1) * channels] * loss_scale
        temporal[pl.ds(later * channels, channels)] = block.astype(jnp.bfloat16)


def split_rows(values, rows):
    pieces = []
    for value in values:
        rest = value
        for _ in range(3):
            piece = rest.astype(jnp.bfloat16).astype(jnp.float32)
            pieces.append(piece)
            rest = rest - piece
    row = lax.broadcasted_iota(jnp.int32, (rows, values[0].shape[-1]), 0)
    packed = jnp.zeros((rows, values[0].shape[-1]), jnp.float32)
    for index, piece in enumerate(pieces):
        packed = jnp.where(row == index, piece, packed)
    return packed.astype(jnp.bfloat16)


def join_rows(packed, count):
    return [
        packed[3 * i : 3 * i + 1] + packed[3 * i + 1 : 3 * i + 2] + packed[3 * i + 2 : 3 * i + 3]
        for i in range(count)
    ]


def store_rows(chunks, rows, first, values):
    done = 0
    while done < values.shape[0]:
        chunk, at = divmod(first + done, rows)
        count = min(rows - at, values.shape[0] - done)
        chunks[chunk, pl.ds(at, count)] = values[done : done + count]
        done += count


def grad_kernel(
    odd, even, normed, pre, sums, temporal, grads
):
    frames, out_rows, out_cols, channels = normed.shape
    lanes = channels // GROUPS
    members = sums.shape[0] * frames * out_rows * out_cols * lanes
    clip = jnp.sum(sums[...], axis=0)
    inv_std = sums[0, 4:5]
    group = group_spread(clip, lanes) * inv_std / members
    group_shift, group_gain = group[2:3], group[3:4]
    flat = (out_rows * out_cols, channels)
    flat_wide = (out_rows * out_cols, 3 * channels)
    rows = grads.shape[1] - EXTRA
    parts = [None, None, None]
    for frame in range(frames):
        back = (
            pre[frame].reshape(flat) - group_shift - normed[frame].reshape(flat) * group_gain
        )
        back = back.astype(jnp.bfloat16).T
        for tap, source in enumerate(
            (odd.at[frame, pl.ds(0, out_rows)], even.at[frame], odd.at[frame, pl.ds(1, out_rows)])
        ):
            term = dot(back, source[...].reshape(flat_wide))
            parts[tap] = term if parts[tap] is None else parts[tap] + term
    for tap in range(3):
        for side in range(3):
            block = parts[tap][:, side * channels : (side + 1) * channels].T
            store_rows(grads, rows, (3 * tap + side) * channels, block.astype(jnp.bfloat16))
    for tap in range(3):
        block = temporal[pl.ds(tap * channels, channels)]
        store_rows(grads, rows, (9 + tap) * channels, block)
    rest = grads.shape[0] * rows - 12 * channels
    if rest:
        store_rows(grads, rows, 12 * channels, jnp.zeros((rest, channels), jnp.bfloat16))
    share = clip * (1.0 / sums.shape[0])
    extra = split_rows([share[1:2], share[0:1]], EXTRA)
    for chunk in range(grads.shape[0]):
        grads[chunk, pl.ds(rows, EXTRA)] = extra


def total_of(arrived, first, count):
    total = arrived[0, pl.ds(first, count)].astype(jnp.float32)
    for chunk in range(1, arrived.shape[0]):
        total += arrived[chunk, pl.ds(first, count)].astype(jnp.float32)
    return total


def half_kernel(arrived, chunk):
    count = chunk.shape[0] - EXTRA
    chunk[pl.ds(0, count)] = total_of(arrived, 0, count).astype(jnp.bfloat16)
    sums = join_rows(total_of(arrived, count, EXTRA), 2)
    chunk[pl.ds(count, EXTRA)] = split_rows(sums, EXTRA)


def sum_kernel(mine, other, spread, grad_gain, grad_shift):
    count = spread.shape[1]
    wide = [source[...].astype(jnp.float32) for source in (mine, other)]
    total = (wide[0][:count] + wide[1][:count]).astype(jnp.bfloat16)
    for slot in range(spread.shape[0]):
        spread[slot] = total
    sums = [join_rows(source[count:], 2) for source in wide]
    grad_gain[...] = sums[0][0] + sums[1][0]
    grad_shift[...] = sums[0][1] + sums[1][1]


def final_kernel(arrived, grad_spatial, grad_temporal):
    rows = grad_spatial.shape[0]
    grad_spatial[...] = arrived[pl.ds(0, rows)].astype(jnp.float32)
    grad_temporal[...] = arrived[pl.ds(rows, grad_temporal.shape[0])].astype(jnp.float32)


def encode_kernel(per_clip, act, halo, weights, encoded):
    frames, out_rows, out_cols, channels = act.shape
    not_first = lax.rem(lax.axis_index("seq"), per_clip) != 0
    flat = (STEP_ROWS * out_cols, channels)
    for frame in range(frames):

        def one(step, frame=frame):
            rows = pl.ds(step * STEP_ROWS, STEP_ROWS)
            total = None
            for tap in range(3):
                if frame >= tap:
                    source = act[frame - tap, rows]
                else:
                    source = halo[frames + frame - tap, rows]
                    source = jnp.where(not_first, source, jnp.zeros_like(source))
                term = dot(source.reshape(flat), weights[tap])
                total = term if total is None else total + term
            encoded[frame, rows] = total.astype(jnp.bfloat16).reshape(
                STEP_ROWS, out_cols, channels
            )

        each(out_rows // STEP_ROWS, one)


def on_device(video_in, w_spatial, w_temporal, norm_gain, norm_shift, cotangent):
    frames, height, width, channels = video_in.shape[1:]
    out_rows, out_cols = height // 2, width // 2
    dp_size, seq_size = lax.axis_size("dp"), lax.axis_size("seq")
    devices = dp_size * seq_size
    per_clip = FRAMES // frames
    assert frames >= 2 and FRAMES % frames == 0
    loss_scale = float(devices * frames * out_rows * out_cols) ** (-0.5)
    shape = (frames, out_rows, out_cols, channels)
    positions = frames * out_rows * out_cols
    video = video_in[0]
    cot = cotangent[0]
    f32, bf16 = jnp.float32, jnp.bfloat16
    struct = jax.ShapeDtypeStruct

    ahead_pairs = [
        (s, s // per_clip * per_clip + (s + 1) % per_clip) for s in range(seq_size)
    ]
    back_pairs = [(target, source) for source, target in ahead_pairs]
    clips = [list(range(first, first + per_clip)) for first in range(0, seq_size, per_clip)]

    def exchange(value, axes, groups=None):
        return lax.all_to_all(value, axes, 0, 0, axis_index_groups=groups, tiled=True)

    gate = pl.pallas_call(
        open_kernel,
        out_shape=struct((8, channels), f32),
        out_specs=WHOLE,
        cost_estimate=pl.CostEstimate(
            flops=2 * positions * 9 * channels * channels,
            bytes_accessed=2 * video.size,
            transcendentals=0,
        ),
    )()
    cot_out, gate = lax.optimization_barrier((cot, gate))
    cot_halo = lax.ppermute(cot_out, "seq", back_pairs)

    pieces = 2 * frames
    def far(value):
        return pltpu.with_memory_space_constraint(value, pltpu.HBM)

    spatial, stats, odd, even, params = call(
        functools.partial(conv_kernel, pieces),
        (
            struct(shape, f32),
            struct((per_clip, 8, channels), f32),
            struct((frames, out_rows + 1, out_cols, 3 * channels), bf16),
            struct((frames, out_rows, out_cols, 3 * channels), bf16),
            struct((8, channels), f32),
        ),
        (
            gate,
            video,
            far(w_spatial.reshape(3, 3 * channels, channels)),
            far(norm_gain[None]),
            far(norm_shift[None]),
        ),
        specs=[WHOLE] * 2 + [FAR] * 3,
        scratch=[
            pltpu.VMEM((4 * STEP_ROWS, 8 + width, channels), f32),
            pltpu.VMEM((3, 3 * channels, channels), bf16),
            pltpu.SemaphoreType.DMA((3,)),
        ],
        flops=2 * positions * 9 * channels * channels,
    )
    stats = exchange(stats, "seq", clips)
    act, normed, pre, temporal, own = call(
        functools.partial(act_kernel, loss_scale),
        (
            struct(shape, bf16),
            struct(shape, f32),
            struct(shape, f32),
            struct((3 * channels, channels), bf16),
            struct((per_clip, 8, channels), f32),
        ),
        (spatial, stats, cot, cot_halo, w_temporal, params),
        scratch=[pltpu.VMEM((2,) + shape[1:], bf16)],
        flops=2 * positions * 3 * channels * channels,
    )
    act_halo = lax.ppermute(act, "seq", ahead_pairs)
    sums = exchange(own, "seq", clips)
    halves = 2 if seq_size % 2 == 0 else 1
    half = seq_size // halves
    near = [
        [d * seq_size + s for d in range(dp_size) for s in range(first, first + half)]
        for first in range(0, seq_size, half)
    ]
    count = dp_size * half
    rows = -(-12 * channels // (16 * count)) * 16
    sums, act_halo = lax.optimization_barrier((sums, act_halo))
    grads = call(
        grad_kernel,
        struct((count, rows + EXTRA, channels), bf16),
        (odd, even, normed, pre, sums, temporal),
        flops=2 * positions * 9 * channels * channels,
    )
    grads = exchange(grads, ("dp", "seq"), near)
    mine = call(half_kernel, struct((rows + EXTRA, channels), bf16), (grads,))
    if halves == 2:
        other = lax.ppermute(mine, "seq", [(s, (s + half) % seq_size) for s in range(seq_size)])
    else:
        other = jnp.zeros_like(mine)
    act, act_halo, _ = lax.optimization_barrier((act, act_halo, mine))
    encoded = call(
        functools.partial(encode_kernel, per_clip),
        struct(shape, bf16),
        (act, act_halo, w_temporal),
        flops=2 * positions * 3 * channels * channels,
    )
    other, encoded = lax.optimization_barrier((other, encoded))
    grads, grad_gain, grad_shift = call(
        sum_kernel,
        (
            struct((count, rows, channels), bf16),
            struct((1, channels), f32),
            struct((1, channels), f32),
        ),
        (mine, other),
    )
    grads = exchange(grads, ("dp", "seq"), near)
    grad_spatial, grad_temporal = call(
        final_kernel,
        (struct((9 * channels, channels), f32), struct((3 * channels, channels), f32)),
        (grads.reshape(count * rows, channels),),
    )
    return (
        encoded[None],
        grad_spatial.reshape(3, 3, channels, channels),
        grad_temporal.reshape(3, channels, channels),
        grad_gain[0],
        grad_shift[0],
    )


def solution(mesh):
    placed = P("dp", "seq", None, None, None)
    return jax.shard_map(
        on_device,
        mesh=mesh,
        in_specs=(placed, P(), P(), P(), P(), placed),
        out_specs=(placed, P(), P(), P(), P()),
        check_vma=False,
    )
```

```python
import functools
import math

import jax
import jax.numpy as jnp
from jax import lax
from jax.experimental import pallas as pl
from jax.experimental.pallas import tpu as pltpu
from jax.sharding import PartitionSpec as P

GROUPS = 32
FRAMES = 8
STEP_ROWS = 8
EXTRA = 8
SPARE_BYTES = 4 * 1024 * 1024

WHOLE = pl.BlockSpec(memory_space=pltpu.VMEM)
FAR = pl.BlockSpec(memory_space=pltpu.HBM)


def dot(left, right):
    return jnp.dot(left, right, preferred_element_type=jnp.float32)


def dot_transposed(left, right):
    return lax.dot_general(
        left, right, (((1,), (1,)), ((), ())), preferred_element_type=jnp.float32
    )


def each(count, body):
    if count <= 8:
        for step in range(count):
            body(step)
    else:
        lax.fori_loop(0, count, lambda step, carry: (body(step), carry)[1], 0)


def call(kernel, out_shape, operands, specs=None, scratch=(), flops=0):
    sizes = [value.size * value.dtype.itemsize for value in operands]
    sizes += [value.size * value.dtype.itemsize for value in jax.tree.leaves(out_shape)]
    held = sum(math.prod(item.shape) * 4 for item in scratch if hasattr(item, "shape"))
    return pl.pallas_call(
        kernel,
        out_shape=out_shape,
        in_specs=specs or [WHOLE] * len(operands),
        out_specs=jax.tree.map(lambda _: WHOLE, out_shape),
        scratch_shapes=list(scratch),
        compiler_params=pltpu.CompilerParams(vmem_limit_bytes=sum(sizes) + held + SPARE_BYTES),
        cost_estimate=pl.CostEstimate(
            flops=flops, bytes_accessed=sum(sizes), transcendentals=0
        ),
    )(*operands)


def group_spread(values, lanes):
    channels = values.shape[-1]
    shift = 1
    while shift < lanes:
        values = values + pltpu.roll(values, channels - shift, 1)
        shift *= 2
    lane = lax.broadcasted_iota(jnp.int32, values.shape, 1)
    values = jnp.where(lax.rem(lane, lanes) == 0, values, 0.0)
    shift = 1
    while shift < lanes:
        values = values + pltpu.roll(values, shift, 1)
        shift *= 2
    return values


def open_kernel(gate):
    gate[...] = jnp.zeros(gate.shape, gate.dtype)


def conv_kernel(
    pieces, blank, video, weights_far, gain_far, shift_far, spatial, stats, odd, even, params, wide,
    weights, arrived,
):
    frames, height, width, channels = video.shape
    out_rows, out_cols = height // 2, width // 2
    positions = frames * out_rows * out_cols
    half = height * frames // pieces
    params[...] = blank[...]
    copies = [
        pltpu.make_async_copy(source, target, arrived.at[index])
        for index, (source, target) in enumerate(
            ((weights_far, weights), (gain_far, params.at[0:1]), (shift_far, params.at[1:2]))
        )
    ]
    for copy in copies:
        copy.start()
    for slot in range(wide.shape[0]):
        wide[slot, 0:8] = jnp.zeros((8, channels), jnp.float32)
    for frame in range(frames):
        odd[frame, 0] = jnp.zeros((out_cols, 3 * channels), jnp.bfloat16)
    flat = (STEP_ROWS * out_cols, 3 * channels)
    steps = half // 2 // STEP_ROWS

    def place(piece, step):
        return piece * half // height, piece * half % height // 2 + step * STEP_ROWS

    def separate(piece, step):
        frame, first = place(piece, step)
        base = piece % 2 * 2 * STEP_ROWS
        for line in range(2 * STEP_ROWS):
            wide[base + line, 8 : 8 + width] = video[frame, 2 * first + line].astype(jnp.float32)
        for line in range(2 * STEP_ROWS):
            for tap in range(3):
                value = wide[base + line, pl.ds(7 + tap, out_cols, stride=2), :]
                lanes = slice(tap * channels, (tap + 1) * channels)
                if line % 2:
                    odd[frame, first + line // 2 + 1, :, lanes] = value.astype(jnp.bfloat16)
                else:
                    even[frame, first + line // 2, :, lanes] = value.astype(jnp.bfloat16)

    def multiply(piece, step):
        frame, first = place(piece, step)
        total = dot(odd[frame, pl.ds(first, STEP_ROWS)].reshape(flat), weights[0])
        total += dot(even[frame, pl.ds(first, STEP_ROWS)].reshape(flat), weights[1])
        total += dot(odd[frame, pl.ds(first + 1, STEP_ROWS)].reshape(flat), weights[2])
        spatial[frame, pl.ds(first, STEP_ROWS)] = total.reshape(STEP_ROWS, out_cols, channels)
        return total

    def fold(values):
        return values.reshape(-1, 8, channels).sum(axis=0)

    def over_steps(piece, term, start):
        if steps <= 8:
            for step in range(steps):
                start = jax.tree.map(jnp.add, start, term(piece, step))
            return start
        return lax.fori_loop(
            0, steps, lambda step, sums: jax.tree.map(jnp.add, sums, term(piece, step)), start
        )

    zero = jnp.zeros((8, channels), jnp.float32)

    def first_sum(piece, step):
        return fold(multiply(piece, step))

    def first_moments(piece, step):
        frame, first = place(piece, step)
        off = spatial[frame, pl.ds(first, STEP_ROWS)].reshape(-1, channels) - near
        return fold(off), fold(off * off)

    def moments(piece, step):
        off = multiply(piece, step) - near
        return fold(off), fold(off * off)

    for piece in range(pieces):
        each(steps, functools.partial(separate, piece))
    copies[0].wait()
    near = over_steps(0, first_sum, zero).sum(axis=0, keepdims=True) * (pieces / positions)
    sums = over_steps(0, first_moments, (zero, zero))
    for piece in range(1, pieces - 1):
        sums = over_steps(piece, moments, sums)
    sums = over_steps(pieces - 1, moments, sums)
    off = sums[0].sum(axis=0, keepdims=True) / positions
    mean = near + off
    square = sums[1].sum(axis=0, keepdims=True) - positions * off * off
    row = lax.broadcasted_iota(jnp.int32, (8, channels), 0)
    packed = jnp.where(row == 0, mean, jnp.where(row == 1, square, 0.0))
    for slot in range(stats.shape[0]):
        stats[slot] = packed
    for copy in copies[1:]:
        copy.wait()

def clip_norm(stats, positions, lanes):
    cells = stats.shape[0] * lanes
    means = [stats[member, 0:1] for member in range(stats.shape[0])]
    squares = [stats[member, 1:2] for member in range(stats.shape[0])]
    mean = group_spread(jnp.broadcast_to(sum(means), (8, means[0].shape[-1])), lanes)[0:1] / cells
    square = sum(squares)
    for value in means:
        square = square + positions * (value - mean) ** 2
    square = group_spread(jnp.broadcast_to(square, (8, square.shape[-1])), lanes)[0:1]
    return mean, lax.rsqrt(square / (cells * positions) + 1e-05)


def act_kernel(
    loss_scale, spatial, stats, cot, arrived, weights, params, act, normed, pre, temporal, sums,
    halo,
):
    frames, out_rows, out_cols, channels = spatial.shape
    positions = frames * out_rows * out_cols
    mean, inv_std = clip_norm(stats, positions, channels // GROUPS)
    gain, shift = params[0:1], params[1:2]
    per_clip = sums.shape[0]
    not_last = lax.rem(lax.axis_index("seq"), per_clip) != per_clip - 1
    for frame in range(2):
        value = arrived[frame]
        halo[frame] = jnp.where(not_last, value, jnp.zeros_like(value))
    turned_weights = jnp.concatenate([weights[tap] for tap in range(3)], axis=1)
    flat = (STEP_ROWS * out_cols, channels)
    shaped = (STEP_ROWS, out_cols, channels)
    sums_shift = jnp.zeros((8, channels), jnp.float32)
    sums_gain = jnp.zeros((8, channels), jnp.float32)

    def fold(values):
        return values.reshape(-1, 8, channels).sum(axis=0)

    for frame in range(frames):

        def cot_block(later, rows):
            if frame + later < frames:
                return cot[frame + later, rows].reshape(flat)
            return halo[frame + later - frames, rows].reshape(flat)

        def one(step, carry):
            rows = pl.ds(step * STEP_ROWS, STEP_ROWS)
            norm = (spatial[frame, rows].reshape(flat) - mean) * inv_std
            before = norm * gain + shift
            sig = jax.nn.sigmoid(before)
            act[frame, rows] = (before * sig).astype(jnp.bfloat16).reshape(shaped)
            cots = jnp.concatenate([cot_block(later, rows) for later in range(3)], axis=1)
            back = dot_transposed(cots, turned_weights)
            back = back.astype(jnp.bfloat16).astype(jnp.float32)
            back_pre = back * loss_scale * sig * (1.0 + before * (1.0 - sig))
            normed[frame, rows] = norm.reshape(shaped)
            pre[frame, rows] = (back_pre * (gain * inv_std)).reshape(shaped)
            return (carry[0] + fold(back_pre), carry[1] + fold(back_pre * norm))

        steps = out_rows // STEP_ROWS
        if steps <= 4:
            for step in range(steps):
                sums_shift, sums_gain = one(step, (sums_shift, sums_gain))
        else:
            sums_shift, sums_gain = lax.fori_loop(0, steps, one, (sums_shift, sums_gain))

    sums_shift = sums_shift.sum(axis=0, keepdims=True)
    sums_gain = sums_gain.sum(axis=0, keepdims=True)
    row = lax.broadcasted_iota(jnp.int32, (8, channels), 0)
    packed = jnp.zeros((8, channels), jnp.float32)
    for index, value in enumerate(
        (sums_shift, sums_gain, gain * sums_shift, gain * sums_gain, inv_std)
    ):
        packed = jnp.where(row == index, value, packed)
    for slot in range(sums.shape[0]):
        sums[slot] = packed

    all_rows = (out_rows * out_cols, channels)
    total = None
    for frame in range(frames):
        cots = jnp.concatenate(
            [
                (cot[frame + later] if frame + later < frames else halo[frame + later - frames])
                .reshape(all_rows)
                for later in range(3)
            ],
            axis=1,
        )
        term = dot(act[frame].reshape(all_rows).T, cots)
        total = term if total is None else total + term
    for later in range(3):
        block = total[:, later * channels : (later + 1) * channels] * loss_scale
        temporal[pl.ds(later * channels, channels)] = block.astype(jnp.bfloat16)


def split_rows(values, rows):
    pieces = []
    for value in values:
        rest = value
        for _ in range(3):
            piece = rest.astype(jnp.bfloat16).astype(jnp.float32)
            pieces.append(piece)
            rest = rest - piece
    row = lax.broadcasted_iota(jnp.int32, (rows, values[0].shape[-1]), 0)
    packed = jnp.zeros((rows, values[0].shape[-1]), jnp.float32)
    for index, piece in enumerate(pieces):
        packed = jnp.where(row == index, piece, packed)
    return packed.astype(jnp.bfloat16)


def join_rows(packed, count):
    return [
        packed[3 * i : 3 * i + 1] + packed[3 * i + 1 : 3 * i + 2] + packed[3 * i + 2 : 3 * i + 3]
        for i in range(count)
    ]


def store_rows(chunks, rows, first, values):
    done = 0
    while done < values.shape[0]:
        chunk, at = divmod(first + done, rows)
        count = min(rows - at, values.shape[0] - done)
        chunks[chunk, pl.ds(at, count)] = values[done : done + count]
        done += count


def grad_kernel(
    odd, even, normed, pre, sums, temporal, grads
):
    frames, out_rows, out_cols, channels = normed.shape
    lanes = channels // GROUPS
    members = sums.shape[0] * frames * out_rows * out_cols * lanes
    clip = jnp.sum(sums[...], axis=0)
    inv_std = sums[0, 4:5]
    group = group_spread(clip, lanes) * inv_std / members
    group_shift, group_gain = group[2:3], group[3:4]
    flat = (out_rows * out_cols, channels)
    flat_wide = (out_rows * out_cols, 3 * channels)
    rows = grads.shape[1] - EXTRA
    parts = [None, None, None]
    for frame in range(frames):
        back = (
            pre[frame].reshape(flat) - group_shift - normed[frame].reshape(flat) * group_gain
        )
        back = back.astype(jnp.bfloat16).T
        for tap, source in enumerate(
            (odd.at[frame, pl.ds(0, out_rows)], even.at[frame], odd.at[frame, pl.ds(1, out_rows)])
        ):
            term = dot(back, source[...].reshape(flat_wide))
            parts[tap] = term if parts[tap] is None else parts[tap] + term
    for tap in range(3):
        for side in range(3):
            block = parts[tap][:, side * channels : (side + 1) * channels].T
            store_rows(grads, rows, (3 * tap + side) * channels, block.astype(jnp.bfloat16))
    for tap in range(3):
        block = temporal[pl.ds(tap * channels, channels)]
        store_rows(grads, rows, (9 + tap) * channels, block)
    rest = grads.shape[0] * rows - 12 * channels
    if rest:
        store_rows(grads, rows, 12 * channels, jnp.zeros((rest, channels), jnp.bfloat16))
    share = clip * (1.0 / sums.shape[0])
    extra = split_rows([share[1:2], share[0:1]], EXTRA)
    for chunk in range(grads.shape[0]):
        grads[chunk, pl.ds(rows, EXTRA)] = extra


def total_of(arrived, first, count):
    total = arrived[0, pl.ds(first, count)].astype(jnp.float32)
    for chunk in range(1, arrived.shape[0]):
        total += arrived[chunk, pl.ds(first, count)].astype(jnp.float32)
    return total


def half_kernel(arrived, chunk):
    count = chunk.shape[0] - EXTRA
    chunk[pl.ds(0, count)] = total_of(arrived, 0, count).astype(jnp.bfloat16)
    sums = join_rows(total_of(arrived, count, EXTRA), 2)
    chunk[pl.ds(count, EXTRA)] = split_rows(sums, EXTRA)


def sum_kernel(mine, other, spread, grad_gain, grad_shift):
    count = spread.shape[1]
    wide = [source[...].astype(jnp.float32) for source in (mine, other)]
    total = (wide[0][:count] + wide[1][:count]).astype(jnp.bfloat16)
    for slot in range(spread.shape[0]):
        spread[slot] = total
    sums = [join_rows(source[count:], 2) for source in wide]
    grad_gain[...] = sums[0][0] + sums[1][0]
    grad_shift[...] = sums[0][1] + sums[1][1]


def final_kernel(arrived, grad_spatial, grad_temporal):
    rows = grad_spatial.shape[0]
    grad_spatial[...] = arrived[pl.ds(0, rows)].astype(jnp.float32)
    grad_temporal[...] = arrived[pl.ds(rows, grad_temporal.shape[0])].astype(jnp.float32)


def near_encode_kernel(act, weights, part):
    frames, out_rows, out_cols, channels = act.shape
    flat = (STEP_ROWS * out_cols, channels)
    for frame in range(frames):

        def one(step, frame=frame):
            rows = pl.ds(step * STEP_ROWS, STEP_ROWS)
            total = dot(act[frame, rows].reshape(flat), weights[0])
            for tap in range(1, min(frame, 2) + 1):
                total += dot(act[frame - tap, rows].reshape(flat), weights[tap])
            part[frame, rows] = total.reshape(STEP_ROWS, out_cols, channels)

        each(out_rows // STEP_ROWS, one)


def encode_kernel(per_clip, part, halo, weights, encoded):
    frames, out_rows, out_cols, channels = halo.shape
    not_first = lax.rem(lax.axis_index("seq"), per_clip) != 0
    flat = (STEP_ROWS * out_cols, channels)
    for frame in range(frames):

        def one(step, frame=frame):
            rows = pl.ds(step * STEP_ROWS, STEP_ROWS)
            total = part[frame, rows].reshape(flat)
            for tap in range(frame + 1, 3):
                source = halo[frames + frame - tap, rows].reshape(flat)
                source = jnp.where(not_first, source, jnp.zeros_like(source))
                total += dot(source, weights[tap])
            encoded[frame, rows] = total.astype(jnp.bfloat16).reshape(
                STEP_ROWS, out_cols, channels
            )

        each(out_rows // STEP_ROWS, one)


def on_device(video_in, w_spatial, w_temporal, norm_gain, norm_shift, cotangent):
    frames, height, width, channels = video_in.shape[1:]
    out_rows, out_cols = height // 2, width // 2
    dp_size, seq_size = lax.axis_size("dp"), lax.axis_size("seq")
    devices = dp_size * seq_size
    per_clip = FRAMES // frames
    assert frames >= 2 and FRAMES % frames == 0
    loss_scale = float(devices * frames * out_rows * out_cols) ** (-0.5)
    shape = (frames, out_rows, out_cols, channels)
    positions = frames * out_rows * out_cols
    video = video_in[0]
    cot = cotangent[0]
    f32, bf16 = jnp.float32, jnp.bfloat16
    struct = jax.ShapeDtypeStruct

    ahead_pairs = [
        (s, s // per_clip * per_clip + (s + 1) % per_clip) for s in range(seq_size)
    ]
    back_pairs = [(target, source) for source, target in ahead_pairs]
    clips = [list(range(first, first + per_clip)) for first in range(0, seq_size, per_clip)]

    def exchange(value, axes, groups=None):
        return lax.all_to_all(value, axes, 0, 0, axis_index_groups=groups, tiled=True)

    gate = pl.pallas_call(
        open_kernel,
        out_shape=pltpu.VMEM((8, channels), f32),
        out_specs=WHOLE,
        cost_estimate=pl.CostEstimate(
            flops=2 * positions * 9 * channels * channels,
            bytes_accessed=2 * video.size,
            transcendentals=0,
        ),
    )()
    cot_out, gate = lax.optimization_barrier((cot, gate))
    cot_halo = lax.ppermute(cot_out, "seq", back_pairs)

    pieces = 2 * frames
    def far(value):
        return pltpu.with_memory_space_constraint(value, pltpu.HBM)

    spatial, stats, odd, even, params = call(
        functools.partial(conv_kernel, pieces),
        (
            struct(shape, f32),
            struct((per_clip, 8, channels), f32),
            struct((frames, out_rows + 1, out_cols, 3 * channels), bf16),
            struct((frames, out_rows, out_cols, 3 * channels), bf16),
            struct((8, channels), f32),
        ),
        (
            gate,
            video,
            far(w_spatial.reshape(3, 3 * channels, channels)),
            far(norm_gain[None]),
            far(norm_shift[None]),
        ),
        specs=[WHOLE] * 2 + [FAR] * 3,
        scratch=[
            pltpu.VMEM((4 * STEP_ROWS, 8 + width, channels), f32),
            pltpu.VMEM((3, 3 * channels, channels), bf16),
            pltpu.SemaphoreType.DMA((3,)),
        ],
        flops=2 * positions * 9 * channels * channels,
    )
    stats = exchange(stats, "seq", clips)
    act, normed, pre, temporal, own = call(
        functools.partial(act_kernel, loss_scale),
        (
            struct(shape, bf16),
            struct(shape, f32),
            struct(shape, f32),
            struct((3 * channels, channels), bf16),
            struct((per_clip, 8, channels), f32),
        ),
        (spatial, stats, cot, cot_halo, w_temporal, params),
        scratch=[pltpu.VMEM((2,) + shape[1:], bf16)],
        flops=2 * positions * 3 * channels * channels,
    )
    sums = exchange(own, "seq", clips)
    halves = 2 if seq_size % 2 == 0 else 1
    half = seq_size // halves
    near = [
        [d * seq_size + s for d in range(dp_size) for s in range(first, first + half)]
        for first in range(0, seq_size, half)
    ]
    count = dp_size * half
    rows = -(-12 * channels // (16 * count)) * 16
    grads = call(
        grad_kernel,
        struct((count, rows + EXTRA, channels), bf16),
        (odd, even, normed, pre, sums, temporal),
        flops=2 * positions * 9 * channels * channels,
    )
    grads = exchange(grads, ("dp", "seq"), near)
    mine = call(half_kernel, struct((rows + EXTRA, channels), bf16), (grads,))
    if halves == 2:
        other = lax.ppermute(mine, "seq", [(s, (s + half) % seq_size) for s in range(seq_size)])
    else:
        other = jnp.zeros_like(mine)
    act, _ = lax.optimization_barrier((act, mine))
    part = call(
        near_encode_kernel,
        struct(shape, f32),
        (act, w_temporal),
        flops=2 * positions * 2 * channels * channels,
    )
    act, part = lax.optimization_barrier((act, part))
    act_halo = lax.ppermute(act, "seq", ahead_pairs)
    other, part = lax.optimization_barrier((other, part))
    encoded = call(
        functools.partial(encode_kernel, per_clip),
        struct(shape, bf16),
        (part, act_halo, w_temporal),
        flops=512 * positions * channels * channels,
    )
    grads, grad_gain, grad_shift = call(
        sum_kernel,
        (
            struct((count, rows, channels), bf16),
            struct((1, channels), f32),
            struct((1, channels), f32),
        ),
        (mine, other),
    )
    grads = exchange(grads, ("dp", "seq"), near)
    grad_spatial, grad_temporal = call(
        final_kernel,
        (struct((9 * channels, channels), f32), struct((3 * channels, channels), f32)),
        (grads.reshape(count * rows, channels),),
    )
    return (
        encoded[None],
        grad_spatial.reshape(3, 3, channels, channels),
        grad_temporal.reshape(3, channels, channels),
        grad_gain[0],
        grad_shift[0],
    )


def solution(mesh):
    placed = P("dp", "seq", None, None, None)
    return jax.shard_map(
        on_device,
        mesh=mesh,
        in_specs=(placed, P(), P(), P(), P(), placed),
        out_specs=(placed, P(), P(), P(), P()),
        check_vma=False,
    )
```

```python
import functools
import math

import jax
import jax.numpy as jnp
from jax import lax
from jax.experimental import pallas as pl
from jax.experimental.pallas import tpu as pltpu
from jax.sharding import PartitionSpec as P

GROUPS = 32
FRAMES = 8
STEP_ROWS = 8
EXTRA = 8
SPARE_BYTES = 4 * 1024 * 1024

WHOLE = pl.BlockSpec(memory_space=pltpu.VMEM)
FAR = pl.BlockSpec(memory_space=pltpu.HBM)


def dot(left, right):
    return jnp.dot(left, right, preferred_element_type=jnp.float32)


def dot_transposed(left, right):
    return lax.dot_general(
        left, right, (((1,), (1,)), ((), ())), preferred_element_type=jnp.float32
    )


def each(count, body):
    if count <= 8:
        for step in range(count):
            body(step)
    else:
        lax.fori_loop(0, count, lambda step, carry: (body(step), carry)[1], 0)


def call(kernel, out_shape, operands, specs=None, scratch=(), flops=0):
    sizes = [value.size * value.dtype.itemsize for value in operands]
    sizes += [value.size * value.dtype.itemsize for value in jax.tree.leaves(out_shape)]
    held = sum(math.prod(item.shape) * 4 for item in scratch if hasattr(item, "shape"))
    return pl.pallas_call(
        kernel,
        out_shape=out_shape,
        in_specs=specs or [WHOLE] * len(operands),
        out_specs=jax.tree.map(lambda _: WHOLE, out_shape),
        scratch_shapes=list(scratch),
        compiler_params=pltpu.CompilerParams(vmem_limit_bytes=sum(sizes) + held + SPARE_BYTES),
        cost_estimate=pl.CostEstimate(
            flops=flops, bytes_accessed=sum(sizes), transcendentals=0
        ),
    )(*operands)


def group_spread(values, lanes):
    channels = values.shape[-1]
    shift = 1
    while shift < lanes:
        values = values + pltpu.roll(values, channels - shift, 1)
        shift *= 2
    lane = lax.broadcasted_iota(jnp.int32, values.shape, 1)
    values = jnp.where(lax.rem(lane, lanes) == 0, values, 0.0)
    shift = 1
    while shift < lanes:
        values = values + pltpu.roll(values, shift, 1)
        shift *= 2
    return values


def open_kernel(gate):
    gate[...] = jnp.zeros(gate.shape, gate.dtype)


def conv_kernel(
    pieces, blank, video, weights_far, gain_far, shift_far, spatial, stats, odd, even, params, wide,
    weights, arrived,
):
    frames, height, width, channels = video.shape
    out_rows, out_cols = height // 2, width // 2
    positions = frames * out_rows * out_cols
    half = height * frames // pieces
    params[...] = blank[...]
    copies = [
        pltpu.make_async_copy(source, target, arrived.at[index])
        for index, (source, target) in enumerate(
            ((weights_far, weights), (gain_far, params.at[0:1]), (shift_far, params.at[1:2]))
        )
    ]
    for copy in copies:
        copy.start()
    for slot in range(wide.shape[0]):
        wide[slot, 0:8] = jnp.zeros((8, channels), jnp.float32)
    for frame in range(frames):
        odd[frame, 0] = jnp.zeros((out_cols, 3 * channels), jnp.bfloat16)
    flat = (STEP_ROWS * out_cols, 3 * channels)
    steps = half // 2 // STEP_ROWS

    def place(piece, step):
        return piece * half // height, piece * half % height // 2 + step * STEP_ROWS

    def separate(piece, step):
        frame, first = place(piece, step)
        base = piece % 2 * 2 * STEP_ROWS
        for line in range(2 * STEP_ROWS):
            wide[base + line, 8 : 8 + width] = video[frame, 2 * first + line].astype(jnp.float32)
        for line in range(2 * STEP_ROWS):
            for tap in range(3):
                value = wide[base + line, pl.ds(7 + tap, out_cols, stride=2), :]
                lanes = slice(tap * channels, (tap + 1) * channels)
                if line % 2:
                    odd[frame, first + line // 2 + 1, :, lanes] = value.astype(jnp.bfloat16)
                else:
                    even[frame, first + line // 2, :, lanes] = value.astype(jnp.bfloat16)

    def multiply(piece, step):
        frame, first = place(piece, step)
        total = dot(odd[frame, pl.ds(first, STEP_ROWS)].reshape(flat), weights[0])
        total += dot(even[frame, pl.ds(first, STEP_ROWS)].reshape(flat), weights[1])
        total += dot(odd[frame, pl.ds(first + 1, STEP_ROWS)].reshape(flat), weights[2])
        spatial[frame, pl.ds(first, STEP_ROWS)] = total.reshape(STEP_ROWS, out_cols, channels)
        return total

    def fold(values):
        return values.reshape(-1, 8, channels).sum(axis=0)

    def over_steps(piece, term, start):
        if steps <= 8:
            for step in range(steps):
                start = jax.tree.map(jnp.add, start, term(piece, step))
            return start
        return lax.fori_loop(
            0, steps, lambda step, sums: jax.tree.map(jnp.add, sums, term(piece, step)), start
        )

    zero = jnp.zeros((8, channels), jnp.float32)

    def first_sum(piece, step):
        return fold(multiply(piece, step))

    def first_moments(piece, step):
        frame, first = place(piece, step)
        off = spatial[frame, pl.ds(first, STEP_ROWS)].reshape(-1, channels) - near
        return fold(off), fold(off * off)

    def moments(piece, step):
        off = multiply(piece, step) - near
        return fold(off), fold(off * off)

    for piece in range(pieces):
        each(steps, functools.partial(separate, piece))
    copies[0].wait()
    near = over_steps(0, first_sum, zero).sum(axis=0, keepdims=True) * (pieces / positions)
    sums = over_steps(0, first_moments, (zero, zero))
    for piece in range(1, pieces - 1):
        sums = over_steps(piece, moments, sums)
    sums = over_steps(pieces - 1, moments, sums)
    off = sums[0].sum(axis=0, keepdims=True) / positions
    mean = near + off
    square = sums[1].sum(axis=0, keepdims=True) - positions * off * off
    row = lax.broadcasted_iota(jnp.int32, (8, channels), 0)
    packed = jnp.where(row == 0, mean, jnp.where(row == 1, square, 0.0))
    for slot in range(stats.shape[0]):
        stats[slot] = packed
    for copy in copies[1:]:
        copy.wait()

def clip_norm(stats, positions, lanes):
    cells = stats.shape[0] * lanes
    means = [stats[member, 0:1] for member in range(stats.shape[0])]
    squares = [stats[member, 1:2] for member in range(stats.shape[0])]
    mean = group_spread(jnp.broadcast_to(sum(means), (8, means[0].shape[-1])), lanes)[0:1] / cells
    square = sum(squares)
    for value in means:
        square = square + positions * (value - mean) ** 2
    square = group_spread(jnp.broadcast_to(square, (8, square.shape[-1])), lanes)[0:1]
    return mean, lax.rsqrt(square / (cells * positions) + 1e-05)


def act_kernel(loss_scale, spatial, stats, params, act, normed, slope, scales):
    frames, out_rows, out_cols, channels = spatial.shape
    positions = frames * out_rows * out_cols
    mean, inv_std = clip_norm(stats, positions, channels // GROUPS)
    gain, shift = params[0:1], params[1:2]
    row = lax.broadcasted_iota(jnp.int32, (8, channels), 0)
    scales[...] = jnp.where(row == 0, inv_std, gain)
    flat = (STEP_ROWS * out_cols, channels)
    shaped = (STEP_ROWS, out_cols, channels)
    for frame in range(frames):

        def one(step, frame=frame):
            rows = pl.ds(step * STEP_ROWS, STEP_ROWS)
            norm = (spatial[frame, rows].reshape(flat) - mean) * inv_std
            before = norm * gain + shift
            sig = jax.nn.sigmoid(before)
            act[frame, rows] = (before * sig).astype(jnp.bfloat16).reshape(shaped)
            normed[frame, rows] = norm.reshape(shaped)
            slope[frame, rows] = (loss_scale * sig * (1.0 + before * (1.0 - sig))).reshape(shaped)

        each(out_rows // STEP_ROWS, one)


def back_kernel(
    loss_scale, cot, arrived, weights, scales, normed, slope, act, pre, temporal, sums, halo
):
    frames, out_rows, out_cols, channels = cot.shape
    inv_std, gain = scales[0:1], scales[1:2]
    per_clip = sums.shape[0]
    not_last = lax.rem(lax.axis_index("seq"), per_clip) != per_clip - 1
    for frame in range(2):
        value = arrived[frame]
        halo[frame] = jnp.where(not_last, value, jnp.zeros_like(value))
    turned_weights = jnp.concatenate([weights[tap] for tap in range(3)], axis=1)
    flat = (STEP_ROWS * out_cols, channels)
    shaped = (STEP_ROWS, out_cols, channels)
    sums_shift = jnp.zeros((8, channels), jnp.float32)
    sums_gain = jnp.zeros((8, channels), jnp.float32)

    def fold(values):
        return values.reshape(-1, 8, channels).sum(axis=0)

    for frame in range(frames):

        def cot_block(later, rows, shape, frame=frame):
            if frame + later < frames:
                return cot[frame + later, rows].reshape(shape)
            return halo[frame + later - frames, rows].reshape(shape)

        def one(step, carry, frame=frame):
            rows = pl.ds(step * STEP_ROWS, STEP_ROWS)
            cots = jnp.concatenate([cot_block(later, rows, flat) for later in range(3)], axis=1)
            back = dot_transposed(cots, turned_weights)
            back = back.astype(jnp.bfloat16).astype(jnp.float32)
            back_pre = back * slope[frame, rows].reshape(flat)
            norm = normed[frame, rows].reshape(flat)
            pre[frame, rows] = (back_pre * (gain * inv_std)).reshape(shaped)
            return (carry[0] + fold(back_pre), carry[1] + fold(back_pre * norm))

        steps = out_rows // STEP_ROWS
        if steps <= 4:
            for step in range(steps):
                sums_shift, sums_gain = one(step, (sums_shift, sums_gain))
        else:
            sums_shift, sums_gain = lax.fori_loop(0, steps, one, (sums_shift, sums_gain))

    sums_shift = sums_shift.sum(axis=0, keepdims=True)
    sums_gain = sums_gain.sum(axis=0, keepdims=True)
    row = lax.broadcasted_iota(jnp.int32, (8, channels), 0)
    packed = jnp.zeros((8, channels), jnp.float32)
    for index, value in enumerate(
        (sums_shift, sums_gain, gain * sums_shift, gain * sums_gain, inv_std)
    ):
        packed = jnp.where(row == index, value, packed)
    for slot in range(sums.shape[0]):
        sums[slot] = packed

    all_rows = (out_rows * out_cols, channels)
    total = None
    for frame in range(frames):
        cots = jnp.concatenate(
            [
                (cot[frame + later] if frame + later < frames else halo[frame + later - frames])
                .reshape(all_rows)
                for later in range(3)
            ],
            axis=1,
        )
        term = dot(act[frame].reshape(all_rows).T, cots)
        total = term if total is None else total + term
    for later in range(3):
        block = total[:, later * channels : (later + 1) * channels] * loss_scale
        temporal[pl.ds(later * channels, channels)] = block.astype(jnp.bfloat16)


def split_rows(values, rows):
    pieces = []
    for value in values:
        rest = value
        for _ in range(3):
            piece = rest.astype(jnp.bfloat16).astype(jnp.float32)
            pieces.append(piece)
            rest = rest - piece
    row = lax.broadcasted_iota(jnp.int32, (rows, values[0].shape[-1]), 0)
    packed = jnp.zeros((rows, values[0].shape[-1]), jnp.float32)
    for index, piece in enumerate(pieces):
        packed = jnp.where(row == index, piece, packed)
    return packed.astype(jnp.bfloat16)


def join_rows(packed, count):
    return [
        packed[3 * i : 3 * i + 1] + packed[3 * i + 1 : 3 * i + 2] + packed[3 * i + 2 : 3 * i + 3]
        for i in range(count)
    ]


def store_rows(chunks, rows, first, values):
    done = 0
    while done < values.shape[0]:
        chunk, at = divmod(first + done, rows)
        count = min(rows - at, values.shape[0] - done)
        chunks[chunk, pl.ds(at, count)] = values[done : done + count]
        done += count


def grad_kernel(
    odd, even, normed, pre, sums, temporal, grads
):
    frames, out_rows, out_cols, channels = normed.shape
    lanes = channels // GROUPS
    members = sums.shape[0] * frames * out_rows * out_cols * lanes
    clip = jnp.sum(sums[...], axis=0)
    inv_std = sums[0, 4:5]
    group = group_spread(clip, lanes) * inv_std / members
    group_shift, group_gain = group[2:3], group[3:4]
    flat = (out_rows * out_cols, channels)
    flat_wide = (out_rows * out_cols, 3 * channels)
    rows = grads.shape[1] - EXTRA
    parts = [None, None, None]
    for frame in range(frames):
        back = (
            pre[frame].reshape(flat) - group_shift - normed[frame].reshape(flat) * group_gain
        )
        back = back.astype(jnp.bfloat16).T
        for tap, source in enumerate(
            (odd.at[frame, pl.ds(0, out_rows)], even.at[frame], odd.at[frame, pl.ds(1, out_rows)])
        ):
            term = dot(back, source[...].reshape(flat_wide))
            parts[tap] = term if parts[tap] is None else parts[tap] + term
    for tap in range(3):
        for side in range(3):
            block = parts[tap][:, side * channels : (side + 1) * channels].T
            store_rows(grads, rows, (3 * tap + side) * channels, block.astype(jnp.bfloat16))
    for tap in range(3):
        block = temporal[pl.ds(tap * channels, channels)]
        store_rows(grads, rows, (9 + tap) * channels, block)
    rest = grads.shape[0] * rows - 12 * channels
    if rest:
        store_rows(grads, rows, 12 * channels, jnp.zeros((rest, channels), jnp.bfloat16))
    share = clip * (1.0 / sums.shape[0])
    extra = split_rows([share[1:2], share[0:1]], EXTRA)
    for chunk in range(grads.shape[0]):
        grads[chunk, pl.ds(rows, EXTRA)] = extra


def total_of(arrived, first, count):
    total = arrived[0, pl.ds(first, count)].astype(jnp.float32)
    for chunk in range(1, arrived.shape[0]):
        total += arrived[chunk, pl.ds(first, count)].astype(jnp.float32)
    return total


def half_kernel(arrived, chunk):
    count = chunk.shape[0] - EXTRA
    chunk[pl.ds(0, count)] = total_of(arrived, 0, count).astype(jnp.bfloat16)
    sums = join_rows(total_of(arrived, count, EXTRA), 2)
    chunk[pl.ds(count, EXTRA)] = split_rows(sums, EXTRA)


def sum_kernel(mine, other, spread, grad_gain, grad_shift):
    count = spread.shape[1]
    wide = [source[...].astype(jnp.float32) for source in (mine, other)]
    total = (wide[0][:count] + wide[1][:count]).astype(jnp.bfloat16)
    for slot in range(spread.shape[0]):
        spread[slot] = total
    sums = [join_rows(source[count:], 2) for source in wide]
    grad_gain[...] = sums[0][0] + sums[1][0]
    grad_shift[...] = sums[0][1] + sums[1][1]


def final_kernel(arrived, grad_spatial, grad_temporal):
    rows = grad_spatial.shape[0]
    grad_spatial[...] = arrived[pl.ds(0, rows)].astype(jnp.float32)
    grad_temporal[...] = arrived[pl.ds(rows, grad_temporal.shape[0])].astype(jnp.float32)


def encode_kernel(per_clip, act, halo, weights, encoded):
    frames, out_rows, out_cols, channels = act.shape
    not_first = lax.rem(lax.axis_index("seq"), per_clip) != 0
    flat = (STEP_ROWS * out_cols, channels)
    for frame in range(frames):

        def one(step, frame=frame):
            rows = pl.ds(step * STEP_ROWS, STEP_ROWS)
            total = None
            for tap in range(3):
                if frame >= tap:
                    source = act[frame - tap, rows]
                else:
                    source = halo[frames + frame - tap, rows]
                    source = jnp.where(not_first, source, jnp.zeros_like(source))
                term = dot(source.reshape(flat), weights[tap])
                total = term if total is None else total + term
            encoded[frame, rows] = total.astype(jnp.bfloat16).reshape(
                STEP_ROWS, out_cols, channels
            )

        each(out_rows // STEP_ROWS, one)


def on_device(video_in, w_spatial, w_temporal, norm_gain, norm_shift, cotangent):
    frames, height, width, channels = video_in.shape[1:]
    out_rows, out_cols = height // 2, width // 2
    dp_size, seq_size = lax.axis_size("dp"), lax.axis_size("seq")
    devices = dp_size * seq_size
    per_clip = FRAMES // frames
    assert frames >= 2 and FRAMES % frames == 0
    loss_scale = float(devices * frames * out_rows * out_cols) ** (-0.5)
    shape = (frames, out_rows, out_cols, channels)
    positions = frames * out_rows * out_cols
    video = video_in[0]
    cot = cotangent[0]
    f32, bf16 = jnp.float32, jnp.bfloat16
    struct = jax.ShapeDtypeStruct

    ahead_pairs = [
        (s, s // per_clip * per_clip + (s + 1) % per_clip) for s in range(seq_size)
    ]
    back_pairs = [(target, source) for source, target in ahead_pairs]
    clips = [list(range(first, first + per_clip)) for first in range(0, seq_size, per_clip)]

    def exchange(value, axes, groups=None):
        return lax.all_to_all(value, axes, 0, 0, axis_index_groups=groups, tiled=True)

    gate = pl.pallas_call(
        open_kernel,
        out_shape=pltpu.VMEM((8, channels), f32),
        out_specs=WHOLE,
        cost_estimate=pl.CostEstimate(
            flops=2 * positions * 9 * channels * channels,
            bytes_accessed=2 * video.size,
            transcendentals=0,
        ),
    )()
    cot_out, gate = lax.optimization_barrier((cot, gate))
    cot_halo = lax.ppermute(cot_out, "seq", back_pairs)

    pieces = 2 * frames
    def far(value):
        return pltpu.with_memory_space_constraint(value, pltpu.HBM)

    spatial, stats, odd, even, params = call(
        functools.partial(conv_kernel, pieces),
        (
            struct(shape, f32),
            struct((per_clip, 8, channels), f32),
            struct((frames, out_rows + 1, out_cols, 3 * channels), bf16),
            struct((frames, out_rows, out_cols, 3 * channels), bf16),
            struct((8, channels), f32),
        ),
        (
            gate,
            video,
            far(w_spatial.reshape(3, 3 * channels, channels)),
            far(norm_gain[None]),
            far(norm_shift[None]),
        ),
        specs=[WHOLE] * 2 + [FAR] * 3,
        scratch=[
            pltpu.VMEM((4 * STEP_ROWS, 8 + width, channels), f32),
            pltpu.VMEM((3, 3 * channels, channels), bf16),
            pltpu.SemaphoreType.DMA((3,)),
        ],
        flops=2 * positions * 9 * channels * channels,
    )
    stats = exchange(stats, "seq", clips)
    act, normed, slope, scales = call(
        functools.partial(act_kernel, loss_scale),
        (
            struct(shape, bf16),
            struct(shape, f32),
            struct(shape, f32),
            struct((8, channels), f32),
        ),
        (spatial, stats, params),
    )
    act_halo = lax.ppermute(act, "seq", ahead_pairs)
    pre, temporal, own = call(
        functools.partial(back_kernel, loss_scale),
        (
            struct(shape, f32),
            struct((3 * channels, channels), bf16),
            struct((per_clip, 8, channels), f32),
        ),
        (cot, cot_halo, w_temporal, scales, normed, slope, act),
        scratch=[pltpu.VMEM((2,) + shape[1:], bf16)],
        flops=2 * positions * 6 * channels * channels,
    )
    sums = exchange(own, "seq", clips)
    halves = 2 if seq_size % 2 == 0 else 1
    half = seq_size // halves
    near = [
        [d * seq_size + s for d in range(dp_size) for s in range(first, first + half)]
        for first in range(0, seq_size, half)
    ]
    count = dp_size * half
    rows = -(-12 * channels // (16 * count)) * 16
    sums, act_halo = lax.optimization_barrier((sums, act_halo))
    grads = call(
        grad_kernel,
        struct((count, rows + EXTRA, channels), bf16),
        (odd, even, normed, pre, sums, temporal),
        flops=2 * positions * 9 * channels * channels,
    )
    grads = exchange(grads, ("dp", "seq"), near)
    mine = call(half_kernel, struct((rows + EXTRA, channels), bf16), (grads,))
    if halves == 2:
        other = lax.ppermute(mine, "seq", [(s, (s + half) % seq_size) for s in range(seq_size)])
    else:
        other = jnp.zeros_like(mine)
    act, act_halo, _ = lax.optimization_barrier((act, act_halo, mine))
    encoded = call(
        functools.partial(encode_kernel, per_clip),
        struct(shape, bf16),
        (act, act_halo, w_temporal),
        flops=2 * positions * 3 * channels * channels,
    )
    other, encoded = lax.optimization_barrier((other, encoded))
    grads, grad_gain, grad_shift = call(
        sum_kernel,
        (
            struct((count, rows, channels), bf16),
            struct((1, channels), f32),
            struct((1, channels), f32),
        ),
        (mine, other),
    )
    grads = exchange(grads, ("dp", "seq"), near)
    grad_spatial, grad_temporal = call(
        final_kernel,
        (struct((9 * channels, channels), f32), struct((3 * channels, channels), f32)),
        (grads.reshape(count * rows, channels),),
    )
    return (
        encoded[None],
        grad_spatial.reshape(3, 3, channels, channels),
        grad_temporal.reshape(3, channels, channels),
        grad_gain[0],
        grad_shift[0],
    )


def solution(mesh):
    placed = P("dp", "seq", None, None, None)
    return jax.shard_map(
        on_device,
        mesh=mesh,
        in_specs=(placed, P(), P(), P(), P(), placed),
        out_specs=(placed, P(), P(), P(), P()),
        check_vma=False,
    )
```

```python
import functools
import math

import jax
import jax.numpy as jnp
from jax import lax
from jax.experimental import pallas as pl
from jax.experimental.pallas import tpu as pltpu
from jax.sharding import PartitionSpec as P

GROUPS = 32
FRAMES = 8
STEP_ROWS = 8
EXTRA = 8
SPARE_BYTES = 4 * 1024 * 1024

WHOLE = pl.BlockSpec(memory_space=pltpu.VMEM)
FAR = pl.BlockSpec(memory_space=pltpu.HBM)


def dot(left, right):
    return jnp.dot(left, right, preferred_element_type=jnp.float32)


def dot_transposed(left, right):
    return lax.dot_general(
        left, right, (((1,), (1,)), ((), ())), preferred_element_type=jnp.float32
    )


def each(count, body):
    if count <= 8:
        for step in range(count):
            body(step)
    else:
        lax.fori_loop(0, count, lambda step, carry: (body(step), carry)[1], 0)


def call(kernel, out_shape, operands, specs=None, scratch=(), flops=0):
    sizes = [value.size * value.dtype.itemsize for value in operands]
    sizes += [value.size * value.dtype.itemsize for value in jax.tree.leaves(out_shape)]
    held = sum(math.prod(item.shape) * 4 for item in scratch if hasattr(item, "shape"))
    return pl.pallas_call(
        kernel,
        out_shape=out_shape,
        in_specs=specs or [WHOLE] * len(operands),
        out_specs=jax.tree.map(lambda _: WHOLE, out_shape),
        scratch_shapes=list(scratch),
        compiler_params=pltpu.CompilerParams(vmem_limit_bytes=sum(sizes) + held + SPARE_BYTES),
        cost_estimate=pl.CostEstimate(
            flops=flops, bytes_accessed=sum(sizes), transcendentals=0
        ),
    )(*operands)


def group_spread(values, lanes):
    channels = values.shape[-1]
    shift = 1
    while shift < lanes:
        values = values + pltpu.roll(values, channels - shift, 1)
        shift *= 2
    lane = lax.broadcasted_iota(jnp.int32, values.shape, 1)
    values = jnp.where(lax.rem(lane, lanes) == 0, values, 0.0)
    shift = 1
    while shift < lanes:
        values = values + pltpu.roll(values, shift, 1)
        shift *= 2
    return values


def open_kernel(gate):
    gate[...] = jnp.zeros(gate.shape, gate.dtype)


def conv_kernel(
    pieces, blank, video, weights_far, gain_far, shift_far, spatial, stats, odd, even, params, wide,
    weights, arrived,
):
    frames, height, width, channels = video.shape
    out_rows, out_cols = height // 2, width // 2
    positions = frames * out_rows * out_cols
    half = height * frames // pieces
    params[...] = blank[...]
    copies = [
        pltpu.make_async_copy(source, target, arrived.at[index])
        for index, (source, target) in enumerate(
            ((weights_far, weights), (gain_far, params.at[0:1]), (shift_far, params.at[1:2]))
        )
    ]
    for copy in copies:
        copy.start()
    for slot in range(wide.shape[0]):
        wide[slot, 0:8] = jnp.zeros((8, channels), jnp.float32)
    for frame in range(frames):
        odd[frame, 0] = jnp.zeros((out_cols, 3 * channels), jnp.bfloat16)
    flat = (STEP_ROWS * out_cols, 3 * channels)
    steps = half // 2 // STEP_ROWS

    def place(piece, step):
        return piece * half // height, piece * half % height // 2 + step * STEP_ROWS

    def separate(piece, step):
        frame, first = place(piece, step)
        base = piece % 2 * 2 * STEP_ROWS
        for line in range(2 * STEP_ROWS):
            wide[base + line, 8 : 8 + width] = video[frame, 2 * first + line].astype(jnp.float32)
        for line in range(2 * STEP_ROWS):
            for tap in range(3):
                value = wide[base + line, pl.ds(7 + tap, out_cols, stride=2), :]
                lanes = slice(tap * channels, (tap + 1) * channels)
                if line % 2:
                    odd[frame, first + line // 2 + 1, :, lanes] = value.astype(jnp.bfloat16)
                else:
                    even[frame, first + line // 2, :, lanes] = value.astype(jnp.bfloat16)

    def multiply(piece, step):
        frame, first = place(piece, step)
        total = dot(odd[frame, pl.ds(first, STEP_ROWS)].reshape(flat), weights[0])
        total += dot(even[frame, pl.ds(first, STEP_ROWS)].reshape(flat), weights[1])
        total += dot(odd[frame, pl.ds(first + 1, STEP_ROWS)].reshape(flat), weights[2])
        spatial[frame, pl.ds(first, STEP_ROWS)] = total.reshape(STEP_ROWS, out_cols, channels)
        return total

    def fold(values):
        return values.reshape(-1, 8, channels).sum(axis=0)

    def over_steps(piece, term, start):
        if steps <= 8:
            for step in range(steps):
                start = jax.tree.map(jnp.add, start, term(piece, step))
            return start
        return lax.fori_loop(
            0, steps, lambda step, sums: jax.tree.map(jnp.add, sums, term(piece, step)), start
        )

    zero = jnp.zeros((8, channels), jnp.float32)

    def first_sum(piece, step):
        return fold(multiply(piece, step))

    def first_moments(piece, step):
        frame, first = place(piece, step)
        off = spatial[frame, pl.ds(first, STEP_ROWS)].reshape(-1, channels) - near
        return fold(off), fold(off * off)

    def moments(piece, step):
        off = multiply(piece, step) - near
        return fold(off), fold(off * off)

    for piece in range(pieces):
        each(steps, functools.partial(separate, piece))
    copies[0].wait()
    near = over_steps(0, first_sum, zero).sum(axis=0, keepdims=True) * (pieces / positions)
    sums = over_steps(0, first_moments, (zero, zero))
    for piece in range(1, pieces - 1):
        sums = over_steps(piece, moments, sums)
    sums = over_steps(pieces - 1, moments, sums)
    off = sums[0].sum(axis=0, keepdims=True) / positions
    mean = near + off
    square = sums[1].sum(axis=0, keepdims=True) - positions * off * off
    row = lax.broadcasted_iota(jnp.int32, (8, channels), 0)
    packed = jnp.where(row == 0, mean, jnp.where(row == 1, square, 0.0))
    for slot in range(stats.shape[0]):
        stats[slot] = packed
    for copy in copies[1:]:
        copy.wait()

def clip_norm(stats, positions, lanes):
    cells = stats.shape[0] * lanes
    means = [stats[member, 0:1] for member in range(stats.shape[0])]
    squares = [stats[member, 1:2] for member in range(stats.shape[0])]
    mean = group_spread(jnp.broadcast_to(sum(means), (8, means[0].shape[-1])), lanes)[0:1] / cells
    square = sum(squares)
    for value in means:
        square = square + positions * (value - mean) ** 2
    square = group_spread(jnp.broadcast_to(square, (8, square.shape[-1])), lanes)[0:1]
    return mean, lax.rsqrt(square / (cells * positions) + 1e-05)


def act_kernel(loss_scale, spatial, stats, params, act, normed, slope, scales):
    frames, out_rows, out_cols, channels = spatial.shape
    positions = frames * out_rows * out_cols
    mean, inv_std = clip_norm(stats, positions, channels // GROUPS)
    gain, shift = params[0:1], params[1:2]
    row = lax.broadcasted_iota(jnp.int32, (8, channels), 0)
    scales[...] = jnp.where(row == 0, inv_std, gain)
    flat = (STEP_ROWS * out_cols, channels)
    shaped = (STEP_ROWS, out_cols, channels)
    for frame in range(frames):

        def one(step, frame=frame):
            rows = pl.ds(step * STEP_ROWS, STEP_ROWS)
            norm = (spatial[frame, rows].reshape(flat) - mean) * inv_std
            before = norm * gain + shift
            sig = 0.5 + 0.5 * jnp.tanh(0.5 * before)
            act[frame, rows] = (before * sig).astype(jnp.bfloat16).reshape(shaped)
            normed[frame, rows] = norm.reshape(shaped)
            slope[frame, rows] = (loss_scale * sig * (1.0 + before * (1.0 - sig))).reshape(shaped)

        each(out_rows // STEP_ROWS, one)


def back_kernel(
    loss_scale, cot, arrived, weights, scales, normed, slope, act, pre, temporal, sums, halo
):
    frames, out_rows, out_cols, channels = cot.shape
    inv_std, gain = scales[0:1], scales[1:2]
    per_clip = sums.shape[0]
    not_last = lax.rem(lax.axis_index("seq"), per_clip) != per_clip - 1
    for frame in range(2):
        value = arrived[frame]
        halo[frame] = jnp.where(not_last, value, jnp.zeros_like(value))
    turned_weights = jnp.concatenate([weights[tap] for tap in range(3)], axis=1)
    flat = (STEP_ROWS * out_cols, channels)
    shaped = (STEP_ROWS, out_cols, channels)
    sums_shift = jnp.zeros((8, channels), jnp.float32)
    sums_gain = jnp.zeros((8, channels), jnp.float32)

    def fold(values):
        return values.reshape(-1, 8, channels).sum(axis=0)

    for frame in range(frames):

        def cot_block(later, rows, shape, frame=frame):
            if frame + later < frames:
                return cot[frame + later, rows].reshape(shape)
            return halo[frame + later - frames, rows].reshape(shape)

        def one(step, carry, frame=frame):
            rows = pl.ds(step * STEP_ROWS, STEP_ROWS)
            cots = jnp.concatenate([cot_block(later, rows, flat) for later in range(3)], axis=1)
            back = dot_transposed(cots, turned_weights)
            back = back.astype(jnp.bfloat16).astype(jnp.float32)
            back_pre = back * slope[frame, rows].reshape(flat)
            norm = normed[frame, rows].reshape(flat)
            pre[frame, rows] = (back_pre * (gain * inv_std)).reshape(shaped)
            return (carry[0] + fold(back_pre), carry[1] + fold(back_pre * norm))

        steps = out_rows // STEP_ROWS
        if steps <= 4:
            for step in range(steps):
                sums_shift, sums_gain = one(step, (sums_shift, sums_gain))
        else:
            sums_shift, sums_gain = lax.fori_loop(0, steps, one, (sums_shift, sums_gain))

    sums_shift = sums_shift.sum(axis=0, keepdims=True)
    sums_gain = sums_gain.sum(axis=0, keepdims=True)
    row = lax.broadcasted_iota(jnp.int32, (8, channels), 0)
    packed = jnp.zeros((8, channels), jnp.float32)
    for index, value in enumerate(
        (sums_shift, sums_gain, gain * sums_shift, gain * sums_gain, inv_std)
    ):
        packed = jnp.where(row == index, value, packed)
    for slot in range(sums.shape[0]):
        sums[slot] = packed

    all_rows = (out_rows * out_cols, channels)
    total = None
    for frame in range(frames):
        cots = jnp.concatenate(
            [
                (cot[frame + later] if frame + later < frames else halo[frame + later - frames])
                .reshape(all_rows)
                for later in range(3)
            ],
            axis=1,
        )
        term = dot(act[frame].reshape(all_rows).T, cots)
        total = term if total is None else total + term
    for later in range(3):
        block = total[:, later * channels : (later + 1) * channels] * loss_scale
        temporal[pl.ds(later * channels, channels)] = block.astype(jnp.bfloat16)


def split_rows(values, rows):
    pieces = []
    for value in values:
        rest = value
        for _ in range(3):
            piece = rest.astype(jnp.bfloat16).astype(jnp.float32)
            pieces.append(piece)
            rest = rest - piece
    row = lax.broadcasted_iota(jnp.int32, (rows, values[0].shape[-1]), 0)
    packed = jnp.zeros((rows, values[0].shape[-1]), jnp.float32)
    for index, piece in enumerate(pieces):
        packed = jnp.where(row == index, piece, packed)
    return packed.astype(jnp.bfloat16)


def join_rows(packed, count):
    return [
        packed[3 * i : 3 * i + 1] + packed[3 * i + 1 : 3 * i + 2] + packed[3 * i + 2 : 3 * i + 3]
        for i in range(count)
    ]


def store_rows(chunks, rows, first, values):
    done = 0
    while done < values.shape[0]:
        chunk, at = divmod(first + done, rows)
        count = min(rows - at, values.shape[0] - done)
        chunks[chunk, pl.ds(at, count)] = values[done : done + count]
        done += count


def grad_kernel(
    odd, even, normed, pre, sums, temporal, grads
):
    frames, out_rows, out_cols, channels = normed.shape
    lanes = channels // GROUPS
    members = sums.shape[0] * frames * out_rows * out_cols * lanes
    clip = jnp.sum(sums[...], axis=0)
    inv_std = sums[0, 4:5]
    group = group_spread(clip, lanes) * inv_std / members
    group_shift, group_gain = group[2:3], group[3:4]
    flat = (out_rows * out_cols, channels)
    flat_wide = (out_rows * out_cols, 3 * channels)
    rows = grads.shape[1] - EXTRA
    parts = [None, None, None]
    for frame in range(frames):
        back = (
            pre[frame].reshape(flat) - group_shift - normed[frame].reshape(flat) * group_gain
        )
        back = back.astype(jnp.bfloat16).T
        for tap, source in enumerate(
            (odd.at[frame, pl.ds(0, out_rows)], even.at[frame], odd.at[frame, pl.ds(1, out_rows)])
        ):
            term = dot(back, source[...].reshape(flat_wide))
            parts[tap] = term if parts[tap] is None else parts[tap] + term
    for tap in range(3):
        for side in range(3):
            block = parts[tap][:, side * channels : (side + 1) * channels].astype(jnp.bfloat16).T
            store_rows(grads, rows, (3 * tap + side) * channels, block)
    for tap in range(3):
        block = temporal[pl.ds(tap * channels, channels)]
        store_rows(grads, rows, (9 + tap) * channels, block)
    rest = grads.shape[0] * rows - 12 * channels
    if rest:
        store_rows(grads, rows, 12 * channels, jnp.zeros((rest, channels), jnp.bfloat16))
    share = clip * (1.0 / sums.shape[0])
    extra = split_rows([share[1:2], share[0:1]], EXTRA)
    for chunk in range(grads.shape[0]):
        grads[chunk, pl.ds(rows, EXTRA)] = extra


def total_of(arrived, first, count):
    total = arrived[0, pl.ds(first, count)].astype(jnp.float32)
    for chunk in range(1, arrived.shape[0]):
        total += arrived[chunk, pl.ds(first, count)].astype(jnp.float32)
    return total


def half_kernel(arrived, chunk):
    count = chunk.shape[0] - EXTRA
    chunk[pl.ds(0, count)] = total_of(arrived, 0, count).astype(jnp.bfloat16)
    sums = join_rows(total_of(arrived, count, EXTRA), 2)
    chunk[pl.ds(count, EXTRA)] = split_rows(sums, EXTRA)


def sum_kernel(mine, other, spread, totals):
    count = spread.shape[1]
    wide = [source[...].astype(jnp.float32) for source in (mine, other)]
    total = (wide[0][:count] + wide[1][:count]).astype(jnp.bfloat16)
    for slot in range(spread.shape[0]):
        spread[slot] = total
    sums = [join_rows(source[count:], 2) for source in wide]
    row = lax.broadcasted_iota(jnp.int32, totals.shape, 0)
    totals[...] = jnp.where(row == 0, sums[0][0] + sums[1][0], sums[0][1] + sums[1][1])


def final_kernel(arrived, totals, grad_spatial, grad_temporal, grad_gain, grad_shift):
    grad_gain[...] = totals[0:1]
    grad_shift[...] = totals[1:2]
    rows = grad_spatial.shape[0]
    grad_spatial[...] = arrived[pl.ds(0, rows)].astype(jnp.float32)
    grad_temporal[...] = arrived[pl.ds(rows, grad_temporal.shape[0])].astype(jnp.float32)


def encode_kernel(per_clip, act, halo, weights, encoded):
    frames, out_rows, out_cols, channels = act.shape
    not_first = lax.rem(lax.axis_index("seq"), per_clip) != 0
    flat = (STEP_ROWS * out_cols, channels)
    for frame in range(frames):

        def one(step, frame=frame):
            rows = pl.ds(step * STEP_ROWS, STEP_ROWS)
            total = None
            for tap in range(3):
                if frame >= tap:
                    source = act[frame - tap, rows]
                else:
                    source = halo[frames + frame - tap, rows]
                    source = jnp.where(not_first, source, jnp.zeros_like(source))
                term = dot(source.reshape(flat), weights[tap])
                total = term if total is None else total + term
            encoded[frame, rows] = total.astype(jnp.bfloat16).reshape(
                STEP_ROWS, out_cols, channels
            )

        each(out_rows // STEP_ROWS, one)


def on_device(video_in, w_spatial, w_temporal, norm_gain, norm_shift, cotangent):
    frames, height, width, channels = video_in.shape[1:]
    out_rows, out_cols = height // 2, width // 2
    dp_size, seq_size = lax.axis_size("dp"), lax.axis_size("seq")
    devices = dp_size * seq_size
    per_clip = FRAMES // frames
    assert frames >= 2 and FRAMES % frames == 0
    loss_scale = float(devices * frames * out_rows * out_cols) ** (-0.5)
    shape = (frames, out_rows, out_cols, channels)
    positions = frames * out_rows * out_cols
    video = video_in[0]
    cot = cotangent[0]
    f32, bf16 = jnp.float32, jnp.bfloat16
    struct = jax.ShapeDtypeStruct

    ahead_pairs = [
        (s, s // per_clip * per_clip + (s + 1) % per_clip) for s in range(seq_size)
    ]
    back_pairs = [(target, source) for source, target in ahead_pairs]
    clips = [list(range(first, first + per_clip)) for first in range(0, seq_size, per_clip)]

    def exchange(value, axes, groups=None):
        return lax.all_to_all(value, axes, 0, 0, axis_index_groups=groups, tiled=True)

    gate = pl.pallas_call(
        open_kernel,
        out_shape=pltpu.VMEM((8, channels), f32),
        out_specs=WHOLE,
        cost_estimate=pl.CostEstimate(
            flops=2 * positions * 9 * channels * channels,
            bytes_accessed=2 * video.size,
            transcendentals=0,
        ),
    )()
    cot_out, gate = lax.optimization_barrier((cot, gate))
    cot_halo = lax.ppermute(cot_out, "seq", back_pairs)

    pieces = 2 * frames
    def far(value):
        return pltpu.with_memory_space_constraint(value, pltpu.HBM)

    spatial, stats, odd, even, params = call(
        functools.partial(conv_kernel, pieces),
        (
            struct(shape, f32),
            struct((per_clip, 8, channels), f32),
            struct((frames, out_rows + 1, out_cols, 3 * channels), bf16),
            struct((frames, out_rows, out_cols, 3 * channels), bf16),
            struct((8, channels), f32),
        ),
        (
            gate,
            video,
            far(w_spatial.reshape(3, 3 * channels, channels)),
            far(norm_gain[None]),
            far(norm_shift[None]),
        ),
        specs=[WHOLE] * 2 + [FAR] * 3,
        scratch=[
            pltpu.VMEM((4 * STEP_ROWS, 8 + width, channels), f32),
            pltpu.VMEM((3, 3 * channels, channels), bf16),
            pltpu.SemaphoreType.DMA((3,)),
        ],
        flops=2 * positions * 9 * channels * channels,
    )
    stats = exchange(stats, "seq", clips)
    act, normed, slope, scales = call(
        functools.partial(act_kernel, loss_scale),
        (
            struct(shape, bf16),
            struct(shape, f32),
            struct(shape, f32),
            struct((8, channels), f32),
        ),
        (spatial, stats, params),
    )
    act_halo = lax.ppermute(act, "seq", ahead_pairs)
    pre, temporal, own = call(
        functools.partial(back_kernel, loss_scale),
        (
            struct(shape, f32),
            struct((3 * channels, channels), bf16),
            struct((per_clip, 8, channels), f32),
        ),
        (cot, cot_halo, w_temporal, scales, normed, slope, act),
        scratch=[pltpu.VMEM((2,) + shape[1:], bf16)],
        flops=2 * positions * 6 * channels * channels,
    )
    sums = exchange(own, "seq", clips)
    halves = 2 if seq_size % 2 == 0 else 1
    half = seq_size // halves
    near = [
        [d * seq_size + s for d in range(dp_size) for s in range(first, first + half)]
        for first in range(0, seq_size, half)
    ]
    count = dp_size * half
    rows = -(-12 * channels // (16 * count)) * 16
    sums, act_halo = lax.optimization_barrier((sums, act_halo))
    grads = call(
        grad_kernel,
        struct((count, rows + EXTRA, channels), bf16),
        (odd, even, normed, pre, sums, temporal),
        flops=2 * positions * 9 * channels * channels,
    )
    grads = exchange(grads, ("dp", "seq"), near)
    mine = call(half_kernel, struct((rows + EXTRA, channels), bf16), (grads,))
    if halves == 2:
        other = lax.ppermute(mine, "seq", [(s, (s + half) % seq_size) for s in range(seq_size)])
    else:
        other = jnp.zeros_like(mine)
    act, act_halo, _ = lax.optimization_barrier((act, act_halo, mine))
    encoded = call(
        functools.partial(encode_kernel, per_clip),
        struct(shape, bf16),
        (act, act_halo, w_temporal),
        flops=2 * positions * 3 * channels * channels,
    )
    other, encoded = lax.optimization_barrier((other, encoded))
    grads, totals = call(
        sum_kernel,
        (struct((count, rows, channels), bf16), struct((8, channels), f32)),
        (mine, other),
    )
    grads = exchange(grads, ("dp", "seq"), near)
    grad_spatial, grad_temporal, grad_gain, grad_shift = call(
        final_kernel,
        (
            struct((9 * channels, channels), f32),
            struct((3 * channels, channels), f32),
            struct((1, channels), f32),
            struct((1, channels), f32),
        ),
        (grads.reshape(count * rows, channels), totals),
    )
    return (
        encoded[None],
        grad_spatial.reshape(3, 3, channels, channels),
        grad_temporal.reshape(3, channels, channels),
        grad_gain[0],
        grad_shift[0],
    )


def solution(mesh):
    placed = P("dp", "seq", None, None, None)
    return jax.shard_map(
        on_device,
        mesh=mesh,
        in_specs=(placed, P(), P(), P(), P(), placed),
        out_specs=(placed, P(), P(), P(), P()),
        check_vma=False,
    )
```

```python
import functools
import math

import jax
import jax.numpy as jnp
from jax import lax
from jax.experimental import pallas as pl
from jax.experimental.pallas import tpu as pltpu
from jax.sharding import PartitionSpec as P

GROUPS = 32
FRAMES = 8
STEP_ROWS = 8
EXTRA = 8
SPARE_BYTES = 4 * 1024 * 1024

WHOLE = pl.BlockSpec(memory_space=pltpu.VMEM)
FAR = pl.BlockSpec(memory_space=pltpu.HBM)


def dot(left, right):
    return jnp.dot(left, right, preferred_element_type=jnp.float32)


def dot_transposed(left, right):
    return lax.dot_general(
        left, right, (((1,), (1,)), ((), ())), preferred_element_type=jnp.float32
    )


def each(count, body):
    if count <= 8:
        for step in range(count):
            body(step)
    else:
        lax.fori_loop(0, count, lambda step, carry: (body(step), carry)[1], 0)


def call(kernel, out_shape, operands, specs=None, scratch=(), flops=0, outs=WHOLE):
    sizes = [value.size * value.dtype.itemsize for value in operands]
    sizes += [value.size * value.dtype.itemsize for value in jax.tree.leaves(out_shape)]
    held = sum(math.prod(item.shape) * 4 for item in scratch if hasattr(item, "shape"))
    return pl.pallas_call(
        kernel,
        out_shape=out_shape,
        in_specs=specs or [WHOLE] * len(operands),
        out_specs=jax.tree.map(lambda _: outs, out_shape),
        scratch_shapes=list(scratch),
        compiler_params=pltpu.CompilerParams(vmem_limit_bytes=sum(sizes) + held + SPARE_BYTES),
        cost_estimate=pl.CostEstimate(
            flops=flops, bytes_accessed=sum(sizes), transcendentals=0
        ),
    )(*operands)


def group_spread(values, lanes):
    channels = values.shape[-1]
    place = lax.rem(lax.broadcasted_iota(jnp.int32, values.shape, 1), lanes)
    total = values
    for shift in range(1, lanes):
        ahead = pltpu.roll(values, channels - shift, 1)
        behind = pltpu.roll(values, shift, 1)
        total += jnp.where(place < lanes - shift, ahead, 0.0)
        total += jnp.where(place >= shift, behind, 0.0)
    return total


def open_kernel(gate):
    gate[...] = jnp.zeros(gate.shape, gate.dtype)


def conv_kernel(
    pieces, blank, video, weights_far, gain_far, shift_far, spatial, stats, patches, params, wide,
    weights, arrived,
):
    frames, height, width, channels = video.shape
    out_rows, out_cols = height // 2, width // 2
    positions = frames * out_rows * out_cols
    half = height * frames // pieces
    params[...] = blank[...]
    copies = [
        pltpu.make_async_copy(source, target, arrived.at[index])
        for index, (source, target) in enumerate(
            ((weights_far, weights), (gain_far, params.at[0:1]), (shift_far, params.at[1:2]))
        )
    ]
    for copy in copies:
        copy.start()
    for slot in range(wide.shape[0]):
        wide[slot, 0:8] = jnp.zeros((8, channels), jnp.float32)
    for frame in range(frames):
        patches[frame, 0, :, 0 : 3 * channels] = jnp.zeros(
            (out_cols, 3 * channels), jnp.bfloat16
        )
    flat = (STEP_ROWS * out_cols, 9 * channels)
    steps = half // 2 // STEP_ROWS

    def place(piece, step):
        return piece * half // height, piece * half % height // 2 + step * STEP_ROWS

    def separate(piece, step):
        frame, first = place(piece, step)
        base = piece % 2 * 2 * STEP_ROWS
        for line in range(2 * STEP_ROWS):
            wide[base + line, 8 : 8 + width] = video[frame, 2 * first + line].astype(jnp.float32)
        for line in range(2 * STEP_ROWS):
            row = first + line // 2

            def put(row, block, value):
                patches[frame, row, :, block * channels : (block + 1) * channels] = value

            for tap in range(3):
                value = wide[base + line, pl.ds(7 + tap, out_cols, stride=2), :]
                value = value.astype(jnp.bfloat16)
                if line % 2 == 0:
                    put(row, 3 + tap, value)
                    continue
                put(row, 6 + tap, value)
                if not isinstance(row, int):
                    pl.when(row + 1 < out_rows)(functools.partial(put, row + 1, tap, value))
                elif row + 1 < out_rows:
                    put(row + 1, tap, value)

    def multiply(piece, step):
        frame, first = place(piece, step)
        total = dot(patches[frame, pl.ds(first, STEP_ROWS)].reshape(flat), weights[...])
        spatial[frame, pl.ds(first, STEP_ROWS)] = total.reshape(STEP_ROWS, out_cols, channels)
        return total

    def fold(values):
        return values.reshape(-1, 8, channels).sum(axis=0)

    def over_steps(piece, term, start):
        if steps <= 8:
            for step in range(steps):
                start = jax.tree.map(jnp.add, start, term(piece, step))
            return start
        return lax.fori_loop(
            0, steps, lambda step, sums: jax.tree.map(jnp.add, sums, term(piece, step)), start
        )

    zero = jnp.zeros((8, channels), jnp.float32)

    def first_sum(piece, step):
        return fold(multiply(piece, step))

    def first_moments(piece, step):
        frame, first = place(piece, step)
        off = spatial[frame, pl.ds(first, STEP_ROWS)].reshape(-1, channels) - near
        return fold(off), fold(off * off)

    def moments(piece, step):
        off = multiply(piece, step) - near
        return fold(off), fold(off * off)

    for piece in range(pieces):
        each(steps, functools.partial(separate, piece))
    copies[0].wait()
    near = over_steps(0, first_sum, zero).sum(axis=0, keepdims=True) * (pieces / positions)
    sums = over_steps(0, first_moments, (zero, zero))
    for piece in range(1, pieces - 1):
        sums = over_steps(piece, moments, sums)
    sums = over_steps(pieces - 1, moments, sums)
    off = sums[0].sum(axis=0, keepdims=True) / positions
    mean = near + off
    square = sums[1].sum(axis=0, keepdims=True) - positions * off * off
    row = lax.broadcasted_iota(jnp.int32, (8, channels), 0)
    packed = jnp.where(row == 0, mean, jnp.where(row == 1, square, 0.0))
    for slot in range(stats.shape[0]):
        stats[slot] = packed
    for copy in copies[1:]:
        copy.wait()

def clip_norm(stats, positions, lanes):
    cells = stats.shape[0] * lanes
    means = [stats[member, 0:1] for member in range(stats.shape[0])]
    squares = [stats[member, 1:2] for member in range(stats.shape[0])]
    mean = group_spread(jnp.broadcast_to(sum(means), (8, means[0].shape[-1])), lanes)[0:1] / cells
    square = sum(squares)
    for value in means:
        square = square + positions * (value - mean) ** 2
    square = group_spread(jnp.broadcast_to(square, (8, square.shape[-1])), lanes)[0:1]
    return mean, lax.rsqrt(square / (cells * positions) + 1e-05)


def act_kernel(loss_scale, spatial, stats, params, act, normed, slope, scales):
    frames, out_rows, out_cols, channels = spatial.shape
    positions = frames * out_rows * out_cols
    mean, inv_std = clip_norm(stats, positions, channels // GROUPS)
    gain, shift = params[0:1], params[1:2]
    row = lax.broadcasted_iota(jnp.int32, (8, channels), 0)
    scales[...] = jnp.where(row == 0, inv_std, gain)
    flat = (STEP_ROWS * out_cols, channels)
    shaped = (STEP_ROWS, out_cols, channels)
    for frame in range(frames):

        def one(step, frame=frame):
            rows = pl.ds(step * STEP_ROWS, STEP_ROWS)
            norm = (spatial[frame, rows].reshape(flat) - mean) * inv_std
            before = norm * gain + shift
            sig = 0.5 + 0.5 * jnp.tanh(0.5 * before)
            act[frame, rows] = (before * sig).astype(jnp.bfloat16).reshape(shaped)
            normed[frame, rows] = norm.reshape(shaped)
            slope[frame, rows] = (loss_scale * sig * (1.0 + before * (1.0 - sig))).reshape(shaped)

        each(out_rows // STEP_ROWS, one)


def back_kernel(
    loss_scale, cot, arrived, weights, scales, normed, slope, act, pre, temporal, sums, halo
):
    frames, out_rows, out_cols, channels = cot.shape
    inv_std, gain = scales[0:1], scales[1:2]
    per_clip = sums.shape[0]
    not_last = lax.rem(lax.axis_index("seq"), per_clip) != per_clip - 1
    for frame in range(2):
        value = arrived[frame]
        halo[frame] = jnp.where(not_last, value, jnp.zeros_like(value))
    turned_weights = jnp.concatenate([weights[tap] for tap in range(3)], axis=1)
    flat = (STEP_ROWS * out_cols, channels)
    shaped = (STEP_ROWS, out_cols, channels)
    sums_shift = jnp.zeros((8, channels), jnp.float32)
    sums_gain = jnp.zeros((8, channels), jnp.float32)

    def fold(values):
        return values.reshape(-1, 8, channels).sum(axis=0)

    for frame in range(frames):

        def cot_block(later, rows, shape, frame=frame):
            if frame + later < frames:
                return cot[frame + later, rows].reshape(shape)
            return halo[frame + later - frames, rows].reshape(shape)

        def one(step, carry, frame=frame):
            rows = pl.ds(step * STEP_ROWS, STEP_ROWS)
            cots = jnp.concatenate([cot_block(later, rows, flat) for later in range(3)], axis=1)
            back = dot_transposed(cots, turned_weights)
            back = back.astype(jnp.bfloat16).astype(jnp.float32)
            back_pre = back * slope[frame, rows].reshape(flat)
            norm = normed[frame, rows].reshape(flat)
            pre[frame, rows] = (back_pre * (gain * inv_std)).reshape(shaped)
            return (carry[0] + fold(back_pre), carry[1] + fold(back_pre * norm))

        steps = out_rows // STEP_ROWS
        if steps <= 4:
            for step in range(steps):
                sums_shift, sums_gain = one(step, (sums_shift, sums_gain))
        else:
            sums_shift, sums_gain = lax.fori_loop(0, steps, one, (sums_shift, sums_gain))

    sums_shift = sums_shift.sum(axis=0, keepdims=True)
    sums_gain = sums_gain.sum(axis=0, keepdims=True)
    row = lax.broadcasted_iota(jnp.int32, (8, channels), 0)
    packed = jnp.zeros((8, channels), jnp.float32)
    for index, value in enumerate(
        (sums_shift, sums_gain, gain * sums_shift, gain * sums_gain, inv_std)
    ):
        packed = jnp.where(row == index, value, packed)
    for slot in range(sums.shape[0]):
        sums[slot] = packed

    all_rows = (out_rows * out_cols, channels)
    total = None
    for frame in range(frames):
        cots = jnp.concatenate(
            [
                (cot[frame + later] if frame + later < frames else halo[frame + later - frames])
                .reshape(all_rows)
                for later in range(3)
            ],
            axis=1,
        )
        term = dot(act[frame].reshape(all_rows).T, cots)
        total = term if total is None else total + term
    for later in range(3):
        block = total[:, later * channels : (later + 1) * channels] * loss_scale
        temporal[pl.ds(later * channels, channels)] = block.astype(jnp.bfloat16)


def split_rows(values, rows):
    pieces = []
    for value in values:
        rest = value
        for _ in range(3):
            piece = rest.astype(jnp.bfloat16).astype(jnp.float32)
            pieces.append(piece)
            rest = rest - piece
    row = lax.broadcasted_iota(jnp.int32, (rows, values[0].shape[-1]), 0)
    packed = jnp.zeros((rows, values[0].shape[-1]), jnp.float32)
    for index, piece in enumerate(pieces):
        packed = jnp.where(row == index, piece, packed)
    return packed.astype(jnp.bfloat16)


def join_rows(packed, count):
    return [
        packed[3 * i : 3 * i + 1] + packed[3 * i + 1 : 3 * i + 2] + packed[3 * i + 2 : 3 * i + 3]
        for i in range(count)
    ]


def store_rows(chunks, rows, first, values):
    done = 0
    while done < values.shape[0]:
        chunk, at = divmod(first + done, rows)
        count = min(rows - at, values.shape[0] - done)
        chunks[chunk, pl.ds(at, count)] = values[done : done + count]
        done += count


def grad_kernel(patches, normed, pre, sums, temporal, grads):
    frames, out_rows, out_cols, channels = normed.shape
    lanes = channels // GROUPS
    members = sums.shape[0] * frames * out_rows * out_cols * lanes
    clip = jnp.sum(sums[...], axis=0)
    inv_std = sums[0, 4:5]
    group = group_spread(clip, lanes) * inv_std / members
    group_shift, group_gain = group[2:3], group[3:4]
    flat = (out_rows * out_cols, channels)
    rows = grads.shape[1] - EXTRA
    backs = []
    for frame in range(frames):
        back = (
            pre[frame].reshape(flat) - group_shift - normed[frame].reshape(flat) * group_gain
        )
        backs.append(back.astype(jnp.bfloat16).T)
    backs = jnp.concatenate(backs, axis=1)
    for first in range(0, 9, 2):
        lanes = slice(first * channels, min(first + 2, 9) * channels)
        source = patches[:, :, :, lanes].reshape(frames * out_rows * out_cols, -1)
        part = dot(backs, source)
        for side in range(part.shape[1] // channels):
            block = part[:, side * channels : (side + 1) * channels].astype(jnp.bfloat16).T
            store_rows(grads, rows, (first + side) * channels, block)
    for tap in range(3):
        block = temporal[pl.ds(tap * channels, channels)]
        store_rows(grads, rows, (9 + tap) * channels, block)
    rest = grads.shape[0] * rows - 12 * channels
    if rest:
        store_rows(grads, rows, 12 * channels, jnp.zeros((rest, channels), jnp.bfloat16))
    share = clip * (1.0 / sums.shape[0])
    extra = split_rows([share[1:2], share[0:1]], EXTRA)
    for chunk in range(grads.shape[0]):
        grads[chunk, pl.ds(rows, EXTRA)] = extra


def total_of(arrived, first, count):
    total = arrived[0, pl.ds(first, count)].astype(jnp.float32)
    for chunk in range(1, arrived.shape[0]):
        total += arrived[chunk, pl.ds(first, count)].astype(jnp.float32)
    return total


def half_kernel(arrived, chunk):
    count = chunk.shape[0] - EXTRA
    chunk[pl.ds(0, count)] = total_of(arrived, 0, count).astype(jnp.bfloat16)
    sums = join_rows(total_of(arrived, count, EXTRA), 2)
    chunk[pl.ds(count, EXTRA)] = split_rows(sums, EXTRA)


def sum_kernel(mine, other, spread, totals):
    count = spread.shape[1]
    wide = [source[...].astype(jnp.float32) for source in (mine, other)]
    total = (wide[0][:count] + wide[1][:count]).astype(jnp.bfloat16)
    for slot in range(spread.shape[0]):
        spread[slot] = total
    sums = [join_rows(source[count:], 2) for source in wide]
    row = lax.broadcasted_iota(jnp.int32, totals.shape, 0)
    totals[...] = jnp.where(row == 0, sums[0][0] + sums[1][0], sums[0][1] + sums[1][1])


def final_kernel(
    arrived, totals, grad_spatial, grad_temporal, grad_gain, grad_shift, held, row_sums, done
):
    channels = arrived.shape[1]
    row_sums[...] = totals[...]
    copies = [
        pltpu.make_async_copy(row_sums.at[0:1], grad_gain, done.at[0]),
        pltpu.make_async_copy(row_sums.at[1:2], grad_shift, done.at[1]),
    ]
    for copy in copies:
        copy.start()
    piece = 3 * channels
    for index in range(4):
        rows = pl.ds(index * piece, piece)
        held[rows] = arrived[rows].astype(jnp.float32)
        target = grad_temporal if index == 3 else grad_spatial.at[rows]
        copies.append(pltpu.make_async_copy(held.at[rows], target, done.at[2 + index]))
        copies[-1].start()
    for copy in copies:
        copy.wait()


def encode_kernel(per_clip, act, halo, weights, encoded):
    frames, out_rows, out_cols, channels = act.shape
    not_first = lax.rem(lax.axis_index("seq"), per_clip) != 0
    flat = (STEP_ROWS * out_cols, channels)
    for frame in range(frames):

        def one(step, frame=frame):
            rows = pl.ds(step * STEP_ROWS, STEP_ROWS)
            total = None
            for tap in range(3):
                if frame >= tap:
                    source = act[frame - tap, rows]
                else:
                    source = halo[frames + frame - tap, rows]
                    source = jnp.where(not_first, source, jnp.zeros_like(source))
                term = dot(source.reshape(flat), weights[tap])
                total = term if total is None else total + term
            encoded[frame, rows] = total.astype(jnp.bfloat16).reshape(
                STEP_ROWS, out_cols, channels
            )

        each(out_rows // STEP_ROWS, one)


def on_device(video_in, w_spatial, w_temporal, norm_gain, norm_shift, cotangent):
    frames, height, width, channels = video_in.shape[1:]
    out_rows, out_cols = height // 2, width // 2
    dp_size, seq_size = lax.axis_size("dp"), lax.axis_size("seq")
    devices = dp_size * seq_size
    per_clip = FRAMES // frames
    assert frames >= 2 and FRAMES % frames == 0
    loss_scale = float(devices * frames * out_rows * out_cols) ** (-0.5)
    shape = (frames, out_rows, out_cols, channels)
    positions = frames * out_rows * out_cols
    video = video_in[0]
    cot = cotangent[0]
    f32, bf16 = jnp.float32, jnp.bfloat16
    struct = jax.ShapeDtypeStruct

    ahead_pairs = [
        (s, s // per_clip * per_clip + (s + 1) % per_clip) for s in range(seq_size)
    ]
    back_pairs = [(target, source) for source, target in ahead_pairs]
    clips = [list(range(first, first + per_clip)) for first in range(0, seq_size, per_clip)]

    def exchange(value, axes, groups=None):
        return lax.all_to_all(value, axes, 0, 0, axis_index_groups=groups, tiled=True)

    gate = pl.pallas_call(
        open_kernel,
        out_shape=pltpu.VMEM((8, channels), f32),
        out_specs=WHOLE,
        cost_estimate=pl.CostEstimate(
            flops=2 * positions * 9 * channels * channels,
            bytes_accessed=2 * video.size,
            transcendentals=0,
        ),
    )()
    cot_out, gate = lax.optimization_barrier((cot, gate))
    cot_halo = lax.ppermute(cot_out, "seq", back_pairs)

    pieces = 2 * frames
    def far(value):
        return pltpu.with_memory_space_constraint(value, pltpu.HBM)

    spatial, stats, patches, params = call(
        functools.partial(conv_kernel, pieces),
        (
            struct(shape, f32),
            struct((per_clip, 8, channels), f32),
            struct((frames, out_rows, out_cols, 9 * channels), bf16),
            struct((8, channels), f32),
        ),
        (
            gate,
            video,
            far(w_spatial.reshape(9 * channels, channels)),
            far(norm_gain[None]),
            far(norm_shift[None]),
        ),
        specs=[WHOLE] * 2 + [FAR] * 3,
        scratch=[
            pltpu.VMEM((4 * STEP_ROWS, 8 + width, channels), f32),
            pltpu.VMEM((9 * channels, channels), bf16),
            pltpu.SemaphoreType.DMA((3,)),
        ],
        flops=2 * positions * 9 * channels * channels,
    )
    stats = exchange(stats, "seq", clips)
    act, normed, slope, scales = call(
        functools.partial(act_kernel, loss_scale),
        (
            struct(shape, bf16),
            struct(shape, f32),
            struct(shape, f32),
            struct((8, channels), f32),
        ),
        (spatial, stats, params),
    )
    act_halo = lax.ppermute(act, "seq", ahead_pairs)
    pre, temporal, own = call(
        functools.partial(back_kernel, loss_scale),
        (
            struct(shape, f32),
            struct((3 * channels, channels), bf16),
            struct((per_clip, 8, channels), f32),
        ),
        (cot, cot_halo, w_temporal, scales, normed, slope, act),
        scratch=[pltpu.VMEM((2,) + shape[1:], bf16)],
        flops=2 * positions * 6 * channels * channels,
    )
    sums = exchange(own, "seq", clips)
    halves = 2 if seq_size % 2 == 0 else 1
    half = seq_size // halves
    near = [
        [d * seq_size + s for d in range(dp_size) for s in range(first, first + half)]
        for first in range(0, seq_size, half)
    ]
    count = dp_size * half
    rows = -(-12 * channels // (16 * count)) * 16
    sums, act_halo = lax.optimization_barrier((sums, act_halo))
    grads = call(
        grad_kernel,
        struct((count, rows + EXTRA, channels), bf16),
        (patches, normed, pre, sums, temporal),
        flops=2 * positions * 9 * channels * channels,
    )
    grads = exchange(grads, ("dp", "seq"), near)
    mine = call(half_kernel, struct((rows + EXTRA, channels), bf16), (grads,))
    if halves == 2:
        other = lax.ppermute(mine, "seq", [(s, (s + half) % seq_size) for s in range(seq_size)])
    else:
        other = jnp.zeros_like(mine)
    act, act_halo, _ = lax.optimization_barrier((act, act_halo, mine))
    encoded = call(
        functools.partial(encode_kernel, per_clip),
        struct(shape, bf16),
        (act, act_halo, w_temporal),
        flops=2 * positions * 3 * channels * channels,
    )
    other, encoded = lax.optimization_barrier((other, encoded))
    grads, totals = call(
        sum_kernel,
        (struct((count, rows, channels), bf16), struct((8, channels), f32)),
        (mine, other),
    )
    grads = exchange(grads, ("dp", "seq"), near)
    grad_spatial, grad_temporal, grad_gain, grad_shift = call(
        final_kernel,
        (
            struct((9 * channels, channels), f32),
            struct((3 * channels, channels), f32),
            struct((1, channels), f32),
            struct((1, channels), f32),
        ),
        (grads.reshape(count * rows, channels), totals),
        outs=FAR,
        scratch=[
            pltpu.VMEM((12 * channels, channels), f32),
            pltpu.VMEM((8, channels), f32),
            pltpu.SemaphoreType.DMA((6,)),
        ],
    )
    return (
        encoded[None],
        grad_spatial.reshape(3, 3, channels, channels),
        grad_temporal.reshape(3, channels, channels),
        grad_gain[0],
        grad_shift[0],
    )


def solution(mesh):
    placed = P("dp", "seq", None, None, None)
    return jax.shard_map(
        on_device,
        mesh=mesh,
        in_specs=(placed, P(), P(), P(), P(), placed),
        out_specs=(placed, P(), P(), P(), P()),
        check_vma=False,
    )
```

```python
import functools
import math

import jax
import jax.numpy as jnp
from jax import lax
from jax.experimental import pallas as pl
from jax.experimental.pallas import tpu as pltpu
from jax.sharding import PartitionSpec as P

GROUPS = 32
FRAMES = 8
STEP_ROWS = 8
EXTRA = 8
SPARE_BYTES = 4 * 1024 * 1024

WHOLE = pl.BlockSpec(memory_space=pltpu.VMEM)
FAR = pl.BlockSpec(memory_space=pltpu.HBM)


def dot(left, right):
    return jnp.dot(left, right, preferred_element_type=jnp.float32)


def dot_transposed(left, right):
    return lax.dot_general(
        left, right, (((1,), (1,)), ((), ())), preferred_element_type=jnp.float32
    )


def each(count, body):
    if count <= 8:
        for step in range(count):
            body(step)
    else:
        lax.fori_loop(0, count, lambda step, carry: (body(step), carry)[1], 0)


def call(kernel, out_shape, operands, specs=None, scratch=(), flops=0):
    sizes = [value.size * value.dtype.itemsize for value in operands]
    sizes += [value.size * value.dtype.itemsize for value in jax.tree.leaves(out_shape)]
    held = sum(math.prod(item.shape) * 4 for item in scratch if hasattr(item, "shape"))
    return pl.pallas_call(
        kernel,
        out_shape=out_shape,
        in_specs=specs or [WHOLE] * len(operands),
        out_specs=jax.tree.map(lambda _: WHOLE, out_shape),
        scratch_shapes=list(scratch),
        compiler_params=pltpu.CompilerParams(vmem_limit_bytes=sum(sizes) + held + SPARE_BYTES),
        cost_estimate=pl.CostEstimate(
            flops=flops, bytes_accessed=sum(sizes), transcendentals=0
        ),
    )(*operands)


def group_spread(values, lanes):
    channels = values.shape[-1]
    place = lax.rem(lax.broadcasted_iota(jnp.int32, values.shape, 1), lanes)
    total = values
    for shift in range(1, lanes):
        ahead = pltpu.roll(values, channels - shift, 1)
        behind = pltpu.roll(values, shift, 1)
        total += jnp.where(place < lanes - shift, ahead, 0.0)
        total += jnp.where(place >= shift, behind, 0.0)
    return total


def open_kernel(gate):
    gate[...] = jnp.zeros(gate.shape, gate.dtype)


def conv_kernel(
    pieces, blank, video, weights_far, gain_far, shift_far, spatial, stats, odd, even, params, wide,
    weights, arrived,
):
    frames, height, width, channels = video.shape
    out_rows, out_cols = height // 2, width // 2
    positions = frames * out_rows * out_cols
    half = height * frames // pieces
    params[...] = blank[...]
    copies = [
        pltpu.make_async_copy(source, target, arrived.at[index])
        for index, (source, target) in enumerate(
            ((weights_far, weights), (gain_far, params.at[0:1]), (shift_far, params.at[1:2]))
        )
    ]
    for copy in copies:
        copy.start()
    for slot in range(wide.shape[0]):
        wide[slot, 0:8] = jnp.zeros((8, channels), jnp.float32)
    for frame in range(frames):
        odd[frame, 0] = jnp.zeros((out_cols, 3 * channels), jnp.bfloat16)
    flat = (STEP_ROWS * out_cols, 3 * channels)
    steps = half // 2 // STEP_ROWS

    def place(piece, step):
        return piece * half // height, piece * half % height // 2 + step * STEP_ROWS

    def separate(piece, step):
        frame, first = place(piece, step)
        base = piece % 2 * 2 * STEP_ROWS
        for line in range(2 * STEP_ROWS):
            wide[base + line, 8 : 8 + width] = video[frame, 2 * first + line].astype(jnp.float32)
        for line in range(2 * STEP_ROWS):
            for tap in range(3):
                value = wide[base + line, pl.ds(7 + tap, out_cols, stride=2), :]
                lanes = slice(tap * channels, (tap + 1) * channels)
                if line % 2:
                    odd[frame, first + line // 2 + 1, :, lanes] = value.astype(jnp.bfloat16)
                else:
                    even[frame, first + line // 2, :, lanes] = value.astype(jnp.bfloat16)

    def multiply(piece, step):
        frame, first = place(piece, step)
        total = dot(odd[frame, pl.ds(first, STEP_ROWS)].reshape(flat), weights[0])
        total += dot(even[frame, pl.ds(first, STEP_ROWS)].reshape(flat), weights[1])
        total += dot(odd[frame, pl.ds(first + 1, STEP_ROWS)].reshape(flat), weights[2])
        spatial[frame, pl.ds(first, STEP_ROWS)] = total.reshape(STEP_ROWS, out_cols, channels)
        return total

    def fold(values):
        return values.reshape(-1, 8, channels).sum(axis=0)

    def over_steps(piece, term, start):
        if steps <= 8:
            for step in range(steps):
                start = jax.tree.map(jnp.add, start, term(piece, step))
            return start
        return lax.fori_loop(
            0, steps, lambda step, sums: jax.tree.map(jnp.add, sums, term(piece, step)), start
        )

    zero = jnp.zeros((8, channels), jnp.float32)

    def first_sum(piece, step):
        return fold(multiply(piece, step))

    def first_moments(piece, step):
        frame, first = place(piece, step)
        off = spatial[frame, pl.ds(first, STEP_ROWS)].reshape(-1, channels) - near
        return fold(off), fold(off * off)

    def moments(piece, step):
        off = multiply(piece, step) - near
        return fold(off), fold(off * off)

    for piece in range(pieces):
        each(steps, functools.partial(separate, piece))
    copies[0].wait()
    near = over_steps(0, first_sum, zero).sum(axis=0, keepdims=True) * (pieces / positions)
    sums = over_steps(0, first_moments, (zero, zero))
    for piece in range(1, pieces - 1):
        sums = over_steps(piece, moments, sums)
    sums = over_steps(pieces - 1, moments, sums)
    off = sums[0].sum(axis=0, keepdims=True) / positions
    mean = near + off
    square = sums[1].sum(axis=0, keepdims=True) - positions * off * off
    row = lax.broadcasted_iota(jnp.int32, (8, channels), 0)
    packed = jnp.where(row == 0, mean, jnp.where(row == 1, square, 0.0))
    for slot in range(stats.shape[0]):
        stats[slot] = packed
    for copy in copies[1:]:
        copy.wait()

def clip_norm(stats, positions, lanes):
    cells = stats.shape[0] * lanes
    means = [stats[member, 0:1] for member in range(stats.shape[0])]
    squares = [stats[member, 1:2] for member in range(stats.shape[0])]
    mean = group_spread(jnp.broadcast_to(sum(means), (8, means[0].shape[-1])), lanes)[0:1] / cells
    square = sum(squares)
    for value in means:
        square = square + positions * (value - mean) ** 2
    square = group_spread(jnp.broadcast_to(square, (8, square.shape[-1])), lanes)[0:1]
    return mean, lax.rsqrt(square / (cells * positions) + 1e-05)


def act_kernel(loss_scale, spatial, stats, params, act, normed, slope, scales):
    frames, out_rows, out_cols, channels = spatial.shape
    positions = frames * out_rows * out_cols
    mean, inv_std = clip_norm(stats, positions, channels // GROUPS)
    gain, shift = params[0:1], params[1:2]
    row = lax.broadcasted_iota(jnp.int32, (8, channels), 0)
    scales[...] = jnp.where(row == 0, inv_std, gain)
    flat = (STEP_ROWS * out_cols, channels)
    shaped = (STEP_ROWS, out_cols, channels)
    for frame in range(frames):

        def one(step, frame=frame):
            rows = pl.ds(step * STEP_ROWS, STEP_ROWS)
            norm = (spatial[frame, rows].reshape(flat) - mean) * inv_std
            before = norm * gain + shift
            sig = 0.5 + 0.5 * jnp.tanh(0.5 * before)
            act[frame, rows] = (before * sig).astype(jnp.bfloat16).reshape(shaped)
            normed[frame, rows] = norm.reshape(shaped)
            slope[frame, rows] = (loss_scale * sig * (1.0 + before * (1.0 - sig))).reshape(shaped)

        each(out_rows // STEP_ROWS, one)


def back_kernel(
    loss_scale, cot, arrived, weights, scales, normed, slope, act, pre, temporal, sums, halo
):
    frames, out_rows, out_cols, channels = cot.shape
    inv_std, gain = scales[0:1], scales[1:2]
    per_clip = sums.shape[0]
    not_last = lax.rem(lax.axis_index("seq"), per_clip) != per_clip - 1
    for frame in range(2):
        value = arrived[frame]
        halo[frame] = jnp.where(not_last, value, jnp.zeros_like(value))
    turned_weights = jnp.concatenate([weights[tap] for tap in range(3)], axis=1)
    flat = (STEP_ROWS * out_cols, channels)
    shaped = (STEP_ROWS, out_cols, channels)
    sums_shift = jnp.zeros((8, channels), jnp.float32)
    sums_gain = jnp.zeros((8, channels), jnp.float32)

    def fold(values):
        return values.reshape(-1, 8, channels).sum(axis=0)

    for frame in range(frames):

        def cot_block(later, rows, shape, frame=frame):
            if frame + later < frames:
                return cot[frame + later, rows].reshape(shape)
            return halo[frame + later - frames, rows].reshape(shape)

        def one(step, carry, frame=frame):
            rows = pl.ds(step * STEP_ROWS, STEP_ROWS)
            cots = jnp.concatenate([cot_block(later, rows, flat) for later in range(3)], axis=1)
            back = dot_transposed(cots, turned_weights)
            back = back.astype(jnp.bfloat16).astype(jnp.float32)
            back_pre = back * slope[frame, rows].reshape(flat)
            norm = normed[frame, rows].reshape(flat)
            pre[frame, rows] = (back_pre * (gain * inv_std)).reshape(shaped)
            return (carry[0] + fold(back_pre), carry[1] + fold(back_pre * norm))

        steps = out_rows // STEP_ROWS
        if steps <= 4:
            for step in range(steps):
                sums_shift, sums_gain = one(step, (sums_shift, sums_gain))
        else:
            sums_shift, sums_gain = lax.fori_loop(0, steps, one, (sums_shift, sums_gain))

    sums_shift = sums_shift.sum(axis=0, keepdims=True)
    sums_gain = sums_gain.sum(axis=0, keepdims=True)
    row = lax.broadcasted_iota(jnp.int32, (8, channels), 0)
    packed = jnp.zeros((8, channels), jnp.float32)
    for index, value in enumerate(
        (sums_shift, sums_gain, gain * sums_shift, gain * sums_gain, inv_std)
    ):
        packed = jnp.where(row == index, value, packed)
    for slot in range(sums.shape[0]):
        sums[slot] = packed

    all_rows = (out_rows * out_cols, channels)
    total = None
    for frame in range(frames):
        cots = jnp.concatenate(
            [
                (cot[frame + later] if frame + later < frames else halo[frame + later - frames])
                .reshape(all_rows)
                for later in range(3)
            ],
            axis=1,
        )
        term = dot(act[frame].reshape(all_rows).T, cots)
        total = term if total is None else total + term
    for later in range(3):
        block = total[:, later * channels : (later + 1) * channels] * loss_scale
        temporal[pl.ds(later * channels, channels)] = block.astype(jnp.bfloat16)


def split_rows(values, rows):
    pieces = []
    for value in values:
        rest = value
        for _ in range(3):
            piece = rest.astype(jnp.bfloat16).astype(jnp.float32)
            pieces.append(piece)
            rest = rest - piece
    row = lax.broadcasted_iota(jnp.int32, (rows, values[0].shape[-1]), 0)
    packed = jnp.zeros((rows, values[0].shape[-1]), jnp.float32)
    for index, piece in enumerate(pieces):
        packed = jnp.where(row == index, piece, packed)
    return packed.astype(jnp.bfloat16)


def join_rows(packed, count):
    return [
        packed[3 * i : 3 * i + 1] + packed[3 * i + 1 : 3 * i + 2] + packed[3 * i + 2 : 3 * i + 3]
        for i in range(count)
    ]


def store_rows(chunks, rows, first, values):
    done = 0
    while done < values.shape[0]:
        chunk, at = divmod(first + done, rows)
        count = min(rows - at, values.shape[0] - done)
        chunks[chunk, pl.ds(at, count)] = values[done : done + count]
        done += count


def grad_kernel(
    odd, even, normed, pre, sums, temporal, grads
):
    frames, out_rows, out_cols, channels = normed.shape
    lanes = channels // GROUPS
    members = sums.shape[0] * frames * out_rows * out_cols * lanes
    clip = jnp.sum(sums[...], axis=0)
    inv_std = sums[0, 4:5]
    group = group_spread(clip, lanes) * inv_std / members
    group_shift, group_gain = group[2:3], group[3:4]
    flat = (out_rows * out_cols, channels)
    rows = grads.shape[1] - EXTRA
    backs = []
    for frame in range(frames):
        back = (
            pre[frame].reshape(flat) - group_shift - normed[frame].reshape(flat) * group_gain
        )
        backs.append(back.astype(jnp.bfloat16).T)
    backs = jnp.concatenate(backs, axis=1)
    for tap, source in enumerate((odd[:, 0:out_rows], even[...], odd[:, 1 : out_rows + 1])):
        part = dot(backs, source.reshape(frames * out_rows * out_cols, 3 * channels))
        for side in range(3):
            block = part[:, side * channels : (side + 1) * channels].astype(jnp.bfloat16).T
            store_rows(grads, rows, (3 * tap + side) * channels, block)
    for tap in range(3):
        block = temporal[pl.ds(tap * channels, channels)]
        store_rows(grads, rows, (9 + tap) * channels, block)
    rest = grads.shape[0] * rows - 12 * channels
    if rest:
        store_rows(grads, rows, 12 * channels, jnp.zeros((rest, channels), jnp.bfloat16))
    share = clip * (1.0 / sums.shape[0])
    extra = split_rows([share[1:2], share[0:1]], EXTRA)
    for chunk in range(grads.shape[0]):
        grads[chunk, pl.ds(rows, EXTRA)] = extra


def total_of(arrived, first, count):
    total = arrived[0, pl.ds(first, count)].astype(jnp.float32)
    for chunk in range(1, arrived.shape[0]):
        total += arrived[chunk, pl.ds(first, count)].astype(jnp.float32)
    return total


def half_kernel(arrived, chunk):
    count = chunk.shape[0] - EXTRA
    chunk[pl.ds(0, count)] = total_of(arrived, 0, count).astype(jnp.bfloat16)
    sums = join_rows(total_of(arrived, count, EXTRA), 2)
    chunk[pl.ds(count, EXTRA)] = split_rows(sums, EXTRA)


def sum_kernel(mine, other, spread, totals):
    count = spread.shape[1]
    wide = [source[...].astype(jnp.float32) for source in (mine, other)]
    total = (wide[0][:count] + wide[1][:count]).astype(jnp.bfloat16)
    for slot in range(spread.shape[0]):
        spread[slot] = total
    sums = [join_rows(source[count:], 2) for source in wide]
    row = lax.broadcasted_iota(jnp.int32, totals.shape, 0)
    totals[...] = jnp.where(row == 0, sums[0][0] + sums[1][0], sums[0][1] + sums[1][1])


def final_kernel(arrived, totals, grad_spatial, grad_temporal, grad_gain, grad_shift):
    grad_gain[...] = totals[0:1]
    grad_shift[...] = totals[1:2]
    rows = grad_spatial.shape[0]
    grad_spatial[...] = arrived[pl.ds(0, rows)].astype(jnp.float32)
    grad_temporal[...] = arrived[pl.ds(rows, grad_temporal.shape[0])].astype(jnp.float32)


def encode_kernel(per_clip, act, halo, weights, encoded):
    frames, out_rows, out_cols, channels = act.shape
    not_first = lax.rem(lax.axis_index("seq"), per_clip) != 0
    flat = (STEP_ROWS * out_cols, channels)
    for frame in range(frames):

        def one(step, frame=frame):
            rows = pl.ds(step * STEP_ROWS, STEP_ROWS)
            total = None
            for tap in range(3):
                if frame >= tap:
                    source = act[frame - tap, rows]
                else:
                    source = halo[frames + frame - tap, rows]
                    source = jnp.where(not_first, source, jnp.zeros_like(source))
                term = dot(source.reshape(flat), weights[tap])
                total = term if total is None else total + term
            encoded[frame, rows] = total.astype(jnp.bfloat16).reshape(
                STEP_ROWS, out_cols, channels
            )

        each(out_rows // STEP_ROWS, one)


def on_device(video_in, w_spatial, w_temporal, norm_gain, norm_shift, cotangent):
    frames, height, width, channels = video_in.shape[1:]
    out_rows, out_cols = height // 2, width // 2
    dp_size, seq_size = lax.axis_size("dp"), lax.axis_size("seq")
    devices = dp_size * seq_size
    per_clip = FRAMES // frames
    assert frames >= 2 and FRAMES % frames == 0
    loss_scale = float(devices * frames * out_rows * out_cols) ** (-0.5)
    shape = (frames, out_rows, out_cols, channels)
    positions = frames * out_rows * out_cols
    video = video_in[0]
    cot = cotangent[0]
    f32, bf16 = jnp.float32, jnp.bfloat16
    struct = jax.ShapeDtypeStruct

    ahead_pairs = [
        (s, s // per_clip * per_clip + (s + 1) % per_clip) for s in range(seq_size)
    ]
    back_pairs = [(target, source) for source, target in ahead_pairs]
    clips = [list(range(first, first + per_clip)) for first in range(0, seq_size, per_clip)]

    def exchange(value, axes, groups=None):
        return lax.all_to_all(value, axes, 0, 0, axis_index_groups=groups, tiled=True)

    gate = pl.pallas_call(
        open_kernel,
        out_shape=pltpu.VMEM((8, channels), f32),
        out_specs=WHOLE,
        cost_estimate=pl.CostEstimate(
            flops=2 * positions * 9 * channels * channels,
            bytes_accessed=2 * video.size,
            transcendentals=0,
        ),
    )()
    cot_out, gate = lax.optimization_barrier((cot, gate))
    cot_halo = lax.ppermute(cot_out, "seq", back_pairs)

    pieces = 2 * frames
    def far(value):
        return pltpu.with_memory_space_constraint(value, pltpu.HBM)

    spatial, stats, odd, even, params = call(
        functools.partial(conv_kernel, pieces),
        (
            struct(shape, f32),
            struct((per_clip, 8, channels), f32),
            struct((frames, out_rows + 1, out_cols, 3 * channels), bf16),
            struct((frames, out_rows, out_cols, 3 * channels), bf16),
            struct((8, channels), f32),
        ),
        (
            gate,
            video,
            far(w_spatial.reshape(3, 3 * channels, channels)),
            far(norm_gain[None]),
            far(norm_shift[None]),
        ),
        specs=[WHOLE] * 2 + [FAR] * 3,
        scratch=[
            pltpu.VMEM((4 * STEP_ROWS, 8 + width, channels), f32),
            pltpu.VMEM((3, 3 * channels, channels), bf16),
            pltpu.SemaphoreType.DMA((3,)),
        ],
        flops=2 * positions * 9 * channels * channels,
    )
    stats = exchange(stats, "seq", clips)
    act, normed, slope, scales = call(
        functools.partial(act_kernel, loss_scale),
        (
            struct(shape, bf16),
            struct(shape, f32),
            struct(shape, f32),
            struct((8, channels), f32),
        ),
        (spatial, stats, params),
    )
    act_halo = lax.ppermute(act, "seq", ahead_pairs)
    pre, temporal, own = call(
        functools.partial(back_kernel, loss_scale),
        (
            struct(shape, f32),
            struct((3 * channels, channels), bf16),
            struct((per_clip, 8, channels), f32),
        ),
        (cot, cot_halo, w_temporal, scales, normed, slope, act),
        scratch=[pltpu.VMEM((2,) + shape[1:], bf16)],
        flops=2 * positions * 6 * channels * channels,
    )
    sums = exchange(own, "seq", clips)
    halves = 2 if seq_size % 2 == 0 else 1
    half = seq_size // halves
    near = [
        [d * seq_size + s for d in range(dp_size) for s in range(first, first + half)]
        for first in range(0, seq_size, half)
    ]
    count = dp_size * half
    rows = -(-12 * channels // (16 * count)) * 16
    sums, act_halo = lax.optimization_barrier((sums, act_halo))
    grads = call(
        grad_kernel,
        struct((count, rows + EXTRA, channels), bf16),
        (odd, even, normed, pre, sums, temporal),
        flops=2 * positions * 9 * channels * channels,
    )
    grads = exchange(grads, ("dp", "seq"), near)
    mine = call(half_kernel, struct((rows + EXTRA, channels), bf16), (grads,))
    if halves == 2:
        other = lax.ppermute(mine, "seq", [(s, (s + half) % seq_size) for s in range(seq_size)])
    else:
        other = jnp.zeros_like(mine)
    act, act_halo, _ = lax.optimization_barrier((act, act_halo, mine))
    encoded = call(
        functools.partial(encode_kernel, per_clip),
        struct(shape, bf16),
        (act, act_halo, w_temporal),
        flops=2 * positions * 3 * channels * channels,
    )
    other, encoded = lax.optimization_barrier((other, encoded))
    grads, totals = call(
        sum_kernel,
        (struct((count, rows, channels), bf16), struct((8, channels), f32)),
        (mine, other),
    )
    grads = exchange(grads, ("dp", "seq"), near)
    grad_spatial, grad_temporal, grad_gain, grad_shift = call(
        final_kernel,
        (
            struct((9 * channels, channels), f32),
            struct((3 * channels, channels), f32),
            struct((1, channels), f32),
            struct((1, channels), f32),
        ),
        (grads.reshape(count * rows, channels), totals),
    )
    return (
        encoded[None],
        grad_spatial.reshape(3, 3, channels, channels),
        grad_temporal.reshape(3, channels, channels),
        grad_gain[0],
        grad_shift[0],
    )


def solution(mesh):
    placed = P("dp", "seq", None, None, None)
    return jax.shard_map(
        on_device,
        mesh=mesh,
        in_specs=(placed, P(), P(), P(), P(), placed),
        out_specs=(placed, P(), P(), P(), P()),
        check_vma=False,
    )
```

```python
import functools
import math

import jax
import jax.numpy as jnp
from jax import lax
from jax.experimental import pallas as pl
from jax.experimental.pallas import tpu as pltpu
from jax.sharding import PartitionSpec as P

GROUPS = 32
FRAMES = 8
STEP_ROWS = 8
EXTRA = 8
SPARE_BYTES = 4 * 1024 * 1024

WHOLE = pl.BlockSpec(memory_space=pltpu.VMEM)
FAR = pl.BlockSpec(memory_space=pltpu.HBM)


def dot(left, right):
    return jnp.dot(left, right, preferred_element_type=jnp.float32)


def dot_transposed(left, right):
    return lax.dot_general(
        left, right, (((1,), (1,)), ((), ())), preferred_element_type=jnp.float32
    )


def each(count, body):
    if count <= 8:
        for step in range(count):
            body(step)
    else:
        lax.fori_loop(0, count, lambda step, carry: (body(step), carry)[1], 0)


def call(kernel, out_shape, operands, specs=None, scratch=(), flops=0):
    sizes = [value.size * value.dtype.itemsize for value in operands]
    sizes += [value.size * value.dtype.itemsize for value in jax.tree.leaves(out_shape)]
    held = sum(math.prod(item.shape) * 4 for item in scratch if hasattr(item, "shape"))
    return pl.pallas_call(
        kernel,
        out_shape=out_shape,
        in_specs=specs or [WHOLE] * len(operands),
        out_specs=jax.tree.map(lambda _: WHOLE, out_shape),
        scratch_shapes=list(scratch),
        compiler_params=pltpu.CompilerParams(vmem_limit_bytes=sum(sizes) + held + SPARE_BYTES),
        cost_estimate=pl.CostEstimate(
            flops=flops, bytes_accessed=sum(sizes), transcendentals=0
        ),
    )(*operands)


def group_spread(values, lanes):
    channels = values.shape[-1]
    place = lax.rem(lax.broadcasted_iota(jnp.int32, values.shape, 1), lanes)
    total = values
    for shift in range(1, lanes):
        ahead = pltpu.roll(values, channels - shift, 1)
        behind = pltpu.roll(values, shift, 1)
        total += jnp.where(place < lanes - shift, ahead, 0.0)
        total += jnp.where(place >= shift, behind, 0.0)
    return total


def open_kernel(gate):
    gate[...] = jnp.zeros(gate.shape, gate.dtype)


def conv_kernel(
    pieces, blank, video, weights_far, gain_far, shift_far, spatial, stats, odd, even, params, wide,
    weights, arrived,
):
    frames, height, width, channels = video.shape
    out_rows, out_cols = height // 2, width // 2
    positions = frames * out_rows * out_cols
    half = height * frames // pieces
    params[...] = blank[...]
    copies = [
        pltpu.make_async_copy(source, target, arrived.at[index])
        for index, (source, target) in enumerate(
            ((weights_far, weights), (gain_far, params.at[0:1]), (shift_far, params.at[1:2]))
        )
    ]
    for copy in copies:
        copy.start()
    for slot in range(wide.shape[0]):
        wide[slot, 0:8] = jnp.zeros((8, channels), jnp.float32)
    for frame in range(frames):
        odd[frame, 0] = jnp.zeros((out_cols, 3 * channels), jnp.bfloat16)
    flat = (STEP_ROWS * out_cols, 3 * channels)
    steps = half // 2 // STEP_ROWS

    def place(piece, step):
        return piece * half // height, piece * half % height // 2 + step * STEP_ROWS

    def separate(piece, step):
        frame, first = place(piece, step)
        base = piece % 2 * 2 * STEP_ROWS
        for line in range(2 * STEP_ROWS):
            wide[base + line, 8 : 8 + width] = video[frame, 2 * first + line].astype(jnp.float32)
        for line in range(2 * STEP_ROWS):
            for tap in range(3):
                value = wide[base + line, pl.ds(7 + tap, out_cols, stride=2), :]
                lanes = slice(tap * channels, (tap + 1) * channels)
                if line % 2:
                    odd[frame, first + line // 2 + 1, :, lanes] = value.astype(jnp.bfloat16)
                else:
                    even[frame, first + line // 2, :, lanes] = value.astype(jnp.bfloat16)

    def multiply(piece, step):
        frame, first = place(piece, step)
        sources = (
            odd[frame, pl.ds(first, STEP_ROWS)],
            even[frame, pl.ds(first, STEP_ROWS)],
            odd[frame, pl.ds(first + 1, STEP_ROWS)],
        )
        side_by_side = jnp.concatenate([source.reshape(flat) for source in sources], axis=1)
        total = dot(side_by_side, weights[...])
        spatial[frame, pl.ds(first, STEP_ROWS)] = total.reshape(STEP_ROWS, out_cols, channels)
        return total

    def fold(values):
        return values.reshape(-1, 8, channels).sum(axis=0)

    def over_steps(piece, term, start):
        if steps <= 8:
            for step in range(steps):
                start = jax.tree.map(jnp.add, start, term(piece, step))
            return start
        return lax.fori_loop(
            0, steps, lambda step, sums: jax.tree.map(jnp.add, sums, term(piece, step)), start
        )

    zero = jnp.zeros((8, channels), jnp.float32)

    def first_sum(piece, step):
        return fold(multiply(piece, step))

    def first_moments(piece, step):
        frame, first = place(piece, step)
        off = spatial[frame, pl.ds(first, STEP_ROWS)].reshape(-1, channels) - near
        return fold(off), fold(off * off)

    def moments(piece, step):
        off = multiply(piece, step) - near
        return fold(off), fold(off * off)

    for piece in range(pieces):
        each(steps, functools.partial(separate, piece))
    copies[0].wait()
    near = over_steps(0, first_sum, zero).sum(axis=0, keepdims=True) * (pieces / positions)
    sums = over_steps(0, first_moments, (zero, zero))
    for piece in range(1, pieces - 1):
        sums = over_steps(piece, moments, sums)
    sums = over_steps(pieces - 1, moments, sums)
    off = sums[0].sum(axis=0, keepdims=True) / positions
    mean = near + off
    square = sums[1].sum(axis=0, keepdims=True) - positions * off * off
    row = lax.broadcasted_iota(jnp.int32, (8, channels), 0)
    packed = jnp.where(row == 0, mean, jnp.where(row == 1, square, 0.0))
    for slot in range(stats.shape[0]):
        stats[slot] = packed
    for copy in copies[1:]:
        copy.wait()

def clip_norm(stats, positions, lanes):
    cells = stats.shape[0] * lanes
    means = [stats[member, 0:1] for member in range(stats.shape[0])]
    squares = [stats[member, 1:2] for member in range(stats.shape[0])]
    mean = group_spread(jnp.broadcast_to(sum(means), (8, means[0].shape[-1])), lanes)[0:1] / cells
    square = sum(squares)
    for value in means:
        square = square + positions * (value - mean) ** 2
    square = group_spread(jnp.broadcast_to(square, (8, square.shape[-1])), lanes)[0:1]
    return mean, lax.rsqrt(square / (cells * positions) + 1e-05)


def act_kernel(loss_scale, spatial, stats, params, act, normed, slope, scales):
    frames, out_rows, out_cols, channels = spatial.shape
    positions = frames * out_rows * out_cols
    mean, inv_std = clip_norm(stats, positions, channels // GROUPS)
    gain, shift = params[0:1], params[1:2]
    row = lax.broadcasted_iota(jnp.int32, (8, channels), 0)
    scales[...] = jnp.where(row == 0, inv_std, gain)
    flat = (STEP_ROWS * out_cols, channels)
    shaped = (STEP_ROWS, out_cols, channels)
    for frame in range(frames):

        def one(step, frame=frame):
            rows = pl.ds(step * STEP_ROWS, STEP_ROWS)
            norm = (spatial[frame, rows].reshape(flat) - mean) * inv_std
            before = norm * gain + shift
            sig = 0.5 + 0.5 * jnp.tanh(0.5 * before)
            act[frame, rows] = (before * sig).astype(jnp.bfloat16).reshape(shaped)
            normed[frame, rows] = norm.reshape(shaped)
            slope[frame, rows] = (loss_scale * sig * (1.0 + before * (1.0 - sig))).reshape(shaped)

        each(out_rows // STEP_ROWS, one)


def back_kernel(
    loss_scale, cot, arrived, weights, scales, normed, slope, act, pre, temporal, sums, halo
):
    frames, out_rows, out_cols, channels = cot.shape
    inv_std, gain = scales[0:1], scales[1:2]
    per_clip = sums.shape[0]
    not_last = lax.rem(lax.axis_index("seq"), per_clip) != per_clip - 1
    for frame in range(2):
        value = arrived[frame]
        halo[frame] = jnp.where(not_last, value, jnp.zeros_like(value))
    turned_weights = jnp.concatenate([weights[tap] for tap in range(3)], axis=1)
    flat = (STEP_ROWS * out_cols, channels)
    shaped = (STEP_ROWS, out_cols, channels)
    sums_shift = jnp.zeros((8, channels), jnp.float32)
    sums_gain = jnp.zeros((8, channels), jnp.float32)

    def fold(values):
        return values.reshape(-1, 8, channels).sum(axis=0)

    for frame in range(frames):

        def cot_block(later, rows, shape, frame=frame):
            if frame + later < frames:
                return cot[frame + later, rows].reshape(shape)
            return halo[frame + later - frames, rows].reshape(shape)

        def one(step, carry, frame=frame):
            rows = pl.ds(step * STEP_ROWS, STEP_ROWS)
            cots = jnp.concatenate([cot_block(later, rows, flat) for later in range(3)], axis=1)
            back = dot_transposed(cots, turned_weights)
            back = back.astype(jnp.bfloat16).astype(jnp.float32)
            back_pre = back * slope[frame, rows].reshape(flat)
            norm = normed[frame, rows].reshape(flat)
            pre[frame, rows] = (back_pre * (gain * inv_std)).reshape(shaped)
            return (carry[0] + fold(back_pre), carry[1] + fold(back_pre * norm))

        steps = out_rows // STEP_ROWS
        if steps <= 4:
            for step in range(steps):
                sums_shift, sums_gain = one(step, (sums_shift, sums_gain))
        else:
            sums_shift, sums_gain = lax.fori_loop(0, steps, one, (sums_shift, sums_gain))

    sums_shift = sums_shift.sum(axis=0, keepdims=True)
    sums_gain = sums_gain.sum(axis=0, keepdims=True)
    row = lax.broadcasted_iota(jnp.int32, (8, channels), 0)
    packed = jnp.zeros((8, channels), jnp.float32)
    for index, value in enumerate(
        (sums_shift, sums_gain, gain * sums_shift, gain * sums_gain, inv_std)
    ):
        packed = jnp.where(row == index, value, packed)
    for slot in range(sums.shape[0]):
        sums[slot] = packed

    all_rows = (out_rows * out_cols, channels)
    total = None
    for frame in range(frames):
        cots = jnp.concatenate(
            [
                (cot[frame + later] if frame + later < frames else halo[frame + later - frames])
                .reshape(all_rows)
                for later in range(3)
            ],
            axis=1,
        )
        term = dot(act[frame].reshape(all_rows).T, cots)
        total = term if total is None else total + term
    for later in range(3):
        block = total[:, later * channels : (later + 1) * channels] * loss_scale
        temporal[pl.ds(later * channels, channels)] = block.astype(jnp.bfloat16)


def split_rows(values, rows):
    pieces = []
    for value in values:
        rest = value
        for _ in range(3):
            piece = rest.astype(jnp.bfloat16).astype(jnp.float32)
            pieces.append(piece)
            rest = rest - piece
    row = lax.broadcasted_iota(jnp.int32, (rows, values[0].shape[-1]), 0)
    packed = jnp.zeros((rows, values[0].shape[-1]), jnp.float32)
    for index, piece in enumerate(pieces):
        packed = jnp.where(row == index, piece, packed)
    return packed.astype(jnp.bfloat16)


def join_rows(packed, count):
    return [
        packed[3 * i : 3 * i + 1] + packed[3 * i + 1 : 3 * i + 2] + packed[3 * i + 2 : 3 * i + 3]
        for i in range(count)
    ]


def store_rows(chunks, rows, first, values):
    done = 0
    while done < values.shape[0]:
        chunk, at = divmod(first + done, rows)
        count = min(rows - at, values.shape[0] - done)
        chunks[chunk, pl.ds(at, count)] = values[done : done + count]
        done += count


def grad_kernel(
    odd, even, normed, pre, sums, temporal, grads
):
    frames, out_rows, out_cols, channels = normed.shape
    lanes = channels // GROUPS
    members = sums.shape[0] * frames * out_rows * out_cols * lanes
    clip = jnp.sum(sums[...], axis=0)
    inv_std = sums[0, 4:5]
    group = group_spread(clip, lanes) * inv_std / members
    group_shift, group_gain = group[2:3], group[3:4]
    flat = (out_rows * out_cols, channels)
    rows = grads.shape[1] - EXTRA
    backs = []
    for frame in range(frames):
        back = (
            pre[frame].reshape(flat) - group_shift - normed[frame].reshape(flat) * group_gain
        )
        backs.append(back.astype(jnp.bfloat16).T)
    backs = jnp.concatenate(backs, axis=1)
    def turned(columns, blocks):
        part = dot(backs, columns)
        for side, block in enumerate(blocks):
            value = part[:, side * channels : (side + 1) * channels].astype(jnp.bfloat16).T
            store_rows(grads, rows, block * channels, value)

    def columns_of(tap, lanes):
        source = even[:, :, :, lanes] if tap == 1 else None
        if source is None:
            source = odd[:, tap // 2 : tap // 2 + out_rows, :, lanes]
        return source.reshape(frames * out_rows * out_cols, -1)

    for tap in range(3):
        turned(columns_of(tap, slice(0, 2 * channels)), (3 * tap, 3 * tap + 1))
    last = slice(2 * channels, 3 * channels)
    turned(jnp.concatenate([columns_of(0, last), columns_of(1, last)], axis=1), (2, 5))
    turned(columns_of(2, last), (8,))
    for tap in range(3):
        block = temporal[pl.ds(tap * channels, channels)]
        store_rows(grads, rows, (9 + tap) * channels, block)
    rest = grads.shape[0] * rows - 12 * channels
    if rest:
        store_rows(grads, rows, 12 * channels, jnp.zeros((rest, channels), jnp.bfloat16))
    share = clip * (1.0 / sums.shape[0])
    extra = split_rows([share[1:2], share[0:1]], EXTRA)
    for chunk in range(grads.shape[0]):
        grads[chunk, pl.ds(rows, EXTRA)] = extra


def total_of(arrived, first, count):
    total = arrived[0, pl.ds(first, count)].astype(jnp.float32)
    for chunk in range(1, arrived.shape[0]):
        total += arrived[chunk, pl.ds(first, count)].astype(jnp.float32)
    return total


def half_kernel(arrived, chunk):
    count = chunk.shape[0] - EXTRA
    chunk[pl.ds(0, count)] = total_of(arrived, 0, count).astype(jnp.bfloat16)
    sums = join_rows(total_of(arrived, count, EXTRA), 2)
    chunk[pl.ds(count, EXTRA)] = split_rows(sums, EXTRA)


def sum_kernel(mine, other, spread, totals):
    count = spread.shape[1]
    wide = [source[...].astype(jnp.float32) for source in (mine, other)]
    total = (wide[0][:count] + wide[1][:count]).astype(jnp.bfloat16)
    for slot in range(spread.shape[0]):
        spread[slot] = total
    sums = [join_rows(source[count:], 2) for source in wide]
    row = lax.broadcasted_iota(jnp.int32, totals.shape, 0)
    totals[...] = jnp.where(row == 0, sums[0][0] + sums[1][0], sums[0][1] + sums[1][1])


def final_kernel(arrived, totals, grad_spatial, grad_temporal, grad_gain, grad_shift):
    grad_gain[...] = totals[0:1]
    grad_shift[...] = totals[1:2]
    rows = grad_spatial.shape[0]
    grad_spatial[...] = arrived[pl.ds(0, rows)].astype(jnp.float32)
    grad_temporal[...] = arrived[pl.ds(rows, grad_temporal.shape[0])].astype(jnp.float32)


def encode_kernel(per_clip, act, halo, weights, encoded):
    frames, out_rows, out_cols, channels = act.shape
    not_first = lax.rem(lax.axis_index("seq"), per_clip) != 0
    flat = (STEP_ROWS * out_cols, channels)
    for frame in range(frames):

        def one(step, frame=frame):
            rows = pl.ds(step * STEP_ROWS, STEP_ROWS)
            total = None
            for tap in range(3):
                if frame >= tap:
                    source = act[frame - tap, rows]
                else:
                    source = halo[frames + frame - tap, rows]
                    source = jnp.where(not_first, source, jnp.zeros_like(source))
                term = dot(source.reshape(flat), weights[tap])
                total = term if total is None else total + term
            encoded[frame, rows] = total.astype(jnp.bfloat16).reshape(
                STEP_ROWS, out_cols, channels
            )

        each(out_rows // STEP_ROWS, one)


def on_device(video_in, w_spatial, w_temporal, norm_gain, norm_shift, cotangent):
    frames, height, width, channels = video_in.shape[1:]
    out_rows, out_cols = height // 2, width // 2
    dp_size, seq_size = lax.axis_size("dp"), lax.axis_size("seq")
    devices = dp_size * seq_size
    per_clip = FRAMES // frames
    assert frames >= 2 and FRAMES % frames == 0
    loss_scale = float(devices * frames * out_rows * out_cols) ** (-0.5)
    shape = (frames, out_rows, out_cols, channels)
    positions = frames * out_rows * out_cols
    video = video_in[0]
    cot = cotangent[0]
    f32, bf16 = jnp.float32, jnp.bfloat16
    struct = jax.ShapeDtypeStruct

    ahead_pairs = [
        (s, s // per_clip * per_clip + (s + 1) % per_clip) for s in range(seq_size)
    ]
    back_pairs = [(target, source) for source, target in ahead_pairs]
    clips = [list(range(first, first + per_clip)) for first in range(0, seq_size, per_clip)]

    def exchange(value, axes, groups=None):
        return lax.all_to_all(value, axes, 0, 0, axis_index_groups=groups, tiled=True)

    gate = pl.pallas_call(
        open_kernel,
        out_shape=pltpu.VMEM((8, channels), f32),
        out_specs=WHOLE,
        cost_estimate=pl.CostEstimate(
            flops=2 * positions * 9 * channels * channels,
            bytes_accessed=2 * video.size,
            transcendentals=0,
        ),
    )()
    cot_out, gate = lax.optimization_barrier((cot, gate))
    cot_halo = lax.ppermute(cot_out, "seq", back_pairs)

    pieces = 2 * frames
    def far(value):
        return pltpu.with_memory_space_constraint(value, pltpu.HBM)

    spatial, stats, odd, even, params = call(
        functools.partial(conv_kernel, pieces),
        (
            struct(shape, f32),
            struct((per_clip, 8, channels), f32),
            struct((frames, out_rows + 1, out_cols, 3 * channels), bf16),
            struct((frames, out_rows, out_cols, 3 * channels), bf16),
            struct((8, channels), f32),
        ),
        (
            gate,
            video,
            far(w_spatial.reshape(9 * channels, channels)),
            far(norm_gain[None]),
            far(norm_shift[None]),
        ),
        specs=[WHOLE] * 2 + [FAR] * 3,
        scratch=[
            pltpu.VMEM((4 * STEP_ROWS, 8 + width, channels), f32),
            pltpu.VMEM((9 * channels, channels), bf16),
            pltpu.SemaphoreType.DMA((3,)),
        ],
        flops=2 * positions * 9 * channels * channels,
    )
    stats = exchange(stats, "seq", clips)
    act, normed, slope, scales = call(
        functools.partial(act_kernel, loss_scale),
        (
            struct(shape, bf16),
            struct(shape, f32),
            struct(shape, f32),
            struct((8, channels), f32),
        ),
        (spatial, stats, params),
    )
    act_halo = lax.ppermute(act, "seq", ahead_pairs)
    pre, temporal, own = call(
        functools.partial(back_kernel, loss_scale),
        (
            struct(shape, f32),
            struct((3 * channels, channels), bf16),
            struct((per_clip, 8, channels), f32),
        ),
        (cot, cot_halo, w_temporal, scales, normed, slope, act),
        scratch=[pltpu.VMEM((2,) + shape[1:], bf16)],
        flops=2 * positions * 6 * channels * channels,
    )
    sums = exchange(own, "seq", clips)
    halves = 2 if seq_size % 2 == 0 else 1
    half = seq_size // halves
    near = [
        [d * seq_size + s for d in range(dp_size) for s in range(first, first + half)]
        for first in range(0, seq_size, half)
    ]
    count = dp_size * half
    rows = -(-12 * channels // (16 * count)) * 16
    sums, act_halo = lax.optimization_barrier((sums, act_halo))
    grads = call(
        grad_kernel,
        struct((count, rows + EXTRA, channels), bf16),
        (odd, even, normed, pre, sums, temporal),
        flops=2 * positions * 9 * channels * channels,
    )
    grads = exchange(grads, ("dp", "seq"), near)
    mine = call(half_kernel, struct((rows + EXTRA, channels), bf16), (grads,))
    if halves == 2:
        other = lax.ppermute(mine, "seq", [(s, (s + half) % seq_size) for s in range(seq_size)])
    else:
        other = jnp.zeros_like(mine)
    act, act_halo, _ = lax.optimization_barrier((act, act_halo, mine))
    encoded = call(
        functools.partial(encode_kernel, per_clip),
        struct(shape, bf16),
        (act, act_halo, w_temporal),
        flops=2 * positions * 3 * channels * channels,
    )
    other, encoded = lax.optimization_barrier((other, encoded))
    grads, totals = call(
        sum_kernel,
        (struct((count, rows, channels), bf16), struct((8, channels), f32)),
        (mine, other),
    )
    grads = exchange(grads, ("dp", "seq"), near)
    grad_spatial, grad_temporal, grad_gain, grad_shift = call(
        final_kernel,
        (
            struct((9 * channels, channels), f32),
            struct((3 * channels, channels), f32),
            struct((1, channels), f32),
            struct((1, channels), f32),
        ),
        (grads.reshape(count * rows, channels), totals),
    )
    return (
        encoded[None],
        grad_spatial.reshape(3, 3, channels, channels),
        grad_temporal.reshape(3, channels, channels),
        grad_gain[0],
        grad_shift[0],
    )


def solution(mesh):
    placed = P("dp", "seq", None, None, None)
    return jax.shard_map(
        on_device,
        mesh=mesh,
        in_specs=(placed, P(), P(), P(), P(), placed),
        out_specs=(placed, P(), P(), P(), P()),
        check_vma=False,
    )
```

```python
import functools
import math

import jax
import jax.numpy as jnp
from jax import lax
from jax.experimental import pallas as pl
from jax.experimental.pallas import tpu as pltpu
from jax.sharding import PartitionSpec as P

GROUPS = 32
FRAMES = 8
STEP_ROWS = 8
EXTRA = 8
WEIGHT_PARTS = 6
SPARE_BYTES = 4 * 1024 * 1024

WHOLE = pl.BlockSpec(memory_space=pltpu.VMEM)
FAR = pl.BlockSpec(memory_space=pltpu.HBM)


def dot(left, right):
    return jnp.dot(left, right, preferred_element_type=jnp.float32)


def dot_transposed(left, right):
    return lax.dot_general(
        left, right, (((1,), (1,)), ((), ())), preferred_element_type=jnp.float32
    )


def each(count, body):
    if count <= 8:
        for step in range(count):
            body(step)
    else:
        lax.fori_loop(0, count, lambda step, carry: (body(step), carry)[1], 0)


def call(kernel, out_shape, operands, specs=None, scratch=(), flops=0):
    sizes = [value.size * value.dtype.itemsize for value in operands]
    sizes += [value.size * value.dtype.itemsize for value in jax.tree.leaves(out_shape)]
    held = sum(math.prod(item.shape) * 4 for item in scratch if hasattr(item, "shape"))
    return pl.pallas_call(
        kernel,
        out_shape=out_shape,
        in_specs=specs or [WHOLE] * len(operands),
        out_specs=jax.tree.map(lambda _: WHOLE, out_shape),
        scratch_shapes=list(scratch),
        compiler_params=pltpu.CompilerParams(vmem_limit_bytes=sum(sizes) + held + SPARE_BYTES),
        cost_estimate=pl.CostEstimate(
            flops=flops, bytes_accessed=sum(sizes), transcendentals=0
        ),
    )(*operands)


def group_spread(values, lanes):
    channels = values.shape[-1]
    place = lax.rem(lax.broadcasted_iota(jnp.int32, values.shape, 1), lanes)
    total = values
    for shift in range(1, lanes):
        ahead = pltpu.roll(values, channels - shift, 1)
        behind = pltpu.roll(values, shift, 1)
        total += jnp.where(place < lanes - shift, ahead, 0.0)
        total += jnp.where(place >= shift, behind, 0.0)
    return total


def open_kernel(gate):
    gate[...] = jnp.zeros(gate.shape, gate.dtype)


def conv_kernel(
    pieces, blank, video, weights_far, gain_far, shift_far, spatial, stats, odd, even, params, wide,
    weights, arrived,
):
    frames, height, width, channels = video.shape
    out_rows, out_cols = height // 2, width // 2
    positions = frames * out_rows * out_cols
    half = height * frames // pieces
    params[...] = blank[...]
    part = weights.shape[0] // WEIGHT_PARTS
    pairs = [
        (weights_far.at[pl.ds(index * part, part)], weights.at[pl.ds(index * part, part)])
        for index in range(WEIGHT_PARTS)
    ]
    pairs += [(gain_far, params.at[0:1]), (shift_far, params.at[1:2])]
    copies = [
        pltpu.make_async_copy(source, target, arrived.at[index])
        for index, (source, target) in enumerate(pairs)
    ]
    for copy in copies:
        copy.start()
    for slot in range(wide.shape[0]):
        wide[slot, 0:8] = jnp.zeros((8, channels), jnp.float32)
    for frame in range(frames):
        odd[frame, 0] = jnp.zeros((out_cols, 3 * channels), jnp.bfloat16)
    flat = (STEP_ROWS * out_cols, 3 * channels)
    steps = half // 2 // STEP_ROWS

    def place(piece, step):
        return piece * half // height, piece * half % height // 2 + step * STEP_ROWS

    def separate(piece, step):
        frame, first = place(piece, step)
        base = piece % 2 * 2 * STEP_ROWS
        for line in range(2 * STEP_ROWS):
            wide[base + line, 8 : 8 + width] = video[frame, 2 * first + line].astype(jnp.float32)
        for line in range(2 * STEP_ROWS):
            for tap in range(3):
                value = wide[base + line, pl.ds(7 + tap, out_cols, stride=2), :]
                lanes = slice(tap * channels, (tap + 1) * channels)
                if line % 2:
                    odd[frame, first + line // 2 + 1, :, lanes] = value.astype(jnp.bfloat16)
                else:
                    even[frame, first + line // 2, :, lanes] = value.astype(jnp.bfloat16)

    def multiply(piece, step):
        frame, first = place(piece, step)
        sources = (
            odd[frame, pl.ds(first, STEP_ROWS)],
            even[frame, pl.ds(first, STEP_ROWS)],
            odd[frame, pl.ds(first + 1, STEP_ROWS)],
        )
        side_by_side = jnp.concatenate([source.reshape(flat) for source in sources], axis=1)
        total = dot(side_by_side, weights[...])
        spatial[frame, pl.ds(first, STEP_ROWS)] = total.reshape(STEP_ROWS, out_cols, channels)
        return total

    def fold(values):
        return values.reshape(-1, 8, channels).sum(axis=0)

    def over_steps(piece, term, start):
        if steps <= 8:
            for step in range(steps):
                start = jax.tree.map(jnp.add, start, term(piece, step))
            return start
        return lax.fori_loop(
            0, steps, lambda step, sums: jax.tree.map(jnp.add, sums, term(piece, step)), start
        )

    zero = jnp.zeros((8, channels), jnp.float32)

    def first_sum(piece, step):
        return fold(multiply(piece, step))

    def first_moments(piece, step):
        frame, first = place(piece, step)
        off = spatial[frame, pl.ds(first, STEP_ROWS)].reshape(-1, channels) - near
        return fold(off), fold(off * off)

    def moments(piece, step):
        off = multiply(piece, step) - near
        return fold(off), fold(off * off)

    for piece in range(pieces):
        each(steps, functools.partial(separate, piece))
    for copy in copies[:WEIGHT_PARTS]:
        copy.wait()
    near = over_steps(0, first_sum, zero).sum(axis=0, keepdims=True) * (pieces / positions)
    sums = over_steps(0, first_moments, (zero, zero))
    for piece in range(1, pieces - 1):
        sums = over_steps(piece, moments, sums)
    sums = over_steps(pieces - 1, moments, sums)
    off = sums[0].sum(axis=0, keepdims=True) / positions
    mean = near + off
    square = sums[1].sum(axis=0, keepdims=True) - positions * off * off
    row = lax.broadcasted_iota(jnp.int32, (8, channels), 0)
    packed = jnp.where(row == 0, mean, jnp.where(row == 1, square, 0.0))
    for slot in range(stats.shape[0]):
        stats[slot] = packed
    for copy in copies[WEIGHT_PARTS:]:
        copy.wait()

def clip_norm(stats, positions, lanes):
    cells = stats.shape[0] * lanes
    means = [stats[member, 0:1] for member in range(stats.shape[0])]
    squares = [stats[member, 1:2] for member in range(stats.shape[0])]
    mean = group_spread(jnp.broadcast_to(sum(means), (8, means[0].shape[-1])), lanes)[0:1] / cells
    square = sum(squares)
    for value in means:
        square = square + positions * (value - mean) ** 2
    square = group_spread(jnp.broadcast_to(square, (8, square.shape[-1])), lanes)[0:1]
    return mean, lax.rsqrt(square / (cells * positions) + 1e-05)


def act_kernel(loss_scale, spatial, stats, params, act, normed, slope, scales):
    frames, out_rows, out_cols, channels = spatial.shape
    positions = frames * out_rows * out_cols
    mean, inv_std = clip_norm(stats, positions, channels // GROUPS)
    gain, shift = params[0:1], params[1:2]
    row = lax.broadcasted_iota(jnp.int32, (8, channels), 0)
    scales[...] = jnp.where(row == 0, inv_std, gain)
    flat = (STEP_ROWS * out_cols, channels)
    shaped = (STEP_ROWS, out_cols, channels)
    for frame in range(frames):

        def one(step, frame=frame):
            rows = pl.ds(step * STEP_ROWS, STEP_ROWS)
            norm = (spatial[frame, rows].reshape(flat) - mean) * inv_std
            before = norm * gain + shift
            sig = 0.5 + 0.5 * jnp.tanh(0.5 * before)
            act[frame, rows] = (before * sig).astype(jnp.bfloat16).reshape(shaped)
            normed[frame, rows] = norm.reshape(shaped)
            slope[frame, rows] = (loss_scale * sig * (1.0 + before * (1.0 - sig))).reshape(shaped)

        each(out_rows // STEP_ROWS, one)


def back_kernel(
    loss_scale, cot, arrived, weights, scales, normed, slope, act, pre, temporal, sums, halo
):
    frames, out_rows, out_cols, channels = cot.shape
    inv_std, gain = scales[0:1], scales[1:2]
    per_clip = sums.shape[0]
    not_last = lax.rem(lax.axis_index("seq"), per_clip) != per_clip - 1
    for frame in range(2):
        value = arrived[frame]
        halo[frame] = jnp.where(not_last, value, jnp.zeros_like(value))
    turned_weights = jnp.concatenate([weights[tap] for tap in range(3)], axis=1)
    flat = (STEP_ROWS * out_cols, channels)
    shaped = (STEP_ROWS, out_cols, channels)
    sums_shift = jnp.zeros((8, channels), jnp.float32)
    sums_gain = jnp.zeros((8, channels), jnp.float32)

    def fold(values):
        return values.reshape(-1, 8, channels).sum(axis=0)

    for frame in range(frames):

        def cot_block(later, rows, shape, frame=frame):
            if frame + later < frames:
                return cot[frame + later, rows].reshape(shape)
            return halo[frame + later - frames, rows].reshape(shape)

        def one(step, carry, frame=frame):
            rows = pl.ds(step * STEP_ROWS, STEP_ROWS)
            cots = jnp.concatenate([cot_block(later, rows, flat) for later in range(3)], axis=1)
            back = dot_transposed(cots, turned_weights)
            back = back.astype(jnp.bfloat16).astype(jnp.float32)
            back_pre = back * slope[frame, rows].reshape(flat)
            norm = normed[frame, rows].reshape(flat)
            pre[frame, rows] = (back_pre * (gain * inv_std)).reshape(shaped)
            return (carry[0] + fold(back_pre), carry[1] + fold(back_pre * norm))

        steps = out_rows // STEP_ROWS
        if steps <= 4:
            for step in range(steps):
                sums_shift, sums_gain = one(step, (sums_shift, sums_gain))
        else:
            sums_shift, sums_gain = lax.fori_loop(0, steps, one, (sums_shift, sums_gain))

    sums_shift = sums_shift.sum(axis=0, keepdims=True)
    sums_gain = sums_gain.sum(axis=0, keepdims=True)
    row = lax.broadcasted_iota(jnp.int32, (8, channels), 0)
    packed = jnp.zeros((8, channels), jnp.float32)
    for index, value in enumerate(
        (sums_shift, sums_gain, gain * sums_shift, gain * sums_gain, inv_std)
    ):
        packed = jnp.where(row == index, value, packed)
    for slot in range(sums.shape[0]):
        sums[slot] = packed

    all_rows = (out_rows * out_cols, channels)
    total = None
    for frame in range(frames):
        cots = jnp.concatenate(
            [
                (cot[frame + later] if frame + later < frames else halo[frame + later - frames])
                .reshape(all_rows)
                for later in range(3)
            ],
            axis=1,
        )
        term = dot(act[frame].reshape(all_rows).T, cots)
        total = term if total is None else total + term
    for later in range(3):
        block = total[:, later * channels : (later + 1) * channels] * loss_scale
        temporal[pl.ds(later * channels, channels)] = block.astype(jnp.bfloat16)


def split_rows(values, rows):
    pieces = []
    for value in values:
        rest = value
        for _ in range(3):
            piece = rest.astype(jnp.bfloat16).astype(jnp.float32)
            pieces.append(piece)
            rest = rest - piece
    row = lax.broadcasted_iota(jnp.int32, (rows, values[0].shape[-1]), 0)
    packed = jnp.zeros((rows, values[0].shape[-1]), jnp.float32)
    for index, piece in enumerate(pieces):
        packed = jnp.where(row == index, piece, packed)
    return packed.astype(jnp.bfloat16)


def join_rows(packed, count):
    return [
        packed[3 * i : 3 * i + 1] + packed[3 * i + 1 : 3 * i + 2] + packed[3 * i + 2 : 3 * i + 3]
        for i in range(count)
    ]


def store_rows(chunks, rows, first, values):
    done = 0
    while done < values.shape[0]:
        chunk, at = divmod(first + done, rows)
        count = min(rows - at, values.shape[0] - done)
        chunks[chunk, pl.ds(at, count)] = values[done : done + count]
        done += count


def grad_kernel(
    odd, even, normed, pre, sums, temporal, grads
):
    frames, out_rows, out_cols, channels = normed.shape
    lanes = channels // GROUPS
    members = sums.shape[0] * frames * out_rows * out_cols * lanes
    clip = jnp.sum(sums[...], axis=0)
    inv_std = sums[0, 4:5]
    group = group_spread(clip, lanes) * inv_std / members
    group_shift, group_gain = group[2:3], group[3:4]
    flat = (out_rows * out_cols, channels)
    rows = grads.shape[1] - EXTRA
    backs = []
    for frame in range(frames):
        back = (
            pre[frame].reshape(flat) - group_shift - normed[frame].reshape(flat) * group_gain
        )
        backs.append(back.astype(jnp.bfloat16).T)
    backs = jnp.concatenate(backs, axis=1)
    def turned(columns, blocks):
        part = dot(backs, columns)
        for side, block in enumerate(blocks):
            value = part[:, side * channels : (side + 1) * channels].astype(jnp.bfloat16).T
            store_rows(grads, rows, block * channels, value)

    def columns_of(tap, lanes):
        source = even[:, :, :, lanes] if tap == 1 else None
        if source is None:
            source = odd[:, tap // 2 : tap // 2 + out_rows, :, lanes]
        return source.reshape(frames * out_rows * out_cols, -1)

    for tap in range(3):
        turned(columns_of(tap, slice(0, 2 * channels)), (3 * tap, 3 * tap + 1))
    last = slice(2 * channels, 3 * channels)
    turned(jnp.concatenate([columns_of(0, last), columns_of(1, last)], axis=1), (2, 5))
    turned(columns_of(2, last), (8,))
    for tap in range(3):
        block = temporal[pl.ds(tap * channels, channels)]
        store_rows(grads, rows, (9 + tap) * channels, block)
    rest = grads.shape[0] * rows - 12 * channels
    if rest:
        store_rows(grads, rows, 12 * channels, jnp.zeros((rest, channels), jnp.bfloat16))
    share = clip * (1.0 / sums.shape[0])
    extra = split_rows([share[1:2], share[0:1]], EXTRA)
    for chunk in range(grads.shape[0]):
        grads[chunk, pl.ds(rows, EXTRA)] = extra


def total_of(arrived, first, count):
    total = arrived[0, pl.ds(first, count)].astype(jnp.float32)
    for chunk in range(1, arrived.shape[0]):
        total += arrived[chunk, pl.ds(first, count)].astype(jnp.float32)
    return total


def half_kernel(arrived, chunk):
    count = chunk.shape[0] - EXTRA
    chunk[pl.ds(0, count)] = total_of(arrived, 0, count).astype(jnp.bfloat16)
    sums = join_rows(total_of(arrived, count, EXTRA), 2)
    chunk[pl.ds(count, EXTRA)] = split_rows(sums, EXTRA)


def sum_kernel(mine, other, spread, totals):
    count = spread.shape[1]
    wide = [source[...].astype(jnp.float32) for source in (mine, other)]
    total = (wide[0][:count] + wide[1][:count]).astype(jnp.bfloat16)
    for slot in range(spread.shape[0]):
        spread[slot] = total
    sums = [join_rows(source[count:], 2) for source in wide]
    row = lax.broadcasted_iota(jnp.int32, totals.shape, 0)
    totals[...] = jnp.where(row == 0, sums[0][0] + sums[1][0], sums[0][1] + sums[1][1])


def final_kernel(arrived, totals, grad_spatial, grad_temporal, grad_gain, grad_shift):
    grad_gain[...] = totals[0:1]
    grad_shift[...] = totals[1:2]
    rows = grad_spatial.shape[0]
    grad_spatial[...] = arrived[pl.ds(0, rows)].astype(jnp.float32)
    grad_temporal[...] = arrived[pl.ds(rows, grad_temporal.shape[0])].astype(jnp.float32)


def encode_kernel(per_clip, act, halo, weights, encoded):
    frames, out_rows, out_cols, channels = act.shape
    not_first = lax.rem(lax.axis_index("seq"), per_clip) != 0
    flat = (STEP_ROWS * out_cols, channels)
    for frame in range(frames):

        def one(step, frame=frame):
            rows = pl.ds(step * STEP_ROWS, STEP_ROWS)
            total = None
            for tap in range(3):
                if frame >= tap:
                    source = act[frame - tap, rows]
                else:
                    source = halo[frames + frame - tap, rows]
                    source = jnp.where(not_first, source, jnp.zeros_like(source))
                term = dot(source.reshape(flat), weights[tap])
                total = term if total is None else total + term
            encoded[frame, rows] = total.astype(jnp.bfloat16).reshape(
                STEP_ROWS, out_cols, channels
            )

        each(out_rows // STEP_ROWS, one)


def on_device(video_in, w_spatial, w_temporal, norm_gain, norm_shift, cotangent):
    frames, height, width, channels = video_in.shape[1:]
    out_rows, out_cols = height // 2, width // 2
    dp_size, seq_size = lax.axis_size("dp"), lax.axis_size("seq")
    devices = dp_size * seq_size
    per_clip = FRAMES // frames
    assert frames >= 2 and FRAMES % frames == 0
    loss_scale = float(devices * frames * out_rows * out_cols) ** (-0.5)
    shape = (frames, out_rows, out_cols, channels)
    positions = frames * out_rows * out_cols
    video = video_in[0]
    cot = cotangent[0]
    f32, bf16 = jnp.float32, jnp.bfloat16
    struct = jax.ShapeDtypeStruct

    ahead_pairs = [
        (s, s // per_clip * per_clip + (s + 1) % per_clip) for s in range(seq_size)
    ]
    back_pairs = [(target, source) for source, target in ahead_pairs]
    clips = [list(range(first, first + per_clip)) for first in range(0, seq_size, per_clip)]

    def exchange(value, axes, groups=None):
        return lax.all_to_all(value, axes, 0, 0, axis_index_groups=groups, tiled=True)

    gate = pl.pallas_call(
        open_kernel,
        out_shape=pltpu.VMEM((8, channels), f32),
        out_specs=WHOLE,
        cost_estimate=pl.CostEstimate(
            flops=2 * positions * 9 * channels * channels,
            bytes_accessed=2 * video.size,
            transcendentals=0,
        ),
    )()
    cot_out, gate = lax.optimization_barrier((cot, gate))
    cot_halo = lax.ppermute(cot_out, "seq", back_pairs)

    pieces = 2 * frames
    def far(value):
        return pltpu.with_memory_space_constraint(value, pltpu.HBM)

    spatial, stats, odd, even, params = call(
        functools.partial(conv_kernel, pieces),
        (
            struct(shape, f32),
            struct((per_clip, 8, channels), f32),
            struct((frames, out_rows + 1, out_cols, 3 * channels), bf16),
            struct((frames, out_rows, out_cols, 3 * channels), bf16),
            struct((8, channels), f32),
        ),
        (
            gate,
            video,
            far(w_spatial.reshape(9 * channels, channels)),
            far(norm_gain[None]),
            far(norm_shift[None]),
        ),
        specs=[WHOLE] * 2 + [FAR] * 3,
        scratch=[
            pltpu.VMEM((4 * STEP_ROWS, 8 + width, channels), f32),
            pltpu.VMEM((9 * channels, channels), bf16),
            pltpu.SemaphoreType.DMA((WEIGHT_PARTS + 2,)),
        ],
        flops=2 * positions * 9 * channels * channels,
    )
    stats = exchange(stats, "seq", clips)
    act, normed, slope, scales = call(
        functools.partial(act_kernel, loss_scale),
        (
            struct(shape, bf16),
            struct(shape, f32),
            struct(shape, f32),
            struct((8, channels), f32),
        ),
        (spatial, stats, params),
    )
    act_halo = lax.ppermute(act, "seq", ahead_pairs)
    pre, temporal, own = call(
        functools.partial(back_kernel, loss_scale),
        (
            struct(shape, f32),
            struct((3 * channels, channels), bf16),
            struct((per_clip, 8, channels), f32),
        ),
        (cot, cot_halo, w_temporal, scales, normed, slope, act),
        scratch=[pltpu.VMEM((2,) + shape[1:], bf16)],
        flops=2 * positions * 6 * channels * channels,
    )
    sums = exchange(own, "seq", clips)
    halves = 2 if seq_size % 2 == 0 else 1
    half = seq_size // halves
    near = [
        [d * seq_size + s for d in range(dp_size) for s in range(first, first + half)]
        for first in range(0, seq_size, half)
    ]
    count = dp_size * half
    rows = -(-12 * channels // (16 * count)) * 16
    sums, act_halo = lax.optimization_barrier((sums, act_halo))
    grads = call(
        grad_kernel,
        struct((count, rows + EXTRA, channels), bf16),
        (odd, even, normed, pre, sums, temporal),
        flops=2 * positions * 9 * channels * channels,
    )
    grads = exchange(grads, ("dp", "seq"), near)
    mine = call(half_kernel, struct((rows + EXTRA, channels), bf16), (grads,))
    if halves == 2:
        other = lax.ppermute(mine, "seq", [(s, (s + half) % seq_size) for s in range(seq_size)])
    else:
        other = jnp.zeros_like(mine)
    act, act_halo, _ = lax.optimization_barrier((act, act_halo, mine))
    encoded = call(
        functools.partial(encode_kernel, per_clip),
        struct(shape, bf16),
        (act, act_halo, w_temporal),
        flops=2 * positions * 3 * channels * channels,
    )
    other, encoded = lax.optimization_barrier((other, encoded))
    grads, totals = call(
        sum_kernel,
        (struct((count, rows, channels), bf16), struct((8, channels), f32)),
        (mine, other),
    )
    grads = exchange(grads, ("dp", "seq"), near)
    grad_spatial, grad_temporal, grad_gain, grad_shift = call(
        final_kernel,
        (
            struct((9 * channels, channels), f32),
            struct((3 * channels, channels), f32),
            struct((1, channels), f32),
            struct((1, channels), f32),
        ),
        (grads.reshape(count * rows, channels), totals),
    )
    return (
        encoded[None],
        grad_spatial.reshape(3, 3, channels, channels),
        grad_temporal.reshape(3, channels, channels),
        grad_gain[0],
        grad_shift[0],
    )


def solution(mesh):
    placed = P("dp", "seq", None, None, None)
    return jax.shard_map(
        on_device,
        mesh=mesh,
        in_specs=(placed, P(), P(), P(), P(), placed),
        out_specs=(placed, P(), P(), P(), P()),
        check_vma=False,
    )
```

```python
import functools
import math

import jax
import jax.numpy as jnp
from jax import lax
from jax.experimental import pallas as pl
from jax.experimental.pallas import tpu as pltpu
from jax.sharding import PartitionSpec as P

GROUPS = 32
FRAMES = 8
STEP_ROWS = 16
EXTRA = 8
SPARE_BYTES = 4 * 1024 * 1024

WHOLE = pl.BlockSpec(memory_space=pltpu.VMEM)
FAR = pl.BlockSpec(memory_space=pltpu.HBM)


def dot(left, right):
    return jnp.dot(left, right, preferred_element_type=jnp.float32)


def dot_transposed(left, right):
    return lax.dot_general(
        left, right, (((1,), (1,)), ((), ())), preferred_element_type=jnp.float32
    )


def each(count, body):
    if count <= 8:
        for step in range(count):
            body(step)
    else:
        lax.fori_loop(0, count, lambda step, carry: (body(step), carry)[1], 0)


def call(kernel, out_shape, operands, specs=None, scratch=(), flops=0):
    sizes = [value.size * value.dtype.itemsize for value in operands]
    sizes += [value.size * value.dtype.itemsize for value in jax.tree.leaves(out_shape)]
    held = sum(math.prod(item.shape) * 4 for item in scratch if hasattr(item, "shape"))
    return pl.pallas_call(
        kernel,
        out_shape=out_shape,
        in_specs=specs or [WHOLE] * len(operands),
        out_specs=jax.tree.map(lambda _: WHOLE, out_shape),
        scratch_shapes=list(scratch),
        compiler_params=pltpu.CompilerParams(vmem_limit_bytes=sum(sizes) + held + SPARE_BYTES),
        cost_estimate=pl.CostEstimate(
            flops=flops, bytes_accessed=sum(sizes), transcendentals=0
        ),
    )(*operands)


def group_spread(values, lanes):
    channels = values.shape[-1]
    place = lax.rem(lax.broadcasted_iota(jnp.int32, values.shape, 1), lanes)
    total = values
    for shift in range(1, lanes):
        ahead = pltpu.roll(values, channels - shift, 1)
        behind = pltpu.roll(values, shift, 1)
        total += jnp.where(place < lanes - shift, ahead, 0.0)
        total += jnp.where(place >= shift, behind, 0.0)
    return total


def open_kernel(gate):
    gate[...] = jnp.zeros(gate.shape, gate.dtype)


def conv_kernel(
    pieces, blank, video, weights_far, gain_far, shift_far, spatial, stats, odd, even, params, wide,
    weights, arrived,
):
    frames, height, width, channels = video.shape
    out_rows, out_cols = height // 2, width // 2
    positions = frames * out_rows * out_cols
    half = height * frames // pieces
    params[...] = blank[...]
    copies = [
        pltpu.make_async_copy(source, target, arrived.at[index])
        for index, (source, target) in enumerate(
            ((weights_far, weights), (gain_far, params.at[0:1]), (shift_far, params.at[1:2]))
        )
    ]
    for copy in copies:
        copy.start()
    for slot in range(wide.shape[0]):
        wide[slot, 0:8] = jnp.zeros((8, channels), jnp.float32)
    for frame in range(frames):
        odd[frame, 0] = jnp.zeros((out_cols, 3 * channels), jnp.bfloat16)
    flat = (STEP_ROWS * out_cols, 3 * channels)
    steps = half // 2 // STEP_ROWS

    def place(piece, step):
        return piece * half // height, piece * half % height // 2 + step * STEP_ROWS

    def separate(piece, step):
        frame, first = place(piece, step)
        base = piece % 2 * 2 * STEP_ROWS
        for line in range(2 * STEP_ROWS):
            wide[base + line, 8 : 8 + width] = video[frame, 2 * first + line].astype(jnp.float32)
        for line in range(2 * STEP_ROWS):
            for tap in range(3):
                value = wide[base + line, pl.ds(7 + tap, out_cols, stride=2), :]
                lanes = slice(tap * channels, (tap + 1) * channels)
                if line % 2:
                    odd[frame, first + line // 2 + 1, :, lanes] = value.astype(jnp.bfloat16)
                else:
                    even[frame, first + line // 2, :, lanes] = value.astype(jnp.bfloat16)

    def multiply(piece, step):
        frame, first = place(piece, step)
        sources = (
            odd[frame, pl.ds(first, STEP_ROWS)],
            even[frame, pl.ds(first, STEP_ROWS)],
            odd[frame, pl.ds(first + 1, STEP_ROWS)],
        )
        side_by_side = jnp.concatenate([source.reshape(flat) for source in sources], axis=1)
        total = dot(side_by_side, weights[...])
        spatial[frame, pl.ds(first, STEP_ROWS)] = total.reshape(STEP_ROWS, out_cols, channels)
        return total

    def fold(values):
        return values.reshape(-1, 8, channels).sum(axis=0)

    def over_steps(piece, term, start):
        if steps <= 8:
            for step in range(steps):
                start = jax.tree.map(jnp.add, start, term(piece, step))
            return start
        return lax.fori_loop(
            0, steps, lambda step, sums: jax.tree.map(jnp.add, sums, term(piece, step)), start
        )

    zero = jnp.zeros((8, channels), jnp.float32)

    def first_sum(piece, step):
        return fold(multiply(piece, step))

    def first_moments(piece, step):
        frame, first = place(piece, step)
        off = spatial[frame, pl.ds(first, STEP_ROWS)].reshape(-1, channels) - near
        return fold(off), fold(off * off)

    def moments(piece, step):
        off = multiply(piece, step) - near
        return fold(off), fold(off * off)

    for piece in range(pieces):
        each(steps, functools.partial(separate, piece))
    copies[0].wait()
    near = over_steps(0, first_sum, zero).sum(axis=0, keepdims=True) * (pieces / positions)
    sums = over_steps(0, first_moments, (zero, zero))
    for piece in range(1, pieces - 1):
        sums = over_steps(piece, moments, sums)
    sums = over_steps(pieces - 1, moments, sums)
    off = sums[0].sum(axis=0, keepdims=True) / positions
    mean = near + off
    square = sums[1].sum(axis=0, keepdims=True) - positions * off * off
    row = lax.broadcasted_iota(jnp.int32, (8, channels), 0)
    packed = jnp.where(row == 0, mean, jnp.where(row == 1, square, 0.0))
    for slot in range(stats.shape[0]):
        stats[slot] = packed
    for copy in copies[1:]:
        copy.wait()

def clip_norm(stats, positions, lanes):
    cells = stats.shape[0] * lanes
    means = [stats[member, 0:1] for member in range(stats.shape[0])]
    squares = [stats[member, 1:2] for member in range(stats.shape[0])]
    mean = group_spread(jnp.broadcast_to(sum(means), (8, means[0].shape[-1])), lanes)[0:1] / cells
    square = sum(squares)
    for value in means:
        square = square + positions * (value - mean) ** 2
    square = group_spread(jnp.broadcast_to(square, (8, square.shape[-1])), lanes)[0:1]
    return mean, lax.rsqrt(square / (cells * positions) + 1e-05)


def act_kernel(loss_scale, spatial, stats, params, act, normed, slope, scales):
    frames, out_rows, out_cols, channels = spatial.shape
    positions = frames * out_rows * out_cols
    mean, inv_std = clip_norm(stats, positions, channels // GROUPS)
    gain, shift = params[0:1], params[1:2]
    row = lax.broadcasted_iota(jnp.int32, (8, channels), 0)
    scales[...] = jnp.where(row == 0, inv_std, gain)
    flat = (STEP_ROWS * out_cols, channels)
    shaped = (STEP_ROWS, out_cols, channels)
    for frame in range(frames):

        def one(step, frame=frame):
            rows = pl.ds(step * STEP_ROWS, STEP_ROWS)
            norm = (spatial[frame, rows].reshape(flat) - mean) * inv_std
            before = norm * gain + shift
            sig = 0.5 + 0.5 * jnp.tanh(0.5 * before)
            act[frame, rows] = (before * sig).astype(jnp.bfloat16).reshape(shaped)
            normed[frame, rows] = norm.reshape(shaped)
            slope[frame, rows] = (loss_scale * sig * (1.0 + before * (1.0 - sig))).reshape(shaped)

        each(out_rows // STEP_ROWS, one)


def back_kernel(
    loss_scale, cot, arrived, weights, scales, normed, slope, act, pre, temporal, sums, halo
):
    frames, out_rows, out_cols, channels = cot.shape
    inv_std, gain = scales[0:1], scales[1:2]
    per_clip = sums.shape[0]
    not_last = lax.rem(lax.axis_index("seq"), per_clip) != per_clip - 1
    for frame in range(2):
        value = arrived[frame]
        halo[frame] = jnp.where(not_last, value, jnp.zeros_like(value))
    turned_weights = jnp.concatenate([weights[tap] for tap in range(3)], axis=1)
    flat = (STEP_ROWS * out_cols, channels)
    shaped = (STEP_ROWS, out_cols, channels)
    sums_shift = jnp.zeros((8, channels), jnp.float32)
    sums_gain = jnp.zeros((8, channels), jnp.float32)

    def fold(values):
        return values.reshape(-1, 8, channels).sum(axis=0)

    for frame in range(frames):

        def cot_block(later, rows, shape, frame=frame):
            if frame + later < frames:
                return cot[frame + later, rows].reshape(shape)
            return halo[frame + later - frames, rows].reshape(shape)

        def one(step, carry, frame=frame):
            rows = pl.ds(step * STEP_ROWS, STEP_ROWS)
            cots = jnp.concatenate([cot_block(later, rows, flat) for later in range(3)], axis=1)
            back = dot_transposed(cots, turned_weights)
            back = back.astype(jnp.bfloat16).astype(jnp.float32)
            back_pre = back * slope[frame, rows].reshape(flat)
            norm = normed[frame, rows].reshape(flat)
            pre[frame, rows] = (back_pre * (gain * inv_std)).reshape(shaped)
            return (carry[0] + fold(back_pre), carry[1] + fold(back_pre * norm))

        steps = out_rows // STEP_ROWS
        if steps <= 4:
            for step in range(steps):
                sums_shift, sums_gain = one(step, (sums_shift, sums_gain))
        else:
            sums_shift, sums_gain = lax.fori_loop(0, steps, one, (sums_shift, sums_gain))

    sums_shift = sums_shift.sum(axis=0, keepdims=True)
    sums_gain = sums_gain.sum(axis=0, keepdims=True)
    row = lax.broadcasted_iota(jnp.int32, (8, channels), 0)
    packed = jnp.zeros((8, channels), jnp.float32)
    for index, value in enumerate(
        (sums_shift, sums_gain, gain * sums_shift, gain * sums_gain, inv_std)
    ):
        packed = jnp.where(row == index, value, packed)
    for slot in range(sums.shape[0]):
        sums[slot] = packed

    all_rows = (out_rows * out_cols, channels)
    total = None
    for frame in range(frames):
        cots = jnp.concatenate(
            [
                (cot[frame + later] if frame + later < frames else halo[frame + later - frames])
                .reshape(all_rows)
                for later in range(3)
            ],
            axis=1,
        )
        term = dot(act[frame].reshape(all_rows).T, cots)
        total = term if total is None else total + term
    for later in range(3):
        block = total[:, later * channels : (later + 1) * channels] * loss_scale
        temporal[pl.ds(later * channels, channels)] = block.astype(jnp.bfloat16)


def split_rows(values, rows):
    pieces = []
    for value in values:
        rest = value
        for _ in range(3):
            piece = rest.astype(jnp.bfloat16).astype(jnp.float32)
            pieces.append(piece)
            rest = rest - piece
    row = lax.broadcasted_iota(jnp.int32, (rows, values[0].shape[-1]), 0)
    packed = jnp.zeros((rows, values[0].shape[-1]), jnp.float32)
    for index, piece in enumerate(pieces):
        packed = jnp.where(row == index, piece, packed)
    return packed.astype(jnp.bfloat16)


def join_rows(packed, count):
    return [
        packed[3 * i : 3 * i + 1] + packed[3 * i + 1 : 3 * i + 2] + packed[3 * i + 2 : 3 * i + 3]
        for i in range(count)
    ]


def store_rows(chunks, rows, first, values):
    done = 0
    while done < values.shape[0]:
        chunk, at = divmod(first + done, rows)
        count = min(rows - at, values.shape[0] - done)
        chunks[chunk, pl.ds(at, count)] = values[done : done + count]
        done += count


def grad_kernel(
    odd, even, normed, pre, sums, temporal, grads
):
    frames, out_rows, out_cols, channels = normed.shape
    lanes = channels // GROUPS
    members = sums.shape[0] * frames * out_rows * out_cols * lanes
    clip = jnp.sum(sums[...], axis=0)
    inv_std = sums[0, 4:5]
    group = group_spread(clip, lanes) * inv_std / members
    group_shift, group_gain = group[2:3], group[3:4]
    flat = (out_rows * out_cols, channels)
    rows = grads.shape[1] - EXTRA
    backs = []
    for frame in range(frames):
        back = (
            pre[frame].reshape(flat) - group_shift - normed[frame].reshape(flat) * group_gain
        )
        backs.append(back.astype(jnp.bfloat16).T)
    backs = jnp.concatenate(backs, axis=1)
    def turned(columns, blocks):
        part = dot(backs, columns)
        for side, block in enumerate(blocks):
            value = part[:, side * channels : (side + 1) * channels].astype(jnp.bfloat16).T
            store_rows(grads, rows, block * channels, value)

    def columns_of(tap, lanes):
        source = even[:, :, :, lanes] if tap == 1 else None
        if source is None:
            source = odd[:, tap // 2 : tap // 2 + out_rows, :, lanes]
        return source.reshape(frames * out_rows * out_cols, -1)

    for tap in range(3):
        turned(columns_of(tap, slice(0, 2 * channels)), (3 * tap, 3 * tap + 1))
    last = slice(2 * channels, 3 * channels)
    turned(jnp.concatenate([columns_of(0, last), columns_of(1, last)], axis=1), (2, 5))
    turned(columns_of(2, last), (8,))
    for tap in range(3):
        block = temporal[pl.ds(tap * channels, channels)]
        store_rows(grads, rows, (9 + tap) * channels, block)
    rest = grads.shape[0] * rows - 12 * channels
    if rest:
        store_rows(grads, rows, 12 * channels, jnp.zeros((rest, channels), jnp.bfloat16))
    share = clip * (1.0 / sums.shape[0])
    extra = split_rows([share[1:2], share[0:1]], EXTRA)
    for chunk in range(grads.shape[0]):
        grads[chunk, pl.ds(rows, EXTRA)] = extra


def total_of(arrived, first, count):
    total = arrived[0, pl.ds(first, count)].astype(jnp.float32)
    for chunk in range(1, arrived.shape[0]):
        total += arrived[chunk, pl.ds(first, count)].astype(jnp.float32)
    return total


def half_kernel(arrived, chunk):
    count = chunk.shape[0] - EXTRA
    chunk[pl.ds(0, count)] = total_of(arrived, 0, count).astype(jnp.bfloat16)
    sums = join_rows(total_of(arrived, count, EXTRA), 2)
    chunk[pl.ds(count, EXTRA)] = split_rows(sums, EXTRA)


def sum_kernel(mine, other, spread, totals):
    count = spread.shape[1]
    wide = [source[...].astype(jnp.float32) for source in (mine, other)]
    total = (wide[0][:count] + wide[1][:count]).astype(jnp.bfloat16)
    for slot in range(spread.shape[0]):
        spread[slot] = total
    sums = [join_rows(source[count:], 2) for source in wide]
    row = lax.broadcasted_iota(jnp.int32, totals.shape, 0)
    totals[...] = jnp.where(row == 0, sums[0][0] + sums[1][0], sums[0][1] + sums[1][1])


def final_kernel(arrived, totals, grad_spatial, grad_temporal, grad_gain, grad_shift):
    grad_gain[...] = totals[0:1]
    grad_shift[...] = totals[1:2]
    rows = grad_spatial.shape[0]
    grad_spatial[...] = arrived[pl.ds(0, rows)].astype(jnp.float32)
    grad_temporal[...] = arrived[pl.ds(rows, grad_temporal.shape[0])].astype(jnp.float32)


def encode_kernel(per_clip, act, halo, weights, encoded):
    frames, out_rows, out_cols, channels = act.shape
    not_first = lax.rem(lax.axis_index("seq"), per_clip) != 0
    flat = (STEP_ROWS * out_cols, channels)
    for frame in range(frames):

        def one(step, frame=frame):
            rows = pl.ds(step * STEP_ROWS, STEP_ROWS)
            total = None
            for tap in range(3):
                if frame >= tap:
                    source = act[frame - tap, rows]
                else:
                    source = halo[frames + frame - tap, rows]
                    source = jnp.where(not_first, source, jnp.zeros_like(source))
                term = dot(source.reshape(flat), weights[tap])
                total = term if total is None else total + term
            encoded[frame, rows] = total.astype(jnp.bfloat16).reshape(
                STEP_ROWS, out_cols, channels
            )

        each(out_rows // STEP_ROWS, one)


def on_device(video_in, w_spatial, w_temporal, norm_gain, norm_shift, cotangent):
    frames, height, width, channels = video_in.shape[1:]
    out_rows, out_cols = height // 2, width // 2
    dp_size, seq_size = lax.axis_size("dp"), lax.axis_size("seq")
    devices = dp_size * seq_size
    per_clip = FRAMES // frames
    assert frames >= 2 and FRAMES % frames == 0
    loss_scale = float(devices * frames * out_rows * out_cols) ** (-0.5)
    shape = (frames, out_rows, out_cols, channels)
    positions = frames * out_rows * out_cols
    video = video_in[0]
    cot = cotangent[0]
    f32, bf16 = jnp.float32, jnp.bfloat16
    struct = jax.ShapeDtypeStruct

    ahead_pairs = [
        (s, s // per_clip * per_clip + (s + 1) % per_clip) for s in range(seq_size)
    ]
    back_pairs = [(target, source) for source, target in ahead_pairs]
    clips = [list(range(first, first + per_clip)) for first in range(0, seq_size, per_clip)]

    def exchange(value, axes, groups=None):
        return lax.all_to_all(value, axes, 0, 0, axis_index_groups=groups, tiled=True)

    gate = pl.pallas_call(
        open_kernel,
        out_shape=pltpu.VMEM((8, channels), f32),
        out_specs=WHOLE,
        cost_estimate=pl.CostEstimate(
            flops=2 * positions * 9 * channels * channels,
            bytes_accessed=2 * video.size,
            transcendentals=0,
        ),
    )()
    cot_out, gate = lax.optimization_barrier((cot, gate))
    cot_halo = lax.ppermute(cot_out, "seq", back_pairs)

    pieces = frames
    def far(value):
        return pltpu.with_memory_space_constraint(value, pltpu.HBM)

    spatial, stats, odd, even, params = call(
        functools.partial(conv_kernel, pieces),
        (
            struct(shape, f32),
            struct((per_clip, 8, channels), f32),
            struct((frames, out_rows + 1, out_cols, 3 * channels), bf16),
            struct((frames, out_rows, out_cols, 3 * channels), bf16),
            struct((8, channels), f32),
        ),
        (
            gate,
            video,
            far(w_spatial.reshape(9 * channels, channels)),
            far(norm_gain[None]),
            far(norm_shift[None]),
        ),
        specs=[WHOLE] * 2 + [FAR] * 3,
        scratch=[
            pltpu.VMEM((4 * STEP_ROWS, 8 + width, channels), f32),
            pltpu.VMEM((9 * channels, channels), bf16),
            pltpu.SemaphoreType.DMA((3,)),
        ],
        flops=2 * positions * 9 * channels * channels,
    )
    stats = exchange(stats, "seq", clips)
    act, normed, slope, scales = call(
        functools.partial(act_kernel, loss_scale),
        (
            struct(shape, bf16),
            struct(shape, f32),
            struct(shape, f32),
            struct((8, channels), f32),
        ),
        (spatial, stats, params),
    )
    act_halo = lax.ppermute(act, "seq", ahead_pairs)
    pre, temporal, own = call(
        functools.partial(back_kernel, loss_scale),
        (
            struct(shape, f32),
            struct((3 * channels, channels), bf16),
            struct((per_clip, 8, channels), f32),
        ),
        (cot, cot_halo, w_temporal, scales, normed, slope, act),
        scratch=[pltpu.VMEM((2,) + shape[1:], bf16)],
        flops=2 * positions * 6 * channels * channels,
    )
    sums = exchange(own, "seq", clips)
    halves = 2 if seq_size % 2 == 0 else 1
    half = seq_size // halves
    near = [
        [d * seq_size + s for d in range(dp_size) for s in range(first, first + half)]
        for first in range(0, seq_size, half)
    ]
    count = dp_size * half
    rows = -(-12 * channels // (16 * count)) * 16
    sums, act_halo = lax.optimization_barrier((sums, act_halo))
    grads = call(
        grad_kernel,
        struct((count, rows + EXTRA, channels), bf16),
        (odd, even, normed, pre, sums, temporal),
        flops=2 * positions * 9 * channels * channels,
    )
    grads = exchange(grads, ("dp", "seq"), near)
    mine = call(half_kernel, struct((rows + EXTRA, channels), bf16), (grads,))
    if halves == 2:
        other = lax.ppermute(mine, "seq", [(s, (s + half) % seq_size) for s in range(seq_size)])
    else:
        other = jnp.zeros_like(mine)
    act, act_halo, _ = lax.optimization_barrier((act, act_halo, mine))
    encoded = call(
        functools.partial(encode_kernel, per_clip),
        struct(shape, bf16),
        (act, act_halo, w_temporal),
        flops=2 * positions * 3 * channels * channels,
    )
    other, encoded = lax.optimization_barrier((other, encoded))
    grads, totals = call(
        sum_kernel,
        (struct((count, rows, channels), bf16), struct((8, channels), f32)),
        (mine, other),
    )
    grads = exchange(grads, ("dp", "seq"), near)
    grad_spatial, grad_temporal, grad_gain, grad_shift = call(
        final_kernel,
        (
            struct((9 * channels, channels), f32),
            struct((3 * channels, channels), f32),
            struct((1, channels), f32),
            struct((1, channels), f32),
        ),
        (grads.reshape(count * rows, channels), totals),
    )
    return (
        encoded[None],
        grad_spatial.reshape(3, 3, channels, channels),
        grad_temporal.reshape(3, channels, channels),
        grad_gain[0],
        grad_shift[0],
    )


def solution(mesh):
    placed = P("dp", "seq", None, None, None)
    return jax.shard_map(
        on_device,
        mesh=mesh,
        in_specs=(placed, P(), P(), P(), P(), placed),
        out_specs=(placed, P(), P(), P(), P()),
        check_vma=False,
    )
```
